32 devices in a mesh: section: 2 (over y), row: 4 (over x, core), col: 4 (over z).
Axes of the slice: x: 2, y: 2, z: 4, core: 2. Of those that a mesh axis runs over, the one named last changes fastest.
Arguments:
- x_down: bfloat16 [2, 1024, 8192], P('section', 'row', 'col'), may hold values from -30 to 30
- gain_down: float32 [2, 8192], P('section', 'col'), may hold values from 0.1 to 1.9
- wq_down: bfloat16 [2, 8192, 4096], P('section', 'col', 'row'), may hold values from -2 to 2
- wk_down: bfloat16 [2, 8192, 512], P('section', 'col', 'row'), may hold values from -1 to 1
- wv_down: bfloat16 [2, 8192, 512], P('section', 'col', 'row'), may hold values from -0.0625 to 0.0625
- wo_down: bfloat16 [2, 4096, 8192], P('section', 'row', 'col'), may hold values from -0.09375 to 0.09375
- x_up: bfloat16 [2, 1024, 8192], P('section', 'row', 'col'), may hold values from -30 to 30
- gain_up: float32 [2, 8192], P('section', 'col'), may hold values from 0.1 to 1.9
- wq_up: bfloat16 [2, 8192, 4096], P('section', 'col', 'row'), may hold values from -2 to 2
- wk_up: bfloat16 [2, 8192, 512], P('section', 'col', 'row'), may hold values from -1 to 1
- wv_up: bfloat16 [2, 8192, 512], P('section', 'col', 'row'), may hold values from -0.0625 to 0.0625
- wo_up: bfloat16 [2, 4096, 8192], P('section', 'row', 'col'), may hold values from -0.09375 to 0.09375
Outputs:
- next_down: bfloat16 [2, 1024, 8192], P('section', 'row', 'col')
- next_up: bfloat16 [2, 1024, 8192], P('section', 'row', 'col')
The draws below stay inside these ranges and needn't reach their ends.
All inputs are finite; a program needn't handle non-finite values.
Results may differ from the reference program's by a relative error of at most 0.0055.
Values may be sent and summed in bfloat16 or wider, within the bound.
No kernel may reach another device: no remote copies, remote signals or barrier semaphores. Data moves between devices by JAX's collectives and lax.ppermute only.
A program may use at most 128 MiB of HBM per device.

```python
import math
import jax
import jax.numpy as jnp
from jax import lax

D = 8192
HEADS = 32
KV_HEADS = 4
HD = 128
TOKENS = 1024
HQ = 4096
KVW = 512
SECTIONS = 2
N_ROW = 4


def activations(key):
    noise_key, row_key, col_key = jax.random.split(key, 3)
    ramp = jnp.arange(D, dtype=jnp.float32) / D
    noise = jnp.clip(jax.random.normal(noise_key, (SECTIONS, TOKENS, D), jnp.float32), -3.0, 3.0)
    slope = 1.0 + 0.8 * ramp
    row_scale = jnp.exp(jax.random.uniform(row_key, (SECTIONS, TOKENS, 1), jnp.float32, math.log(0.2), math.log(2.0)))
    col_scale = jnp.exp(jax.random.uniform(col_key, (SECTIONS, 1, D), jnp.float32, 0.0, math.log(3.2)))
    result = noise * row_scale * col_scale * slope[None, None, :]
    return jnp.clip(result, -30.0, 30.0).astype(jnp.bfloat16)


def query_key(key):
    base = jnp.clip(jax.random.normal(jax.random.fold_in(key, 11), (SECTIONS, D, KVW), jnp.float32), -4.0, 4.0) * D ** (-0.5)
    free_query = jnp.clip(jax.random.normal(jax.random.fold_in(key, 12), (SECTIONS, D, HQ), jnp.float32), -4.0, 4.0) * D ** (-0.5)
    query = free_query
    return (jnp.clip(query, -2.0, 2.0).astype(jnp.bfloat16), jnp.clip(base, -1.0, 1.0).astype(jnp.bfloat16))


def draw_x_down(key, part):
    return activations(jax.random.fold_in(key, 3))


def draw_x_up(key, part):
    return activations(jax.random.fold_in(key, 4))


def draw_wq_down(key, part):
    return query_key(jax.random.fold_in(key, 1))[0]


def draw_wk_down(key, part):
    return query_key(jax.random.fold_in(key, 1))[1]


def draw_wq_up(key, part):
    return query_key(jax.random.fold_in(key, 2))[0]


def draw_wk_up(key, part):
    return query_key(jax.random.fold_in(key, 2))[1]


def level_of(own_key, dims, cuts, low, largest):
    def one(axis_at, parts):
        steps = jax.random.uniform(jax.random.fold_in(jax.random.fold_in(own_key, 6), axis_at), (parts,), jnp.float32, low / len(cuts), largest / len(cuts))
        return jnp.repeat(jnp.exp(steps), dims[axis_at] // parts).reshape((-1,) + (1,) * (len(dims) - axis_at - 1))

    level = one(*cuts[0])
    for cut in cuts[1:]:
        level = level * one(*cut)
    return level


def bell_draw(rng, extent, spread, reach, pieces=(), kind=jnp.bfloat16):
    factor_of = level_of(rng, extent, pieces, -0.22, 0.18) if pieces else 1.0
    values = jax.random.normal(rng, extent, jnp.float32) * spread * factor_of
    return jnp.minimum(jnp.maximum(values, -reach), reach).astype(kind)


def setup_inputs(seed: int = 0) -> dict:
    key_list = jax.random.split(jax.random.key(seed), 13)
    x_down = draw_x_down(jax.random.fold_in(key_list[12], 71), 0)
    gain_down = jnp.clip(1.0 + 0.18 * jax.random.normal(key_list[1], (SECTIONS, D), jnp.float32), 0.1, 1.9)
    wq_down = draw_wq_down(jax.random.fold_in(key_list[12], 71), 0)
    wk_down = draw_wk_down(jax.random.fold_in(key_list[12], 71), 0)
    wv_down = bell_draw(key_list[4], (SECTIONS, D, KVW), D ** -0.5, 0.0625, ((0, 2), (1, 4), (2, 4)))
    wo_down = bell_draw(key_list[5], (SECTIONS, HQ, D), HQ ** -0.5, 0.09375, ((0, 2), (1, 4), (2, 4)))
    x_up = draw_x_up(jax.random.fold_in(key_list[12], 71), 0)
    gain_up = jnp.clip(1.0 + 0.18 * jax.random.normal(key_list[7], (SECTIONS, D), jnp.float32), 0.1, 1.9)
    wq_up = draw_wq_up(jax.random.fold_in(key_list[12], 71), 0)
    wk_up = draw_wk_up(jax.random.fold_in(key_list[12], 71), 0)
    wv_up = bell_draw(key_list[10], (SECTIONS, D, KVW), D ** -0.5, 0.0625, ((0, 2), (1, 4), (2, 4)))
    wo_up = bell_draw(key_list[11], (SECTIONS, HQ, D), HQ ** -0.5, 0.09375, ((0, 2), (1, 4), (2, 4)))
    return {"x_down": x_down, "gain_down": gain_down, "wq_down": wq_down, "wk_down": wk_down, "wv_down": wv_down, "wo_down": wo_down, "x_up": x_up, "gain_up": gain_up, "wq_up": wq_up, "wk_up": wk_up, "wv_up": wv_up, "wo_up": wo_up}


epsilon = 1e-05

def rounded(array):
    return lax.optimization_barrier(array.astype(jnp.bfloat16)).astype(jnp.float32)

def rotary(matrix, positions):
    row_count = matrix.shape[0]
    shaped = matrix.reshape(row_count, -1, HD)
    half_width = HD // 2
    inverse = 10000.0 ** (-jnp.arange(half_width, dtype=jnp.float32) / half_width)
    angles = positions[:, None] * inverse[None, :]
    cosine = jnp.cos(angles)[:, None, :]
    sine_part = jnp.sin(angles)[:, None, :]
    front_half = shaped[..., :half_width]
    back_half = shaped[..., half_width:]
    turned = jnp.concatenate([front_half * cosine - back_half * sine_part, back_half * cosine + front_half * sine_part], axis=-1)
    return turned.reshape(row_count, -1)

def attention_block(activ, gain_vector, w_query, w_key, w_value, w_out):
    floats = activ.astype(jnp.float32)
    total_sq = lax.optimization_barrier(jnp.sum(floats * floats, axis=1))
    normed = (floats * lax.rsqrt(total_sq / D + epsilon)[:, None] * gain_vector[None, :]).astype(jnp.bfloat16)
    positions = jnp.arange(TOKENS, dtype=jnp.float32)
    queries = rotary(jnp.dot(normed, w_query, preferred_element_type=jnp.float32), positions)
    keys_all = rotary(jnp.dot(normed, w_key, preferred_element_type=jnp.float32), positions)
    values_all = jnp.dot(normed, w_value, preferred_element_type=jnp.float32)
    group_size = HEADS // KV_HEADS
    query_heads = rounded(queries).reshape(TOKENS, KV_HEADS, group_size, HD)
    key_heads = rounded(keys_all).reshape(TOKENS, KV_HEADS, HD)
    value_heads = rounded(values_all).reshape(TOKENS, KV_HEADS, HD)
    scores = jnp.einsum('qkgd,tkd->kgqt', query_heads, key_heads) * (1.0 / HD ** 0.5)
    visible = positions[:, None] >= positions[None, :]
    masked = jnp.where(visible, scores, -1e+30)
    row_top = lax.optimization_barrier(jnp.max(masked, axis=-1, keepdims=True))
    exponent = jnp.where(visible, jnp.exp(masked - row_top), 0.0)
    row_total = lax.optimization_barrier(jnp.sum(exponent, axis=-1))
    mixed_out = jnp.einsum('kgqt,tkd->kgqd', rounded(exponent), value_heads) / row_total[..., None]
    attended = mixed_out.transpose(2, 0, 1, 3).reshape(TOKENS, HQ).astype(jnp.bfloat16)
    group_width = HQ // N_ROW
    summed = jnp.zeros((TOKENS, D), jnp.float32)
    for group_index in range(N_ROW):
        lower = group_index * group_width
        partial_value = jnp.dot(attended[:, lower:lower + group_width], w_out[lower:lower + group_width], preferred_element_type=jnp.float32)
        summed = summed + rounded(partial_value)
    return (floats + summed).astype(jnp.bfloat16)

def reference(x_down, gain_down, wq_down, wk_down, wv_down, wo_down, x_up, gain_up, wq_up, wk_up, wv_up, wo_up):
    down_list = []
    up_list = []
    for section_index in range(SECTIONS):
        down_list.append(attention_block(x_down[section_index], gain_down[section_index], wq_down[section_index], wk_down[section_index], wv_down[section_index], wo_down[section_index]))
        up_list.append(attention_block(x_up[section_index], gain_up[section_index], wq_up[section_index], wk_up[section_index], wv_up[section_index], wo_up[section_index]))
    next_down = jnp.roll(jnp.stack(down_list), 1, axis=0)
    next_up = jnp.roll(jnp.stack(up_list), -1, axis=0)
    return (next_down, next_up)
```

```python
import jax
import jax.numpy as jnp
from jax import lax
from jax.sharding import PartitionSpec as P

HD = 128
EPSILON = 1e-05
BF16 = jnp.bfloat16
F32 = jnp.float32


def swapped(value, axis, bit):
    return lax.ppermute(value, axis, [(i, i ^ (1 << bit)) for i in range(lax.axis_size(axis))])


def from_behind(value, axis, steps):
    count = lax.axis_size(axis)
    return lax.ppermute(value, axis, [(i, (i + steps) % count) for i in range(count)])


def bits_of(axis):
    return lax.axis_size(axis).bit_length() - 1


def my_bit(axis, bit):
    return (lax.axis_index(axis) >> bit) & 1


def pick(value, index, dim):
    return lax.dynamic_index_in_dim(value, index, dim, keepdims=False)


def rope_tables(positions):
    half = HD // 2
    inverse = 10000.0 ** (-jnp.arange(half, dtype=F32) / half)
    angles = positions[..., None] * inverse
    return jnp.cos(angles), jnp.sin(angles)


def rotary(matrix, tables):
    cosine, sine = (t[..., None, :] for t in tables)
    shaped = matrix.reshape(matrix.shape[:-1] + (-1, HD))
    front, back = shaped[..., : HD // 2], shaped[..., HD // 2 :]
    turned = jnp.concatenate([front * cosine - back * sine, back * cosine + front * sine], axis=-1)
    return turned.reshape(matrix.shape)


def gather_rows(block):
    blocks = {0: block}
    for bit in range(1, bits_of("row")):
        for o in list(blocks):
            blocks[o | 1 << bit] = swapped(blocks[o], "row", bit)
    for o in list(blocks):
        blocks[o | 1] = swapped(blocks[o], "row", 0)
    return blocks


class Cascade:
    def __init__(self, x, gain, wq, wk, wv, wo):
        self.x, self.gain, self.wo = x, gain, wo
        if wk.shape[1] < HD:
            other_k, other_v = swapped((wk, wv), "row", 0)
            even = lax.axis_index("row") % 2 == 0
            wk = jnp.where(even, jnp.concatenate([wk, other_k], 1), jnp.concatenate([other_k, wk], 1))
            wv = jnp.where(even, jnp.concatenate([wv, other_v], 1), jnp.concatenate([other_v, wv], 1))
        self.qw, self.kvw = wq.shape[1], wk.shape[1]
        self.w = jnp.concatenate([wq, wk, wv], axis=1)
        self.n_row, self.n_col = lax.axis_size("row"), lax.axis_size("col")
        self.sub = x.shape[0] // self.n_col
        self.features = x.shape[1] * self.n_col

    def split(self, block):
        b = block.reshape(self.n_col // 2, 2, self.sub, -1)
        low = my_bit("col", 0)
        keep, send = pick(b, low, 1), pick(b, 1 - low, 1)
        return keep, send

    def project(self, block_list):
        low = my_bit("col", 0)
        blocks = jnp.stack(block_list).reshape(len(block_list), self.n_col // 2, 2, self.sub, -1)

        def dot(half):
            scaled = (half.astype(F32) * self.gain).astype(BF16)
            rows = scaled.reshape(-1, scaled.shape[-1])
            out = jnp.dot(rows, self.w, preferred_element_type=F32)
            return out.reshape(half.shape[:-1] + (-1,))

        arrived = swapped(dot(pick(blocks, 1 - low, 2)).astype(BF16), "col", 0)
        total = dot(pick(blocks, low, 2)) + arrived.astype(F32)
        for bit in range(1, bits_of("col")):
            mine = my_bit("col", bit)
            shaped = total.reshape(total.shape[0], -1, 2, *total.shape[2:])
            arrived = swapped(pick(shaped, 1 - mine, 2).astype(BF16), "col", bit)
            total = pick(shaped, mine, 2) + arrived.astype(F32)
        return total[:, 0]

    def squares(self, block_list):
        return jnp.stack([jnp.sum(jnp.square(b.astype(F32)), axis=1) for b in block_list])

    def attend(self):
        blocks = gather_rows(self.x)
        order = sorted(blocks)
        half = max(len(order) // 2, 1)
        groups = [order[:half], order[half:]]
        sums = jnp.concatenate([self.project([blocks[o] for o in g]) for g in groups])
        squares = self.squares([blocks[o] for o in order])
        for bit in range(bits_of("col")):
            squares = squares + swapped(squares, "col", bit)
        z, r = lax.axis_index("col"), lax.axis_index("row")
        squares = pick(squares.reshape(len(order), self.n_col, self.sub), z, 1)
        scaled = sums * lax.rsqrt(squares / self.features + EPSILON)[..., None]
        block_start = (r ^ jnp.array(order, jnp.int32)) * self.x.shape[0]
        offsets = jnp.arange(self.sub, dtype=jnp.int32)
        positions = (block_start[:, None] + z * self.sub + offsets).astype(F32)
        tables = rope_tables(positions)
        queries = rotary(scaled[..., : self.qw], tables).astype(BF16)
        keys = rotary(scaled[..., self.qw : self.qw + self.kvw], tables).astype(BF16)
        values = scaled[..., self.qw + self.kvw :].astype(BF16)
        pairs = jnp.concatenate([keys, values], axis=-1)[None]
        owners = jnp.zeros((1,), jnp.int32)
        for bit in reversed(range(bits_of("col"))):
            pairs = jnp.concatenate([pairs, swapped(pairs, "col", bit)])
            owners = jnp.concatenate([owners, owners ^ (1 << bit)])
        owners = (z ^ owners) * self.sub
        key_positions = (owners[:, None, None] + block_start[:, None] + offsets).astype(F32).reshape(-1)
        pairs = pairs.reshape(-1, pairs.shape[-1])
        kv_heads = self.kvw // HD
        rows = len(order) * self.sub
        q = queries.reshape(rows, kv_heads, -1, HD)
        k = pairs[:, : self.kvw].reshape(-1, kv_heads, HD)
        v = pairs[:, self.kvw :].reshape(-1, kv_heads, HD)
        scores = jnp.einsum("qkgd,tkd->kgqt", q, k, preferred_element_type=F32) * (1.0 / HD**0.5)
        visible = positions.reshape(-1)[:, None] >= key_positions[None, :]
        masked = jnp.where(visible, scores, -1e30)
        top = jnp.max(masked, axis=-1, keepdims=True)
        weights = jnp.where(visible, jnp.exp(masked - top), 0.0)
        total = jnp.sum(weights, axis=-1)
        mixed = jnp.einsum("kgqt,tkd->kgqd", weights.astype(BF16), v, preferred_element_type=F32)
        mixed = mixed / total[..., None]
        attended = mixed.transpose(2, 0, 1, 3).reshape(len(order), self.sub, self.qw).astype(BF16)
        self.order = order
        return attended

    def finish(self, attended, steps):
        order, row_bits = self.order, bits_of("row")
        low = my_bit("col", 0)
        near = attended[:, None]
        for bit in range(1, bits_of("col")):
            other = swapped(near, "col", bit)
            mine = my_bit("col", bit)
            near = jnp.where(
                mine == 0, jnp.concatenate([near, other], 1), jnp.concatenate([other, near], 1)
            )
        far = swapped(near, "col", 0)
        residual = self.x.reshape(self.n_col // 2, 2, self.sub, -1)
        pieces = []
        for rows, which in ((near, low), (far, 1 - low)):
            part = jnp.dot(
                rows.reshape(-1, self.qw), self.wo, preferred_element_type=F32
            ).reshape(len(order), -1, self.wo.shape[1])
            for bit in range(row_bits):
                shaped = part.reshape(-1, 2, *part.shape[1:])
                arrived = swapped(shaped[:, 1].astype(BF16), "row", bit)
                part = shaped[:, 0] + arrived.astype(F32)
            own = pick(residual, which, 1).astype(F32).reshape(part[0].shape)
            fresh = (own + part[0]).astype(BF16)
            pieces.append(from_behind(fresh, "section", steps).reshape(self.n_col // 2, self.sub, -1))
        first, second = pieces
        joined = jnp.where(
            low == 0, jnp.stack([first, second], 1), jnp.stack([second, first], 1)
        )
        return joined.reshape(self.x.shape)[None]


def on_device(*arrays):
    arrays = [a[0] for a in arrays]
    half = len(arrays) // 2
    down, up = Cascade(*arrays[:half]), Cascade(*arrays[half:])
    return down.finish(down.attend(), 1), up.finish(up.attend(), -1)


def solution(mesh):
    tokens = P("section", "row", "col")
    into, out_of = P("section", "col", "row"), P("section", "row", "col")
    one = (tokens, P("section", "col"), into, into, into, out_of)
    return jax.shard_map(
        on_device, mesh=mesh, in_specs=one + one, out_specs=(tokens, tokens), check_vma=False
    )
```

```python
import functools

import jax
import jax.numpy as jnp
from jax import lax
from jax.experimental import pallas as pl
from jax.experimental.pallas import tpu as pltpu
from jax.sharding import PartitionSpec as P

HD = 128
EPSILON = 1e-05
HIDDEN = -1e30
LOG2E = 1.4426950408889634
BF16 = jnp.bfloat16
F32 = jnp.float32


def swapped(value, axis, bit):
    return lax.ppermute(value, axis, [(i, i ^ (1 << bit)) for i in range(lax.axis_size(axis))])


def crossed(value, axis, bits):
    return lax.ppermute(value, axis, [(i, i ^ bits) for i in range(lax.axis_size(axis))])


def from_behind(value, axis, steps):
    count = lax.axis_size(axis)
    return lax.ppermute(value, axis, [(i, (i + steps) % count) for i in range(count)])


def bits_of(axis):
    return lax.axis_size(axis).bit_length() - 1


def my_bit(axis, bit):
    return (lax.axis_index(axis) >> bit) & 1


def pick(value, index, dim):
    return lax.dynamic_index_in_dim(value, index, dim, keepdims=False)


def tie(value, *deps):
    return lax.optimization_barrier((value, deps))[0]


class Chain:
    def __init__(self):
        self.token = None

    def enter(self, *values):
        out = values if self.token is None else tie(values, self.token)
        return out[0] if len(values) == 1 else out

    def leave(self, array):
        self.token = array


def turn(value, cosine, sine):
    return value * cosine + pltpu.roll(value, HD // 2, 1) * sine


def rows_of(keeps, arrivals, inverse, columns):
    parts = [k[:, columns] + a[:, columns].astype(F32) for k, a in zip(keeps, arrivals)]
    return jnp.concatenate(parts, axis=0) * inverse[...]


def kv_kernel(qw, kvw, keep_a, keep_b, arr_a, arr_b, inverse, cosine, sine, out):
    for start in range(0, 2 * kvw, HD):
        columns = slice(qw + start, qw + start + HD)
        value = rows_of((keep_a, keep_b), (arr_a, arr_b), inverse, columns)
        if start < kvw:
            value = turn(value, cosine[...], sine[...])
        out[:, start : start + HD] = value.astype(BF16)


def attention_kernel(
    qw, kvw, count, keep_a, keep_b, arr_a, arr_b, inverse, cosine, sine, q_pos, k_pos, *rest
):
    pairs, (out, keys, values, bias) = rest[:count], rest[count:]
    rows = pairs[0].shape[0]
    for i, pair in enumerate(pairs):
        keys[i * rows : (i + 1) * rows] = pair[:, :kvw]
        values[i * rows : (i + 1) * rows] = pair[:, kvw:]
    bias[...] = jnp.where(q_pos[...] >= k_pos[...], 0.0, HIDDEN)
    group = (qw // HD) // (kvw // HD)
    for head in range(qw // HD):
        columns = slice(head * HD, (head + 1) * HD)
        kv_columns = slice(head // group * HD, (head // group + 1) * HD)
        query = rows_of((keep_a, keep_b), (arr_a, arr_b), inverse, columns)
        query = turn(query, cosine[...], sine[...]).astype(BF16)
        scores = lax.dot_general(
            query, keys[:, kv_columns], (((1,), (1,)), ((), ())), preferred_element_type=F32
        )
        scores = scores + bias[...]
        top = jnp.max(scores, axis=1, keepdims=True)
        probs = jnp.exp2((scores - top) * (LOG2E / HD**0.5))
        total = jnp.sum(probs, axis=1, keepdims=True)
        mixed = jnp.dot(probs.astype(BF16), values[:, kv_columns], preferred_element_type=F32)
        out[:, columns] = (mixed / total).astype(BF16)


def gather(block, axis, after_far=None):
    blocks = {0: block}
    for bit in range(1, bits_of(axis)):
        for o in list(blocks):
            blocks[o | 1 << bit] = swapped(blocks[o], axis, bit)
    return blocks


class Cascade:
    def __init__(self, x, gain, wq, wk, wv, wo):
        self.x, self.gain, self.wo = x, gain, wo
        if wk.shape[1] < HD:
            other_k, other_v = swapped((wk, wv), "row", 0)
            even = lax.axis_index("row") % 2 == 0
            wk = jnp.where(even, jnp.concatenate([wk, other_k], 1), jnp.concatenate([other_k, wk], 1))
            wv = jnp.where(even, jnp.concatenate([wv, other_v], 1), jnp.concatenate([other_v, wv], 1))
        self.qw, self.kvw = wq.shape[1], wk.shape[1]
        self.w = jnp.concatenate([wq, wk, wv], axis=1)
        self.n_row, self.n_col = lax.axis_size("row"), lax.axis_size("col")
        self.sub = x.shape[0] // self.n_col
        self.keep, self.arrived = [], []
        self.first, self.second = [None, None], [None, None]

    def halves(self, block_list):
        low = my_bit("col", 0)
        blocks = jnp.stack(block_list).reshape(len(block_list), self.n_col // 2, 2, self.sub, -1)
        return pick(blocks, 1 - low, 2), pick(blocks, low, 2)

    def project(self, half):
        scaled = (half.astype(F32) * self.gain).astype(BF16)
        rows = scaled.reshape(-1, scaled.shape[-1])
        out = jnp.dot(rows, self.w, preferred_element_type=F32)
        return out.reshape(half.shape[:-1] + (-1,))

    def halve(self, total, arrived, bit):
        mine = my_bit("col", bit)
        shape = (total.shape[0], -1, 2) + total.shape[2:]
        total, arrived = total.reshape(shape), arrived.reshape(shape)

        def part(which):
            return pick(total, which, 2) + pick(arrived, which, 2).astype(F32)

        return part(mine), part(1 - mine).astype(BF16)

    def flat(self, value):
        return value.reshape(-1, value.shape[-1])

    def kernel_rows(self):
        return [self.flat(v) for v in self.keep] + [self.flat(v) for v in self.arrived]


def whole(body, out_shape, scratch=(), flops=0, exps=0, moved=0):
    return pl.pallas_call(
        body,
        out_shape=out_shape,
        scratch_shapes=list(scratch),
        compiler_params=pltpu.CompilerParams(vmem_limit_bytes=40 * 1024 * 1024),
        cost_estimate=pl.CostEstimate(flops=flops, transcendentals=exps, bytes_accessed=moved),
    )


def on_device(*arrays):
    arrays = [a[0] for a in arrays]
    half = len(arrays) // 2
    d, u = Cascade(*arrays[:half]), Cascade(*arrays[half:])
    n_row, n_col, sub = d.n_row, d.n_col, d.sub
    block = n_col * sub
    features = d.x.shape[1] * n_col
    rows = n_row * sub
    qw, kvw = d.qw, d.kvw
    z, r = lax.axis_index("col"), lax.axis_index("row")
    chain = Chain()

    order = [o for o in range(n_row) if o < 2] + [o for o in range(n_row) if o >= 2]
    starts = (r ^ jnp.array(order, jnp.int32)) * block
    offsets = jnp.arange(sub, dtype=jnp.int32)
    q_pos = (starts[:, None] + z * sub + offsets).astype(F32).reshape(rows, 1)
    owners = (z ^ jnp.arange(n_col, dtype=jnp.int32)) * sub
    k_pos = (owners[:, None, None] + starts[:, None] + offsets).astype(F32).reshape(1, -1)
    width = HD // 2
    inverse_freq = 10000.0 ** (-jnp.arange(width, dtype=F32) / width)
    angles = q_pos * inverse_freq
    cosine = jnp.concatenate([jnp.cos(angles)] * 2, axis=1)
    sine = jnp.sin(angles)
    sine = jnp.concatenate([-sine, sine], axis=1)

    d_blocks = gather(d.x, "row")
    d_blocks[1] = swapped(d.x, "row", 0)
    squares = jnp.stack([jnp.sum(jnp.square(c.x.astype(F32)), axis=1) for c in (d, u)])
    other = swapped(squares, "col", 0)

    def send_first(c, group, blocks_):
        send, kept = c.halves(chain.enter(*blocks_))
        product = c.project(send).astype(BF16)
        return product, kept

    def keep_first(c, kept, token):
        return c.project(tie(kept, token))

    product, kept = send_first(d, 0, [d_blocks[0], d_blocks[1]])
    d_arr_a = swapped(product, "col", 0)
    d_tot_a = keep_first(d, kept, product)
    chain.leave(d_tot_a)
    squares, other = chain.enter(squares, other)
    squares = squares + other
    for bit in range(1, bits_of("col")):
        squares = squares + swapped(squares, "col", bit)
    chain.leave(squares)
    u_near = swapped(chain.enter(u.x), "row", 0)

    far = [o for o in d_blocks if o >= 2]
    d_far = chain.enter(*[d_blocks[o] for o in far])
    d_far = list(d_far) if len(far) > 1 else [d_far]
    u_blocks = gather(tie(u.x, *d_far), "row")
    u_blocks[1] = u_near
    for o, value in zip(far, d_far):
        d_blocks[o] = value
        d_blocks[o | 1] = swapped(value, "row", 0)
    chain.leave(d_far[-1])
    sq = {0: squares}
    for bit in range(1, bits_of("row")):
        for o in list(sq):
            sq[o | 1 << bit] = swapped(tie(sq[o], *d_far), "row", bit)

    def second(c, total, arrived):
        total, arrived = chain.enter(total, arrived)
        kept, product = c.halve(total, arrived, 1)
        arrived = swapped(product, "col", 1)
        chain.leave(product)
        for bit in range(2, bits_of("col")):
            kept, product = c.halve(kept, arrived, bit)
            arrived = swapped(product, "col", bit)
        c.keep.append(kept)
        c.arrived.append(arrived)

    second(d, d_tot_a, d_arr_a)

    far_order = [o for o in order if o >= 2]
    product, kept = send_first(d, 1, [d_blocks[o] for o in far_order])
    d_arr_b = swapped(product, "col", 0)
    d_tot_b = keep_first(d, kept, product)
    chain.leave(d_tot_b)

    u_prod_a, kept = send_first(u, 0, [u_blocks[0], u_blocks[1]])
    u_tot_a = keep_first(u, kept, u_prod_a)
    chain.leave(u_tot_a)

    second(d, d_tot_b, d_arr_b)
    u_arr_a = swapped(tie(u_prod_a, chain.token), "col", 0)

    u_far = chain.enter(*[u_blocks[o] for o in far])
    u_far = list(u_far) if len(far) > 1 else [u_far]
    for o, value in zip(far, u_far):
        u_blocks[o] = value
        u_blocks[o | 1] = swapped(value, "row", 0)
    chain.leave(u_far[-1])
    for o in list(sq):
        sq[o | 1] = swapped(tie(sq[o], *u_far), "row", 0)
    u_prod_b, kept = send_first(u, 1, [u_blocks[o] for o in far_order])
    u_tot_b = keep_first(u, kept, u_prod_b)
    chain.leave(u_tot_b)

    sums = jnp.stack([sq[o] for o in order])
    sums = pick(sums.reshape(n_row, 2, n_col, sub), z, 2)
    inverse = lax.rsqrt(sums / features + EPSILON).transpose(1, 0, 2).reshape(2, rows, 1)

    def make_pairs(c, scale):
        inputs = chain.enter(*c.kernel_rows())
        pair = whole(
            functools.partial(kv_kernel, qw, kvw),
            jax.ShapeDtypeStruct((rows, 2 * kvw), BF16),
            moved=2 * rows * (qw + 2 * kvw) * 6,
        )(*inputs, scale, cosine, sine)
        chain.leave(pair)
        return inputs, [pair] + [crossed(pair, "col", o) for o in range(1, n_col)]

    def attend(c, inputs, scale, pairs):
        pairs = chain.enter(*pairs)
        keys = rows * n_col
        out = whole(
            functools.partial(attention_kernel, qw, kvw, n_col),
            jax.ShapeDtypeStruct((rows, qw), BF16),
            scratch=[pltpu.VMEM((keys, kvw), BF16), pltpu.VMEM((keys, kvw), BF16), pltpu.VMEM((rows, keys), F32)],
            flops=4 * rows * keys * qw,
            exps=rows * keys * qw // HD,
            moved=rows * qw * 8,
        )(*inputs, scale, cosine, sine, q_pos, k_pos, *pairs)
        chain.leave(out)
        return out

    d_inputs, d_pairs = make_pairs(d, inverse[0])
    second(u, u_tot_a, u_arr_a)
    u_arr_b = swapped(tie(u_prod_b, chain.token), "col", 0)
    d_att = attend(d, d_inputs, inverse[0], d_pairs)
    d_got = gather(d_att, "col")
    d_got[1] = swapped(d_att, "col", 0)
    second(u, u_tot_b, u_arr_b)

    order_rows = jnp.array(order)

    def out_first(c, pieces):
        pieces = chain.enter(*pieces)
        pieces = pieces if isinstance(pieces, (list, tuple)) else [pieces]
        shaped = jnp.stack([p.reshape(n_row // 2, 2, sub, qw) for p in pieces], axis=2)

        def dot(value):
            out = jnp.dot(value.reshape(-1, qw), c.wo, preferred_element_type=F32)
            return out.reshape(n_row // 2, -1, c.wo.shape[1])

        product = dot(shaped[:, 1]).astype(BF16)
        arrived = swapped(product, "row", 0)
        kept = dot(tie(shaped[:, 0], product))
        chain.leave(kept)
        return kept, arrived

    def out_second(kept, arrived):
        kept, arrived = chain.enter(kept, arrived)
        for bit in range(1, bits_of("row")):
            total = (kept + arrived.astype(F32)).reshape(-1, 2, *kept.shape[1:])
            product = total[:, 1].astype(BF16)
            kept, arrived = total[:, 0], swapped(product, "row", bit)
        chain.leave(product)
        return kept, arrived

    def out_third(c, kept, arrived, which, steps):
        kept, arrived = chain.enter(kept, arrived)
        residual = c.x.reshape(n_col, sub, -1)
        own = jnp.stack([pick(residual, z ^ o, 0) for o in which]).astype(F32)
        total = kept[0] + arrived[0].astype(F32)
        fresh = (own + total.reshape(own.shape)).astype(BF16)
        chain.leave(fresh)
        return from_behind(fresh, "section", steps)

    def finish(c, sent_p, sent_q):
        both = jnp.concatenate([sent_p, sent_q]).reshape((2,) * bits_of("col") + (sub, -1))
        for bit in range(bits_of("col")):
            dim = bits_of("col") - 1 - bit
            both = jnp.where(my_bit("col", bit) == 0, both, jnp.flip(both, dim))
        return both.reshape(c.x.shape)[None]

    def far_pieces(got):
        names = [o for o in got if o >= 2]
        values = chain.enter(*[got[o] for o in names])
        values = list(values) if len(names) > 1 else [values]
        chain.leave(values[-1])
        for o, value in zip(names, values):
            got[o] = value
            got[o | 1] = swapped(value, "col", 0)

    near_names, far_names = [0, 1], list(range(2, n_col))
    d_p = out_first(d, [d_got[o] for o in near_names])
    u_inputs, u_pairs = make_pairs(u, inverse[1])
    d_p = out_second(*d_p)
    far_pieces(d_got)
    u_att = attend(u, u_inputs, inverse[1], u_pairs)
    u_got = gather(u_att, "col")
    u_got[1] = swapped(u_att, "col", 0)
    d_p = out_third(d, *d_p, near_names, 1)
    d_q = out_first(d, [d_got[o] for o in far_names])
    d_q = out_second(*d_q)
    u_p = out_first(u, [u_got[o] for o in near_names])
    far_pieces(u_got)
    u_p = out_second(*u_p)
    d_q = out_third(d, *d_q, far_names, 1)
    u_q = out_first(u, [u_got[o] for o in far_names])
    u_p = out_third(u, *u_p, near_names, -1)
    u_q = out_second(*u_q)
    u_q = out_third(u, *u_q, far_names, -1)
    return finish(d, d_p, d_q), finish(u, u_p, u_q)


def solution(mesh):
    tokens = P("section", "row", "col")
    into, out_of = P("section", "col", "row"), P("section", "row", "col")
    one = (tokens, P("section", "col"), into, into, into, out_of)
    return jax.shard_map(
        on_device, mesh=mesh, in_specs=one + one, out_specs=(tokens, tokens), check_vma=False
    )
```

```python
import functools

import jax
import jax.numpy as jnp
from jax import lax
from jax.experimental import pallas as pl
from jax.experimental.pallas import tpu as pltpu
from jax.sharding import PartitionSpec as P

HD = 128
EPSILON = 1e-05
HIDDEN = -1e30
LOG2E = 1.4426950408889634
BF16 = jnp.bfloat16
F32 = jnp.float32


def swapped(value, axis, bit):
    return lax.ppermute(value, axis, [(i, i ^ (1 << bit)) for i in range(lax.axis_size(axis))])


def crossed(value, axis, bits):
    return lax.ppermute(value, axis, [(i, i ^ bits) for i in range(lax.axis_size(axis))])


def from_behind(value, axis, steps):
    count = lax.axis_size(axis)
    return lax.ppermute(value, axis, [(i, (i + steps) % count) for i in range(count)])


def bits_of(axis):
    return lax.axis_size(axis).bit_length() - 1


def my_bit(axis, bit):
    return (lax.axis_index(axis) >> bit) & 1


def pick(value, index, dim):
    return lax.dynamic_index_in_dim(value, index, dim, keepdims=False)


def tie(value, *deps):
    return lax.optimization_barrier((value, deps))[0]


class Chain:
    def __init__(self):
        self.token = None

    def enter(self, *values):
        out = values if self.token is None else tie(values, self.token)
        return out[0] if len(values) == 1 else out

    def leave(self, array):
        self.token = array


def turn(value, cosine, sine):
    return value * cosine + pltpu.roll(value, HD // 2, 1) * sine


def rows_of(keeps, arrivals, inverse, columns):
    parts = [k[:, columns] + a[:, columns].astype(F32) for k, a in zip(keeps, arrivals)]
    return jnp.concatenate(parts, axis=0) * inverse[...]


def kv_kernel(qw, kvw, keep_a, keep_b, arr_a, arr_b, inverse, cosine, sine, out):
    for start in range(0, 2 * kvw, HD):
        columns = slice(qw + start, qw + start + HD)
        value = rows_of((keep_a, keep_b), (arr_a, arr_b), inverse, columns)
        if start < kvw:
            value = turn(value, cosine[...], sine[...])
        out[:, start : start + HD] = value.astype(BF16)


def attention_kernel(
    qw, kvw, count, keep_a, keep_b, arr_a, arr_b, inverse, cosine, sine, q_pos, k_pos, *rest
):
    pairs, (out, keys, values, bias) = rest[:count], rest[count:]
    rows = pairs[0].shape[0]
    for i, pair in enumerate(pairs):
        keys[i * rows : (i + 1) * rows] = pair[:, :kvw]
        values[i * rows : (i + 1) * rows] = pair[:, kvw:]
    bias[...] = jnp.where(q_pos[...] >= k_pos[...], 0.0, HIDDEN)
    group = (qw // HD) // (kvw // HD)
    for head in range(qw // HD):
        columns = slice(head * HD, (head + 1) * HD)
        kv_columns = slice(head // group * HD, (head // group + 1) * HD)
        query = rows_of((keep_a, keep_b), (arr_a, arr_b), inverse, columns)
        query = turn(query, cosine[...], sine[...]).astype(BF16)
        scores = lax.dot_general(
            query, keys[:, kv_columns], (((1,), (1,)), ((), ())), preferred_element_type=F32
        )
        scores = scores + bias[...]
        top = jnp.max(scores, axis=1, keepdims=True)
        probs = jnp.exp2((scores - top) * (LOG2E / HD**0.5))
        total = jnp.sum(probs, axis=1, keepdims=True)
        mixed = jnp.dot(probs.astype(BF16), values[:, kv_columns], preferred_element_type=F32)
        out[:, columns] = (mixed / total).astype(BF16)


def gather(block, axis):
    blocks = {0: block}
    for bit in range(1, bits_of(axis)):
        for o in list(blocks):
            blocks[o | 1 << bit] = swapped(blocks[o], axis, bit)
    return blocks


class Cascade:
    def __init__(self, x, gain, wq, wk, wv, wo):
        self.x, self.gain, self.wo = x, gain, wo
        if wk.shape[1] < HD:
            other_k, other_v = swapped((wk, wv), "row", 0)
            even = lax.axis_index("row") % 2 == 0
            wk = jnp.where(even, jnp.concatenate([wk, other_k], 1), jnp.concatenate([other_k, wk], 1))
            wv = jnp.where(even, jnp.concatenate([wv, other_v], 1), jnp.concatenate([other_v, wv], 1))
        self.qw, self.kvw = wq.shape[1], wk.shape[1]
        self.w = jnp.concatenate([wq, wk, wv], axis=1)
        self.n_row, self.n_col = lax.axis_size("row"), lax.axis_size("col")
        self.sub = x.shape[0] // self.n_col
        self.keep, self.arrived = [], []

    def halves(self, block_list):
        low = my_bit("col", 0)
        blocks = jnp.stack(block_list).reshape(len(block_list), self.n_col // 2, 2, self.sub, -1)
        return pick(blocks, 1 - low, 2), pick(blocks, low, 2)

    def project(self, half):
        scaled = (half.astype(F32) * self.gain).astype(BF16)
        rows = scaled.reshape(-1, scaled.shape[-1])
        out = jnp.dot(rows, self.w, preferred_element_type=F32)
        return out.reshape(half.shape[:-1] + (-1,))

    def halve(self, total, arrived, bit):
        mine = my_bit("col", bit)
        shape = (total.shape[0], -1, 2) + total.shape[2:]
        total, arrived = total.reshape(shape), arrived.reshape(shape)

        def part(which):
            return pick(total, which, 2) + pick(arrived, which, 2).astype(F32)

        return part(mine), part(1 - mine).astype(BF16)

    def flat(self, value):
        return value.reshape(-1, value.shape[-1])

    def kernel_rows(self):
        return [self.flat(v) for v in self.keep] + [self.flat(v) for v in self.arrived]


def whole(body, out_shape, scratch=(), flops=0, exps=0, moved=0):
    return pl.pallas_call(
        body,
        out_shape=out_shape,
        scratch_shapes=list(scratch),
        compiler_params=pltpu.CompilerParams(vmem_limit_bytes=40 * 1024 * 1024),
        cost_estimate=pl.CostEstimate(flops=flops, transcendentals=exps, bytes_accessed=moved),
    )


def on_device(*arrays):
    arrays = [a[0] for a in arrays]
    half = len(arrays) // 2
    d, u = Cascade(*arrays[:half]), Cascade(*arrays[half:])
    n_row, n_col, sub = d.n_row, d.n_col, d.sub
    block = n_col * sub
    features = d.x.shape[1] * n_col
    rows = n_row * sub
    qw, kvw = d.qw, d.kvw
    z, r = lax.axis_index("col"), lax.axis_index("row")
    chain = Chain()

    order = [o for o in range(n_row) if o < 2] + [o for o in range(n_row) if o >= 2]
    starts = (r ^ jnp.array(order, jnp.int32)) * block
    offsets = jnp.arange(sub, dtype=jnp.int32)
    q_pos = (starts[:, None] + z * sub + offsets).astype(F32).reshape(rows, 1)
    owners = (z ^ jnp.arange(n_col, dtype=jnp.int32)) * sub
    k_pos = (owners[:, None, None] + starts[:, None] + offsets).astype(F32).reshape(1, -1)
    width = HD // 2
    inverse_freq = 10000.0 ** (-jnp.arange(width, dtype=F32) / width)
    angles = q_pos * inverse_freq
    cosine = jnp.concatenate([jnp.cos(angles)] * 2, axis=1)
    sine = jnp.sin(angles)
    sine = jnp.concatenate([-sine, sine], axis=1)

    d_blocks = gather(d.x, "row")
    d_blocks[1] = swapped(d.x, "row", 0)
    squares = jnp.stack([jnp.sum(jnp.square(c.x.astype(F32)), axis=1) for c in (d, u)])
    squares = lax.all_gather(squares, ("row", "col")).reshape(n_row, n_col, 2, block)

    def send_first(c, group, blocks_):
        send, kept = c.halves(chain.enter(*blocks_))
        product = c.project(send).astype(BF16)
        return product, kept

    def keep_first(c, kept, token):
        return c.project(tie(kept, token))

    def second(c, total, arrived):
        total, arrived = chain.enter(total, arrived)
        kept, product = c.halve(total, arrived, 1)
        arrived = swapped(product, "col", 1)
        chain.leave(product)
        for bit in range(2, bits_of("col")):
            kept, product = c.halve(kept, arrived, bit)
            arrived = swapped(product, "col", bit)
        c.keep.append(kept)
        c.arrived.append(arrived)

    def settle(c):
        c.arrived[-1] = chain.enter(c.arrived[-1])
        chain.leave(c.arrived[-1])

    def take_far(blocks_):
        values = chain.enter(*[blocks_[o] for o in far])
        values = list(values) if len(far) > 1 else [values]
        for o, value in zip(far, values):
            blocks_[o] = value
            blocks_[o | 1] = swapped(value, "row", 0)
        chain.leave(values[-1])
        return values

    far = [o for o in d_blocks if o >= 2]
    far_order = [o for o in order if o >= 2]

    product, kept = send_first(d, 0, [d_blocks[0], d_blocks[1]])
    d_arr_a = swapped(product, "col", 0)
    d_tot_a = keep_first(d, kept, product)
    u_near = swapped(tie(u.x, product), "row", 0)
    chain.leave(d_tot_a)
    u_prod_a, kept = send_first(u, 0, [u.x, u_near])
    u_tot_a = keep_first(u, kept, u_prod_a)
    chain.leave(u_tot_a)
    second(d, d_tot_a, d_arr_a)

    d_far = take_far(d_blocks)
    u_blocks = gather(tie(u.x, *d_far), "row")
    product, kept = send_first(d, 1, [d_blocks[o] for o in far_order])
    d_arr_b = swapped(product, "col", 0)
    d_tot_b = keep_first(d, kept, product)
    chain.leave(d_tot_b)
    settle(d)
    second(d, d_tot_b, d_arr_b)
    u_arr_a = swapped(tie(u_prod_a, chain.token), "col", 0)

    take_far(u_blocks)
    u_prod_b, kept = send_first(u, 1, [u_blocks[o] for o in far_order])
    u_tot_b = keep_first(u, kept, u_prod_b)
    chain.leave(u_tot_b)

    sums = jnp.sum(pick(squares.reshape(n_row, n_col, 2, n_col, sub), z, 3), axis=1)
    inverse = lax.rsqrt(sums / features + EPSILON)
    inverse = jnp.stack([pick(inverse, r ^ o, 0) for o in order], axis=1).reshape(2, rows, 1)

    def make_pairs(c, scale):
        inputs = chain.enter(*c.kernel_rows())
        pair = whole(
            functools.partial(kv_kernel, qw, kvw),
            jax.ShapeDtypeStruct((rows, 2 * kvw), BF16),
            moved=2 * rows * (qw + 2 * kvw) * 6,
        )(*inputs, scale, cosine, sine)
        chain.leave(pair)
        return inputs, [pair] + [crossed(pair, "col", o) for o in range(1, n_col)]

    def attend(c, inputs, scale, pairs):
        pairs = chain.enter(*pairs)
        keys = rows * n_col
        out = whole(
            functools.partial(attention_kernel, qw, kvw, n_col),
            jax.ShapeDtypeStruct((rows, qw), BF16),
            scratch=[pltpu.VMEM((keys, kvw), BF16), pltpu.VMEM((keys, kvw), BF16), pltpu.VMEM((rows, keys), F32)],
            flops=4 * rows * keys * qw,
            exps=rows * keys * qw // HD,
            moved=rows * qw * 8,
        )(*inputs, scale, cosine, sine, q_pos, k_pos, *pairs)
        chain.leave(out)
        return out

    second(u, u_tot_a, u_arr_a)
    u_arr_b = swapped(tie(u_prod_b, chain.token), "col", 0)
    d_inputs, d_pairs = make_pairs(d, inverse[0])
    settle(u)
    d_att = attend(d, d_inputs, inverse[0], d_pairs)
    d_got = gather(d_att, "col")
    d_got[1] = swapped(d_att, "col", 0)
    second(u, u_tot_b, u_arr_b)

    def out_first(c, pieces):
        pieces = chain.enter(*pieces)
        pieces = pieces if isinstance(pieces, (list, tuple)) else [pieces]
        shaped = jnp.stack([p.reshape(n_row // 2, 2, sub, qw) for p in pieces], axis=2)

        def dot(value):
            out = jnp.dot(value.reshape(-1, qw), c.wo, preferred_element_type=F32)
            return out.reshape(n_row // 2, -1, c.wo.shape[1])

        product = dot(shaped[:, 1]).astype(BF16)
        arrived = swapped(product, "row", 0)
        kept = dot(tie(shaped[:, 0], product))
        chain.leave(kept)
        return kept, arrived

    def out_second(kept, arrived):
        kept, arrived = chain.enter(kept, arrived)
        for bit in range(1, bits_of("row")):
            total = (kept + arrived.astype(F32)).reshape(-1, 2, *kept.shape[1:])
            product = total[:, 1].astype(BF16)
            kept, arrived = total[:, 0], swapped(product, "row", bit)
        chain.leave(product)
        return kept, arrived

    def out_third(c, kept, arrived, which, steps):
        kept, arrived = chain.enter(kept, arrived)
        residual = c.x.reshape(n_col, sub, -1)
        own = jnp.stack([pick(residual, z ^ o, 0) for o in which]).astype(F32)
        total = kept[0] + arrived[0].astype(F32)
        fresh = (own + total.reshape(own.shape)).astype(BF16)
        chain.leave(fresh)
        return from_behind(fresh, "section", steps)

    def finish(c, sent_p, sent_q):
        both = jnp.concatenate([sent_p, sent_q]).reshape((2,) * bits_of("col") + (sub, -1))
        for bit in range(bits_of("col")):
            dim = bits_of("col") - 1 - bit
            both = jnp.where(my_bit("col", bit) == 0, both, jnp.flip(both, dim))
        return both.reshape(c.x.shape)[None]

    def far_pieces(got):
        names = [o for o in got if o >= 2]
        values = chain.enter(*[got[o] for o in names])
        values = list(values) if len(names) > 1 else [values]
        chain.leave(values[-1])
        for o, value in zip(names, values):
            got[o] = value
            got[o | 1] = swapped(value, "col", 0)

    near_names, far_names = [0, 1], list(range(2, n_col))
    far_pieces(d_got)
    d_p = out_first(d, [d_got[o] for o in near_names])
    u_inputs, u_pairs = make_pairs(u, inverse[1])
    d_p = out_second(*d_p)
    u_att = attend(u, u_inputs, inverse[1], u_pairs)
    u_got = gather(u_att, "col")
    u_got[1] = swapped(u_att, "col", 0)
    d_q = out_first(d, [d_got[o] for o in far_names])
    d_p = out_third(d, *d_p, near_names, 1)
    d_q = out_second(*d_q)
    far_pieces(u_got)
    u_p = out_first(u, [u_got[o] for o in near_names])
    u_p = out_second(*u_p)
    d_q = out_third(d, *d_q, far_names, 1)
    u_q = out_first(u, [u_got[o] for o in far_names])
    u_p = out_third(u, *u_p, near_names, -1)
    u_q = out_second(*u_q)
    u_q = out_third(u, *u_q, far_names, -1)
    return finish(d, d_p, d_q), finish(u, u_p, u_q)


def solution(mesh):
    tokens = P("section", "row", "col")
    into, out_of = P("section", "col", "row"), P("section", "row", "col")
    one = (tokens, P("section", "col"), into, into, into, out_of)
    return jax.shard_map(
        on_device, mesh=mesh, in_specs=one + one, out_specs=(tokens, tokens), check_vma=False
    )
```

```python
import functools

import jax
import jax.numpy as jnp
from jax import lax
from jax.experimental import pallas as pl
from jax.experimental.pallas import tpu as pltpu
from jax.sharding import PartitionSpec as P

HD = 128
EPSILON = 1e-05
HIDDEN = -1e30
LOG2E = 1.4426950408889634
BF16 = jnp.bfloat16
F32 = jnp.float32


def swapped(value, axis, bit):
    return lax.ppermute(value, axis, [(i, i ^ (1 << bit)) for i in range(lax.axis_size(axis))])


def crossed(value, axis, bits):
    return lax.ppermute(value, axis, [(i, i ^ bits) for i in range(lax.axis_size(axis))])


def from_behind(value, axis, steps):
    count = lax.axis_size(axis)
    return lax.ppermute(value, axis, [(i, (i + steps) % count) for i in range(count)])


def bits_of(axis):
    return lax.axis_size(axis).bit_length() - 1


def my_bit(axis, bit):
    return (lax.axis_index(axis) >> bit) & 1


def pick(value, index, dim):
    return lax.dynamic_index_in_dim(value, index, dim, keepdims=False)


def tie(value, *deps):
    return lax.optimization_barrier((value, deps))[0]


class Chain:
    def __init__(self):
        self.token = None

    def enter(self, *values):
        out = values if self.token is None else tie(values, self.token)
        return out[0] if len(values) == 1 else out

    def leave(self, array):
        self.token = array


def turn(value, cosine, sine):
    return value * cosine + pltpu.roll(value, HD // 2, 1) * sine


def rows_of(keeps, arrivals, inverse, columns):
    parts = [k[:, columns] + a[:, columns].astype(F32) for k, a in zip(keeps, arrivals)]
    return jnp.concatenate(parts, axis=0) * inverse[...]


def kv_kernel(qw, kvw, keep_a, keep_b, arr_a, arr_b, inverse, cosine, sine, out):
    for start in range(0, 2 * kvw, HD):
        columns = slice(qw + start, qw + start + HD)
        value = rows_of((keep_a, keep_b), (arr_a, arr_b), inverse, columns)
        if start < kvw:
            value = turn(value, cosine[...], sine[...])
        out[:, start : start + HD] = value.astype(BF16)


def attention_kernel(
    qw, kvw, count, keep_a, keep_b, arr_a, arr_b, inverse, cosine, sine, q_pos, k_pos, *rest
):
    pairs, (out, keys, values, bias) = rest[:count], rest[count:]
    rows = pairs[0].shape[0]
    for i, pair in enumerate(pairs):
        keys[i * rows : (i + 1) * rows] = pair[:, :kvw]
        values[i * rows : (i + 1) * rows] = pair[:, kvw:]
    bias[...] = jnp.where(q_pos[...] >= k_pos[...], 0.0, HIDDEN)
    group = (qw // HD) // (kvw // HD)
    for head in range(qw // HD):
        columns = slice(head * HD, (head + 1) * HD)
        kv_columns = slice(head // group * HD, (head // group + 1) * HD)
        query = rows_of((keep_a, keep_b), (arr_a, arr_b), inverse, columns)
        query = turn(query, cosine[...], sine[...]).astype(BF16)
        scores = lax.dot_general(
            query, keys[:, kv_columns], (((1,), (1,)), ((), ())), preferred_element_type=F32
        )
        scores = scores + bias[...]
        top = jnp.max(scores, axis=1, keepdims=True)
        probs = jnp.exp2((scores - top) * (LOG2E / HD**0.5))
        total = jnp.sum(probs, axis=1, keepdims=True)
        mixed = jnp.dot(probs.astype(BF16), values[:, kv_columns], preferred_element_type=F32)
        out[:, columns] = (mixed / total).astype(BF16)


def gather(block, axis):
    blocks = {0: block}
    for bit in range(1, bits_of(axis)):
        for o in list(blocks):
            blocks[o | 1 << bit] = swapped(blocks[o], axis, bit)
    return blocks


class Cascade:
    def __init__(self, x, gain, wq, wk, wv, wo):
        self.x, self.gain, self.wo = x, gain, wo
        if wk.shape[1] < HD:
            other_k, other_v = swapped((wk, wv), "row", 0)
            even = lax.axis_index("row") % 2 == 0
            wk = jnp.where(even, jnp.concatenate([wk, other_k], 1), jnp.concatenate([other_k, wk], 1))
            wv = jnp.where(even, jnp.concatenate([wv, other_v], 1), jnp.concatenate([other_v, wv], 1))
        self.qw, self.kvw = wq.shape[1], wk.shape[1]
        self.w = jnp.concatenate([wq, wk, wv], axis=1)
        self.n_row, self.n_col = lax.axis_size("row"), lax.axis_size("col")
        self.sub = x.shape[0] // self.n_col
        self.keep, self.arrived = [], []

    def halves(self, block_list):
        low = my_bit("col", 0)
        blocks = jnp.stack(block_list).reshape(len(block_list), self.n_col // 2, 2, self.sub, -1)
        return pick(blocks, 1 - low, 2), pick(blocks, low, 2)

    def project(self, half):
        scaled = (half.astype(F32) * self.gain).astype(BF16)
        rows = scaled.reshape(-1, scaled.shape[-1])
        out = jnp.dot(rows, self.w, preferred_element_type=F32)
        return out.reshape(half.shape[:-1] + (-1,))

    def halve(self, total, arrived, bit):
        mine = my_bit("col", bit)
        shape = (total.shape[0], -1, 2) + total.shape[2:]
        total, arrived = total.reshape(shape), arrived.reshape(shape)

        def part(which):
            return pick(total, which, 2) + pick(arrived, which, 2).astype(F32)

        return part(mine), part(1 - mine).astype(BF16)

    def flat(self, value):
        return value.reshape(-1, value.shape[-1])

    def kernel_rows(self):
        return [self.flat(v) for v in self.keep] + [self.flat(v) for v in self.arrived]


def whole(body, out_shape, scratch=(), flops=0, exps=0, moved=0):
    return pl.pallas_call(
        body,
        out_shape=out_shape,
        scratch_shapes=list(scratch),
        compiler_params=pltpu.CompilerParams(vmem_limit_bytes=40 * 1024 * 1024),
        cost_estimate=pl.CostEstimate(flops=flops, transcendentals=exps, bytes_accessed=moved),
    )


def on_device(*arrays):
    arrays = [a[0] for a in arrays]
    half = len(arrays) // 2
    d, u = Cascade(*arrays[:half]), Cascade(*arrays[half:])
    n_row, n_col, sub = d.n_row, d.n_col, d.sub
    block = n_col * sub
    features = d.x.shape[1] * n_col
    rows = n_row * sub
    qw, kvw = d.qw, d.kvw
    z, r = lax.axis_index("col"), lax.axis_index("row")
    chain = Chain()

    order = [o for o in range(n_row) if o < 2] + [o for o in range(n_row) if o >= 2]
    starts = (r ^ jnp.array(order, jnp.int32)) * block
    offsets = jnp.arange(sub, dtype=jnp.int32)
    q_pos = (starts[:, None] + z * sub + offsets).astype(F32).reshape(rows, 1)
    owners = (z ^ jnp.arange(n_col, dtype=jnp.int32)) * sub
    k_pos = (owners[:, None, None] + starts[:, None] + offsets).astype(F32).reshape(1, -1)
    width = HD // 2
    inverse_freq = 10000.0 ** (-jnp.arange(width, dtype=F32) / width)
    angles = q_pos * inverse_freq
    cosine = jnp.concatenate([jnp.cos(angles)] * 2, axis=1)
    sine = jnp.sin(angles)
    sine = jnp.concatenate([-sine, sine], axis=1)

    d_blocks = gather(d.x, "row")
    d_blocks[1] = swapped(d.x, "row", 0)
    squares = jnp.stack([jnp.sum(jnp.square(c.x.astype(F32)), axis=1) for c in (d, u)])
    other = swapped(squares, "col", 0)

    def send_first(c, group, blocks_):
        send, kept = c.halves(chain.enter(*blocks_))
        product = c.project(send).astype(BF16)
        return product, kept

    def keep_first(c, kept, token):
        return c.project(tie(kept, token))

    def second(c, total, arrived):
        total, arrived = chain.enter(total, arrived)
        kept, product = c.halve(total, arrived, 1)
        arrived = swapped(product, "col", 1)
        chain.leave(product)
        for bit in range(2, bits_of("col")):
            kept, product = c.halve(kept, arrived, bit)
            arrived = swapped(product, "col", bit)
        c.keep.append(kept)
        c.arrived.append(arrived)

    def settle(c):
        c.arrived[-1] = chain.enter(c.arrived[-1])
        chain.leave(c.arrived[-1])

    def take_far(blocks_):
        values = chain.enter(*[blocks_[o] for o in far])
        values = list(values) if len(far) > 1 else [values]
        for o, value in zip(far, values):
            blocks_[o] = value
            blocks_[o | 1] = swapped(value, "row", 0)
        chain.leave(values[-1])
        return values

    far = [o for o in d_blocks if o >= 2]
    far_order = [o for o in order if o >= 2]

    product, kept = send_first(d, 0, [d_blocks[0], d_blocks[1]])
    d_arr_a = swapped(product, "col", 0)
    d_tot_a = keep_first(d, kept, product)
    u_near = swapped(tie(u.x, product), "row", 0)
    chain.leave(d_tot_a)
    squares, other = chain.enter(squares, other)
    squares = squares + other
    other = swapped(squares, "col", 1)
    chain.leave(squares)
    u_prod_a, kept = send_first(u, 0, [u.x, u_near])
    u_tot_a = keep_first(u, kept, u_prod_a)
    chain.leave(u_tot_a)
    second(d, d_tot_a, d_arr_a)
    u_arr_a = swapped(tie(u_prod_a, chain.token), "col", 0)
    squares, other = chain.enter(squares, other)
    squares = squares + other
    for bit in range(2, bits_of("col")):
        squares = squares + swapped(squares, "col", bit)
    chain.leave(squares)
    sq = gather(squares, "row")

    d_far = take_far(d_blocks)
    u_blocks = gather(tie(u.x, *d_far), "row")
    product, kept = send_first(d, 1, [d_blocks[o] for o in far_order])
    d_arr_b = swapped(product, "col", 0)
    d_tot_b = keep_first(d, kept, product)
    chain.leave(d_tot_b)
    settle(d)
    second(u, u_tot_a, u_arr_a)
    second(d, d_tot_b, d_arr_b)

    settle(u)
    take_far(u_blocks)
    for o in list(sq):
        sq[o | 1] = swapped(tie(sq[o], chain.token), "row", 0)
    u_prod_b, kept = send_first(u, 1, [u_blocks[o] for o in far_order])
    u_arr_b = swapped(u_prod_b, "col", 0)
    u_tot_b = keep_first(u, kept, u_prod_b)
    chain.leave(u_tot_b)

    sums = jnp.stack([sq[o] for o in order])
    sums = pick(sums.reshape(n_row, 2, n_col, sub), z, 2)
    inverse = lax.rsqrt(sums / features + EPSILON).transpose(1, 0, 2).reshape(2, rows, 1)

    def make_pairs(c, scale):
        inputs = chain.enter(*c.kernel_rows())
        pair = whole(
            functools.partial(kv_kernel, qw, kvw),
            jax.ShapeDtypeStruct((rows, 2 * kvw), BF16),
            moved=2 * rows * (qw + 2 * kvw) * 6,
        )(*inputs, scale, cosine, sine)
        chain.leave(pair)
        return inputs, [pair] + [crossed(pair, "col", o) for o in range(1, n_col)]

    def attend(c, inputs, scale, pairs):
        pairs = chain.enter(*pairs)
        keys = rows * n_col
        out = whole(
            functools.partial(attention_kernel, qw, kvw, n_col),
            jax.ShapeDtypeStruct((rows, qw), BF16),
            scratch=[pltpu.VMEM((keys, kvw), BF16), pltpu.VMEM((keys, kvw), BF16), pltpu.VMEM((rows, keys), F32)],
            flops=4 * rows * keys * qw,
            exps=rows * keys * qw // HD,
            moved=rows * qw * 8,
        )(*inputs, scale, cosine, sine, q_pos, k_pos, *pairs)
        chain.leave(out)
        return out

    d_inputs, d_pairs = make_pairs(d, inverse[0])
    d_pairs = list(chain.enter(*d_pairs))
    chain.leave(d_pairs[-1])
    second(u, u_tot_b, u_arr_b)
    d_att = attend(d, d_inputs, inverse[0], d_pairs)
    d_got = gather(d_att, "col")
    d_got[1] = swapped(d_att, "col", 0)
    u_inputs, u_pairs = make_pairs(u, inverse[1])
    u_att = attend(u, u_inputs, inverse[1], u_pairs)
    u_got = gather(u_att, "col")
    u_got[1] = swapped(u_att, "col", 0)

    def out_first(c, pieces):
        pieces = chain.enter(*pieces)
        pieces = pieces if isinstance(pieces, (list, tuple)) else [pieces]
        shaped = jnp.stack([p.reshape(n_row // 2, 2, sub, qw) for p in pieces], axis=2)

        def dot(value):
            out = jnp.dot(value.reshape(-1, qw), c.wo, preferred_element_type=F32)
            return out.reshape(n_row // 2, -1, c.wo.shape[1])

        product = dot(shaped[:, 1]).astype(BF16)
        arrived = swapped(product, "row", 0)
        kept = dot(tie(shaped[:, 0], product))
        chain.leave(kept)
        return kept, arrived

    def out_second(kept, arrived):
        kept, arrived = chain.enter(kept, arrived)
        for bit in range(1, bits_of("row")):
            total = (kept + arrived.astype(F32)).reshape(-1, 2, *kept.shape[1:])
            product = total[:, 1].astype(BF16)
            kept, arrived = total[:, 0], swapped(product, "row", bit)
        chain.leave(product)
        return kept, arrived

    def out_third(c, kept, arrived, which, steps):
        kept, arrived = chain.enter(kept, arrived)
        residual = c.x.reshape(n_col, sub, -1)
        own = jnp.stack([pick(residual, z ^ o, 0) for o in which]).astype(F32)
        total = kept[0] + arrived[0].astype(F32)
        fresh = (own + total.reshape(own.shape)).astype(BF16)
        chain.leave(fresh)
        return from_behind(fresh, "section", steps)

    def finish(c, sent_p, sent_q):
        both = jnp.concatenate([sent_p, sent_q]).reshape((2,) * bits_of("col") + (sub, -1))
        for bit in range(bits_of("col")):
            dim = bits_of("col") - 1 - bit
            both = jnp.where(my_bit("col", bit) == 0, both, jnp.flip(both, dim))
        return both.reshape(c.x.shape)[None]

    def far_pieces(got):
        names = [o for o in got if o >= 2]
        values = chain.enter(*[got[o] for o in names])
        values = list(values) if len(names) > 1 else [values]
        chain.leave(values[-1])
        for o, value in zip(names, values):
            got[o] = value
            got[o | 1] = swapped(value, "col", 0)

    near_names, far_names = [0, 1], list(range(2, n_col))
    far_pieces(d_got)
    d_p = out_first(d, [d_got[o] for o in near_names])
    d_p = out_second(*d_p)
    d_q = out_first(d, [d_got[o] for o in far_names])
    d_p = out_third(d, *d_p, near_names, 1)
    d_q = out_second(*d_q)
    far_pieces(u_got)
    u_p = out_first(u, [u_got[o] for o in near_names])
    u_p = out_second(*u_p)
    d_q = out_third(d, *d_q, far_names, 1)
    u_q = out_first(u, [u_got[o] for o in far_names])
    u_p = out_third(u, *u_p, near_names, -1)
    u_q = out_second(*u_q)
    u_q = out_third(u, *u_q, far_names, -1)
    return finish(d, d_p, d_q), finish(u, u_p, u_q)


def solution(mesh):
    tokens = P("section", "row", "col")
    into, out_of = P("section", "col", "row"), P("section", "row", "col")
    one = (tokens, P("section", "col"), into, into, into, out_of)
    return jax.shard_map(
        on_device, mesh=mesh, in_specs=one + one, out_specs=(tokens, tokens), check_vma=False
    )
```

```python
import functools

import jax
import jax.numpy as jnp
from jax import lax
from jax.experimental import pallas as pl
from jax.experimental.pallas import tpu as pltpu
from jax.sharding import PartitionSpec as P

HD = 128
EPSILON = 1e-05
HIDDEN = -1e30
LOG2E = 1.4426950408889634
BF16 = jnp.bfloat16
F32 = jnp.float32


def swapped(value, axis, bit):
    return lax.ppermute(value, axis, [(i, i ^ (1 << bit)) for i in range(lax.axis_size(axis))])


def crossed(value, axis, bits):
    return lax.ppermute(value, axis, [(i, i ^ bits) for i in range(lax.axis_size(axis))])


def from_behind(value, axis, steps):
    count = lax.axis_size(axis)
    return lax.ppermute(value, axis, [(i, (i + steps) % count) for i in range(count)])


def bits_of(axis):
    return lax.axis_size(axis).bit_length() - 1


def my_bit(axis, bit):
    return (lax.axis_index(axis) >> bit) & 1


def pick(value, index, dim):
    return lax.dynamic_index_in_dim(value, index, dim, keepdims=False)


def tie(value, *deps):
    return lax.optimization_barrier((value, deps))[0]


class Chain:
    def __init__(self):
        self.token = None

    def enter(self, *values):
        out = values if self.token is None else tie(values, self.token)
        return out[0] if len(values) == 1 else out

    def leave(self, array):
        self.token = array


def turn(value, cosine, sine):
    return value * cosine + pltpu.roll(value, HD // 2, 1) * sine


def rows_of(keeps, arrivals, inverse, columns):
    parts = [k[:, columns] + a[:, columns].astype(F32) for k, a in zip(keeps, arrivals)]
    return jnp.concatenate(parts, axis=0) * inverse[...]


def kv_kernel(qw, kvw, keep_a, keep_b, arr_a, arr_b, inverse, cosine, sine, out):
    for start in range(0, 2 * kvw, HD):
        columns = slice(qw + start, qw + start + HD)
        value = rows_of((keep_a, keep_b), (arr_a, arr_b), inverse, columns)
        if start < kvw:
            value = turn(value, cosine[...], sine[...])
        out[:, start : start + HD] = value.astype(BF16)


def attention_kernel(
    qw, kvw, count, keep_a, keep_b, arr_a, arr_b, inverse, cosine, sine, q_pos, k_pos, *rest
):
    pairs, (out, keys, values, bias) = rest[:count], rest[count:]
    rows = pairs[0].shape[0]
    for i, pair in enumerate(pairs):
        keys[i * rows : (i + 1) * rows] = pair[:, :kvw]
        values[i * rows : (i + 1) * rows] = pair[:, kvw:]
    bias[...] = jnp.where(q_pos[...] >= k_pos[...], 0.0, HIDDEN)
    group = (qw // HD) // (kvw // HD)
    for head in range(qw // HD):
        columns = slice(head * HD, (head + 1) * HD)
        kv_columns = slice(head // group * HD, (head // group + 1) * HD)
        query = rows_of((keep_a, keep_b), (arr_a, arr_b), inverse, columns)
        query = turn(query, cosine[...], sine[...]).astype(BF16)
        scores = lax.dot_general(
            query, keys[:, kv_columns], (((1,), (1,)), ((), ())), preferred_element_type=F32
        )
        scores = scores + bias[...]
        top = jnp.max(scores, axis=1, keepdims=True)
        probs = jnp.exp2((scores - top) * (LOG2E / HD**0.5))
        total = jnp.sum(probs, axis=1, keepdims=True)
        mixed = jnp.dot(probs.astype(BF16), values[:, kv_columns], preferred_element_type=F32)
        out[:, columns] = (mixed / total).astype(BF16)


def gather(block, axis):
    blocks = {0: block}
    for bit in range(1, bits_of(axis)):
        for o in list(blocks):
            blocks[o | 1 << bit] = swapped(blocks[o], axis, bit)
    return blocks


class Cascade:
    def __init__(self, x, gain, wq, wk, wv, wo):
        self.x, self.gain, self.wo = x, gain, wo
        if wk.shape[1] < HD:
            other_k, other_v = swapped((wk, wv), "row", 0)
            even = lax.axis_index("row") % 2 == 0
            wk = jnp.where(even, jnp.concatenate([wk, other_k], 1), jnp.concatenate([other_k, wk], 1))
            wv = jnp.where(even, jnp.concatenate([wv, other_v], 1), jnp.concatenate([other_v, wv], 1))
        self.qw, self.kvw = wq.shape[1], wk.shape[1]
        self.w = jnp.concatenate([wq, wk, wv], axis=1)
        self.n_row, self.n_col = lax.axis_size("row"), lax.axis_size("col")
        self.sub = x.shape[0] // self.n_col
        self.keep, self.arrived = [], []

    def halves(self, block_list):
        low = my_bit("col", 0)
        blocks = jnp.stack(block_list).reshape(len(block_list), self.n_col // 2, 2, self.sub, -1)
        return pick(blocks, 1 - low, 2), pick(blocks, low, 2)

    def project(self, half):
        scaled = (half.astype(F32) * self.gain).astype(BF16)
        rows = scaled.reshape(-1, scaled.shape[-1])
        out = jnp.dot(rows, self.w, preferred_element_type=F32)
        return out.reshape(half.shape[:-1] + (-1,))

    def halve(self, total, arrived, bit):
        mine = my_bit("col", bit)
        shape = (total.shape[0], -1, 2) + total.shape[2:]
        total, arrived = total.reshape(shape), arrived.reshape(shape)

        def part(which):
            return pick(total, which, 2) + pick(arrived, which, 2).astype(F32)

        return part(mine), part(1 - mine).astype(BF16)

    def flat(self, value):
        return value.reshape(-1, value.shape[-1])

    def kernel_rows(self):
        return [self.flat(v) for v in self.keep] + [self.flat(v) for v in self.arrived]


def whole(body, out_shape, scratch=(), flops=0, exps=0, moved=0):
    return pl.pallas_call(
        body,
        out_shape=out_shape,
        scratch_shapes=list(scratch),
        compiler_params=pltpu.CompilerParams(vmem_limit_bytes=40 * 1024 * 1024),
        cost_estimate=pl.CostEstimate(flops=flops, transcendentals=exps, bytes_accessed=moved),
    )


def on_device(*arrays):
    arrays = [a[0] for a in arrays]
    half = len(arrays) // 2
    d, u = Cascade(*arrays[:half]), Cascade(*arrays[half:])
    n_row, n_col, sub = d.n_row, d.n_col, d.sub
    block = n_col * sub
    features = d.x.shape[1] * n_col
    rows = n_row * sub
    qw, kvw = d.qw, d.kvw
    z, r = lax.axis_index("col"), lax.axis_index("row")
    chain = Chain()

    order = [o for o in range(n_row) if o < 2] + [o for o in range(n_row) if o >= 2]
    starts = (r ^ jnp.array(order, jnp.int32)) * block
    offsets = jnp.arange(sub, dtype=jnp.int32)
    q_pos = (starts[:, None] + z * sub + offsets).astype(F32).reshape(rows, 1)
    owners = (z ^ jnp.arange(n_col, dtype=jnp.int32)) * sub
    k_pos = (owners[:, None, None] + starts[:, None] + offsets).astype(F32).reshape(1, -1)
    width = HD // 2
    inverse_freq = 10000.0 ** (-jnp.arange(width, dtype=F32) / width)
    angles = q_pos * inverse_freq
    cosine = jnp.concatenate([jnp.cos(angles)] * 2, axis=1)
    sine = jnp.sin(angles)
    sine = jnp.concatenate([-sine, sine], axis=1)

    d_blocks = gather(d.x, "row")
    d_blocks[1] = swapped(d.x, "row", 0)

    def send_first(c, group, blocks_):
        send, kept = c.halves(chain.enter(*blocks_))
        product = c.project(send).astype(BF16)
        return product, kept

    def keep_first(c, kept, token):
        return c.project(tie(kept, token))

    def second(c, total, arrived):
        total, arrived = chain.enter(total, arrived)
        kept, product = c.halve(total, arrived, 1)
        arrived = swapped(product, "col", 1)
        chain.leave(product)
        for bit in range(2, bits_of("col")):
            kept, product = c.halve(kept, arrived, bit)
            arrived = swapped(product, "col", bit)
        c.keep.append(kept)
        c.arrived.append(arrived)

    def settle(c):
        c.arrived[-1] = chain.enter(c.arrived[-1])
        chain.leave(c.arrived[-1])

    def take_far(blocks_):
        values = chain.enter(*[blocks_[o] for o in far])
        values = list(values) if len(far) > 1 else [values]
        for o, value in zip(far, values):
            blocks_[o] = value
            blocks_[o | 1] = swapped(value, "row", 0)
        chain.leave(values[-1])
        return values

    far = [o for o in d_blocks if o >= 2]
    far_order = [o for o in order if o >= 2]

    product, kept = send_first(d, 0, [d_blocks[0], d_blocks[1]])
    d_arr_a = swapped(product, "col", 0)
    d_tot_a = keep_first(d, kept, product)
    u_near = swapped(tie(u.x, product), "row", 0)
    chain.leave(d_tot_a)
    squares = jnp.stack([jnp.sum(jnp.square(chain.enter(c.x).astype(F32)), axis=1) for c in (d, u)])
    other = swapped(squares, "col", 0)
    chain.leave(squares)
    u_prod_a, kept = send_first(u, 0, [u.x, u_near])
    u_kept = kept
    chain.leave(u_prod_a)
    squares, other = chain.enter(squares, other)
    squares = squares + other
    other = swapped(squares, "col", 1)
    chain.leave(squares)
    second(d, d_tot_a, d_arr_a)
    u_arr_a = swapped(tie(u_prod_a, chain.token), "col", 0)
    squares, other = chain.enter(squares, other)
    squares = squares + other
    for bit in range(2, bits_of("col")):
        squares = squares + swapped(squares, "col", bit)
    chain.leave(squares)
    sq = gather(squares, "row")

    d_far = take_far(d_blocks)
    u_blocks = gather(tie(u.x, *d_far), "row")
    u_tot_a = u.project(chain.enter(u_kept))
    chain.leave(u_tot_a)
    product, kept = send_first(d, 1, [d_blocks[o] for o in far_order])
    d_arr_b = swapped(product, "col", 0)
    d_tot_b = keep_first(d, kept, product)
    chain.leave(d_tot_b)
    settle(d)
    second(u, u_tot_a, u_arr_a)

    take_far(u_blocks)
    second(d, d_tot_b, d_arr_b)
    for o in list(sq):
        sq[o | 1] = swapped(tie(sq[o], chain.token), "row", 0)
    u_prod_b, kept = send_first(u, 1, [u_blocks[o] for o in far_order])
    u_arr_b = swapped(u_prod_b, "col", 0)
    u_tot_b = keep_first(u, kept, u_prod_b)
    chain.leave(u_tot_b)
    settle(u)

    sums = jnp.stack([sq[o] for o in order])
    sums = pick(sums.reshape(n_row, 2, n_col, sub), z, 2)
    inverse = lax.rsqrt(sums / features + EPSILON).transpose(1, 0, 2).reshape(2, rows, 1)

    def make_pairs(c, scale):
        inputs = chain.enter(*c.kernel_rows())
        pair = whole(
            functools.partial(kv_kernel, qw, kvw),
            jax.ShapeDtypeStruct((rows, 2 * kvw), BF16),
            moved=2 * rows * (qw + 2 * kvw) * 6,
        )(*inputs, scale, cosine, sine)
        chain.leave(pair)
        return inputs, [pair] + [crossed(pair, "col", o) for o in range(1, n_col)]

    def attend(c, inputs, scale, pairs):
        pairs = chain.enter(*pairs)
        keys = rows * n_col
        out = whole(
            functools.partial(attention_kernel, qw, kvw, n_col),
            jax.ShapeDtypeStruct((rows, qw), BF16),
            scratch=[pltpu.VMEM((keys, kvw), BF16), pltpu.VMEM((keys, kvw), BF16), pltpu.VMEM((rows, keys), F32)],
            flops=4 * rows * keys * qw,
            exps=rows * keys * qw // HD,
            moved=rows * qw * 8,
        )(*inputs, scale, cosine, sine, q_pos, k_pos, *pairs)
        chain.leave(out)
        return out

    d_inputs, d_pairs = make_pairs(d, inverse[0])
    second(u, u_tot_b, u_arr_b)
    d_att = attend(d, d_inputs, inverse[0], d_pairs)
    d_got = gather(d_att, "col")
    d_got[1] = swapped(d_att, "col", 0)
    u_inputs, u_pairs = make_pairs(u, inverse[1])

    def out_first(c, pieces):
        pieces = chain.enter(*pieces)
        pieces = pieces if isinstance(pieces, (list, tuple)) else [pieces]
        shaped = jnp.stack([p.reshape(n_row // 2, 2, sub, qw) for p in pieces], axis=2)

        def dot(value):
            out = jnp.dot(value.reshape(-1, qw), c.wo, preferred_element_type=F32)
            return out.reshape(n_row // 2, -1, c.wo.shape[1])

        product = dot(shaped[:, 1]).astype(BF16)
        arrived = swapped(product, "row", 0)
        kept = dot(tie(shaped[:, 0], product))
        chain.leave(kept)
        return kept, arrived

    def out_second(kept, arrived):
        kept, arrived = chain.enter(kept, arrived)
        for bit in range(1, bits_of("row")):
            total = (kept + arrived.astype(F32)).reshape(-1, 2, *kept.shape[1:])
            product = total[:, 1].astype(BF16)
            kept, arrived = total[:, 0], swapped(product, "row", bit)
        chain.leave(product)
        return kept, arrived

    def out_third(c, kept, arrived, which, steps):
        kept, arrived = chain.enter(kept, arrived)
        residual = c.x.reshape(n_col, sub, -1)
        own = jnp.stack([pick(residual, z ^ o, 0) for o in which]).astype(F32)
        total = kept[0] + arrived[0].astype(F32)
        fresh = (own + total.reshape(own.shape)).astype(BF16)
        chain.leave(fresh)
        return from_behind(fresh, "section", steps)

    def finish(c, *sent):
        by_name = {o: piece[i] for names, piece in zip(groups, sent) for i, o in enumerate(names)}
        both = jnp.stack([by_name[o] for o in range(n_col)])
        both = both.reshape((2,) * bits_of("col") + (sub, -1))
        for bit in range(bits_of("col")):
            dim = bits_of("col") - 1 - bit
            both = jnp.where(my_bit("col", bit) == 0, both, jnp.flip(both, dim))
        return both.reshape(c.x.shape)[None]

    def far_pieces(got):
        names = [o for o in got if o >= 2]
        values = chain.enter(*[got[o] for o in names])
        values = list(values) if len(names) > 1 else [values]
        chain.leave(values[-1])
        for o, value in zip(names, values):
            got[o] = value
            got[o | 1] = swapped(value, "col", 0)

    groups = [[0, 1], [o for o in range(2, n_col) if o % 2 == 0], [o for o in range(2, n_col) if o % 2]]

    def first(c, got, i):
        return out_first(c, [got[o] for o in groups[i]])

    far_pieces(d_got)
    u_att = attend(u, u_inputs, inverse[1], u_pairs)
    u_got = gather(u_att, "col")
    u_got[1] = swapped(u_att, "col", 0)
    d_p = first(d, d_got, 0)
    d_p = out_second(*d_p)
    d_m = first(d, d_got, 1)
    d_m = out_second(*d_m)
    d_p = out_third(d, *d_p, groups[0], 1)
    d_q = first(d, d_got, 2)
    u_p = first(u, u_got, 0)
    d_q = out_second(*d_q)
    far_pieces(u_got)
    d_m = out_third(d, *d_m, groups[1], 1)
    u_p = out_second(*u_p)
    u_m = first(u, u_got, 1)
    u_m = out_second(*u_m)
    d_q = out_third(d, *d_q, groups[2], 1)
    u_q = first(u, u_got, 2)
    u_p = out_third(u, *u_p, groups[0], -1)
    u_q = out_second(*u_q)
    u_m = out_third(u, *u_m, groups[1], -1)
    u_q = out_third(u, *u_q, groups[2], -1)
    return finish(d, d_p, d_m, d_q), finish(u, u_p, u_m, u_q)


def solution(mesh):
    tokens = P("section", "row", "col")
    into, out_of = P("section", "col", "row"), P("section", "row", "col")
    one = (tokens, P("section", "col"), into, into, into, out_of)
    return jax.shard_map(
        on_device, mesh=mesh, in_specs=one + one, out_specs=(tokens, tokens), check_vma=False
    )
```

```python
import functools

import jax
import jax.numpy as jnp
from jax import lax
from jax.experimental import pallas as pl
from jax.experimental.pallas import tpu as pltpu
from jax.sharding import PartitionSpec as P

HD = 128
EPSILON = 1e-05
HIDDEN = -1e30
LOG2E = 1.4426950408889634
BF16 = jnp.bfloat16
F32 = jnp.float32


def swapped(value, axis, bit):
    return lax.ppermute(value, axis, [(i, i ^ (1 << bit)) for i in range(lax.axis_size(axis))])


def crossed(value, axis, bits):
    return lax.ppermute(value, axis, [(i, i ^ bits) for i in range(lax.axis_size(axis))])


def from_behind(value, axis, steps):
    count = lax.axis_size(axis)
    return lax.ppermute(value, axis, [(i, (i + steps) % count) for i in range(count)])


def bits_of(axis):
    return lax.axis_size(axis).bit_length() - 1


def my_bit(axis, bit):
    return (lax.axis_index(axis) >> bit) & 1


def pick(value, index, dim):
    return lax.dynamic_index_in_dim(value, index, dim, keepdims=False)


def tie(value, *deps):
    return lax.optimization_barrier((value, deps))[0]


class Chain:
    def __init__(self):
        self.token = None

    def enter(self, *values):
        out = values if self.token is None else tie(values, self.token)
        return out[0] if len(values) == 1 else out

    def leave(self, array):
        self.token = array


def turn(value, cosine, sine):
    return value * cosine + pltpu.roll(value, HD // 2, 1) * sine


def rows_of(keeps, arrivals, inverse, columns):
    parts = [k[:, columns] + a[:, columns].astype(F32) for k, a in zip(keeps, arrivals)]
    return jnp.concatenate(parts, axis=0) * inverse[...]


def kv_kernel(qw, kvw, keep_a, keep_b, arr_a, arr_b, inverse, cosine, sine, out):
    for start in range(0, 2 * kvw, HD):
        columns = slice(qw + start, qw + start + HD)
        value = rows_of((keep_a, keep_b), (arr_a, arr_b), inverse, columns)
        if start < kvw:
            value = turn(value, cosine[...], sine[...])
        out[:, start : start + HD] = value.astype(BF16)


def attention_kernel(
    qw, kvw, count, keep_a, keep_b, arr_a, arr_b, inverse, cosine, sine, q_pos, k_pos, *rest
):
    pairs, (out, keys, values, bias) = rest[:count], rest[count:]
    rows = pairs[0].shape[0]
    for i, pair in enumerate(pairs):
        keys[i * rows : (i + 1) * rows] = pair[:, :kvw]
        values[i * rows : (i + 1) * rows] = pair[:, kvw:]
    bias[...] = jnp.where(q_pos[...] >= k_pos[...], 0.0, HIDDEN)
    group = (qw // HD) // (kvw // HD)
    for head in range(qw // HD):
        columns = slice(head * HD, (head + 1) * HD)
        kv_columns = slice(head // group * HD, (head // group + 1) * HD)
        query = rows_of((keep_a, keep_b), (arr_a, arr_b), inverse, columns)
        query = turn(query, cosine[...], sine[...]).astype(BF16)
        scores = lax.dot_general(
            query, keys[:, kv_columns], (((1,), (1,)), ((), ())), preferred_element_type=F32
        )
        scores = scores + bias[...]
        top = jnp.max(scores, axis=1, keepdims=True)
        probs = jnp.exp2((scores - top) * (LOG2E / HD**0.5))
        total = jnp.sum(probs, axis=1, keepdims=True)
        mixed = jnp.dot(probs.astype(BF16), values[:, kv_columns], preferred_element_type=F32)
        out[:, columns] = (mixed / total).astype(BF16)


def gather(block, axis):
    blocks = {0: block}
    for bit in range(1, bits_of(axis)):
        for o in list(blocks):
            blocks[o | 1 << bit] = swapped(blocks[o], axis, bit)
    return blocks


class Cascade:
    def __init__(self, x, gain, wq, wk, wv, wo):
        self.x, self.gain, self.wo = x, gain, wo
        if wk.shape[1] < HD:
            other_k, other_v = swapped((wk, wv), "row", 0)
            even = lax.axis_index("row") % 2 == 0
            wk = jnp.where(even, jnp.concatenate([wk, other_k], 1), jnp.concatenate([other_k, wk], 1))
            wv = jnp.where(even, jnp.concatenate([wv, other_v], 1), jnp.concatenate([other_v, wv], 1))
        self.qw, self.kvw = wq.shape[1], wk.shape[1]
        self.w = jnp.concatenate([wq, wk, wv], axis=1)
        self.n_row, self.n_col = lax.axis_size("row"), lax.axis_size("col")
        self.sub = x.shape[0] // self.n_col
        self.keep, self.arrived = [], []

    def halves(self, block_list):
        low = my_bit("col", 0)
        blocks = jnp.stack(block_list).reshape(len(block_list), self.n_col // 2, 2, self.sub, -1)
        return pick(blocks, 1 - low, 2), pick(blocks, low, 2)

    def project(self, half):
        scaled = (half.astype(F32) * self.gain).astype(BF16)
        rows = scaled.reshape(-1, scaled.shape[-1])
        out = jnp.dot(rows, self.w, preferred_element_type=F32)
        return out.reshape(half.shape[:-1] + (-1,))

    def halve(self, total, arrived, bit):
        mine = my_bit("col", bit)
        shape = (total.shape[0], -1, 2) + total.shape[2:]
        total, arrived = total.reshape(shape), arrived.reshape(shape)

        def part(which):
            return pick(total, which, 2) + pick(arrived, which, 2).astype(F32)

        return part(mine), part(1 - mine).astype(BF16)

    def flat(self, value):
        return value.reshape(-1, value.shape[-1])

    def kernel_rows(self):
        return [self.flat(v) for v in self.keep] + [self.flat(v) for v in self.arrived]


def whole(body, out_shape, scratch=(), flops=0, exps=0, moved=0):
    return pl.pallas_call(
        body,
        out_shape=out_shape,
        scratch_shapes=list(scratch),
        compiler_params=pltpu.CompilerParams(vmem_limit_bytes=40 * 1024 * 1024),
        cost_estimate=pl.CostEstimate(flops=flops, transcendentals=exps, bytes_accessed=moved),
    )


def on_device(*arrays):
    arrays = [a[0] for a in arrays]
    half = len(arrays) // 2
    d, u = Cascade(*arrays[:half]), Cascade(*arrays[half:])
    n_row, n_col, sub = d.n_row, d.n_col, d.sub
    block = n_col * sub
    features = d.x.shape[1] * n_col
    rows = n_row * sub
    qw, kvw = d.qw, d.kvw
    z, r = lax.axis_index("col"), lax.axis_index("row")
    chain = Chain()

    order = [o for o in range(n_row) if o < 2] + [o for o in range(n_row) if o >= 2]
    starts = (r ^ jnp.array(order, jnp.int32)) * block
    offsets = jnp.arange(sub, dtype=jnp.int32)
    q_pos = (starts[:, None] + z * sub + offsets).astype(F32).reshape(rows, 1)
    owners = (z ^ jnp.arange(n_col, dtype=jnp.int32)) * sub
    k_pos = (owners[:, None, None] + starts[:, None] + offsets).astype(F32).reshape(1, -1)
    width = HD // 2
    inverse_freq = 10000.0 ** (-jnp.arange(width, dtype=F32) / width)
    angles = q_pos * inverse_freq
    cosine = jnp.concatenate([jnp.cos(angles)] * 2, axis=1)
    sine = jnp.sin(angles)
    sine = jnp.concatenate([-sine, sine], axis=1)

    d_blocks = gather(d.x, "row")
    d_blocks[1] = swapped(d.x, "row", 0)

    def send_first(c, group, blocks_):
        send, kept = c.halves(chain.enter(*blocks_))
        product = c.project(send).astype(BF16)
        return product, kept

    def keep_first(c, kept, token):
        return c.project(tie(kept, token))

    def second(c, total, arrived):
        total, arrived = chain.enter(total, arrived)
        kept, product = c.halve(total, arrived, 1)
        arrived = swapped(product, "col", 1)
        chain.leave(product)
        for bit in range(2, bits_of("col")):
            kept, product = c.halve(kept, arrived, bit)
            arrived = swapped(product, "col", bit)
        c.keep.append(kept)
        c.arrived.append(arrived)

    def settle(c):
        c.arrived[-1] = chain.enter(c.arrived[-1])
        chain.leave(c.arrived[-1])

    def take_far(blocks_):
        values = chain.enter(*[blocks_[o] for o in far])
        values = list(values) if len(far) > 1 else [values]
        for o, value in zip(far, values):
            blocks_[o] = value
            blocks_[o | 1] = swapped(value, "row", 0)
        chain.leave(values[-1])
        return values

    far = [o for o in d_blocks if o >= 2]
    far_order = [o for o in order if o >= 2]

    product, kept = send_first(d, 0, [d_blocks[0], d_blocks[1]])
    d_arr_a = swapped(product, "col", 0)
    d_tot_a = keep_first(d, kept, product)
    u_near = swapped(tie(u.x, product), "row", 0)
    chain.leave(d_tot_a)
    squares = jnp.stack([jnp.sum(jnp.square(chain.enter(c.x).astype(F32)), axis=1) for c in (d, u)])
    other = swapped(squares, "col", 0)
    chain.leave(squares)
    u_prod_a, kept = send_first(u, 0, [u.x, u_near])
    u_kept = kept
    chain.leave(u_prod_a)
    squares, other = chain.enter(squares, other)
    squares = squares + other
    other = swapped(squares, "col", 1)
    chain.leave(squares)
    second(d, d_tot_a, d_arr_a)
    u_arr_a = swapped(tie(u_prod_a, chain.token), "col", 0)
    squares, other = chain.enter(squares, other)
    squares = squares + other
    for bit in range(2, bits_of("col")):
        squares = squares + swapped(squares, "col", bit)
    chain.leave(squares)
    sq = gather(squares, "row")

    d_far = take_far(d_blocks)
    u_blocks = gather(tie(u.x, *d_far), "row")
    u_tot_a = u.project(chain.enter(u_kept))
    chain.leave(u_tot_a)
    product, kept = send_first(d, 1, [d_blocks[o] for o in far_order])
    d_arr_b = swapped(product, "col", 0)
    d_tot_b = keep_first(d, kept, product)
    chain.leave(d_tot_b)
    settle(d)
    second(u, u_tot_a, u_arr_a)

    take_far(u_blocks)
    second(d, d_tot_b, d_arr_b)
    for o in list(sq):
        sq[o | 1] = swapped(tie(sq[o], chain.token), "row", 0)
    u_prod_b, kept = send_first(u, 1, [u_blocks[o] for o in far_order])
    u_arr_b = swapped(u_prod_b, "col", 0)
    u_tot_b = keep_first(u, kept, u_prod_b)
    chain.leave(u_tot_b)
    settle(u)

    sums = jnp.stack([sq[o] for o in order])
    sums = pick(sums.reshape(n_row, 2, n_col, sub), z, 2)
    inverse = lax.rsqrt(sums / features + EPSILON).transpose(1, 0, 2).reshape(2, rows, 1)

    def make_pairs(c, scale):
        inputs = chain.enter(*c.kernel_rows())
        pair = whole(
            functools.partial(kv_kernel, qw, kvw),
            jax.ShapeDtypeStruct((rows, 2 * kvw), BF16),
            moved=2 * rows * (qw + 2 * kvw) * 6,
        )(*inputs, scale, cosine, sine)
        chain.leave(pair)
        return inputs, [pair] + [crossed(pair, "col", o) for o in range(1, n_col)]

    def attend(c, inputs, scale, pairs):
        pairs = chain.enter(*pairs)
        keys = rows * n_col
        out = whole(
            functools.partial(attention_kernel, qw, kvw, n_col),
            jax.ShapeDtypeStruct((rows, qw), BF16),
            scratch=[pltpu.VMEM((keys, kvw), BF16), pltpu.VMEM((keys, kvw), BF16), pltpu.VMEM((rows, keys), F32)],
            flops=4 * rows * keys * qw,
            exps=rows * keys * qw // HD,
            moved=rows * qw * 8,
        )(*inputs, scale, cosine, sine, q_pos, k_pos, *pairs)
        chain.leave(out)
        return out

    d_inputs, d_pairs = make_pairs(d, inverse[0])
    d_pairs = list(chain.enter(*d_pairs))
    chain.leave(d_pairs[-1])
    second(u, u_tot_b, u_arr_b)
    d_att = attend(d, d_inputs, inverse[0], d_pairs)
    d_got = gather(d_att, "col")
    d_got[1] = swapped(d_att, "col", 0)
    u_inputs, u_pairs = make_pairs(u, inverse[1])
    u_att = attend(u, u_inputs, inverse[1], u_pairs)
    u_got = gather(u_att, "col")
    u_got[1] = swapped(u_att, "col", 0)

    def out_first(c, pieces):
        pieces = chain.enter(*pieces)
        pieces = pieces if isinstance(pieces, (list, tuple)) else [pieces]
        shaped = jnp.stack([p.reshape(n_row // 2, 2, sub, qw) for p in pieces], axis=2)

        def dot(value):
            out = jnp.dot(value.reshape(-1, qw), c.wo, preferred_element_type=F32)
            return out.reshape(n_row // 2, -1, c.wo.shape[1])

        product = dot(shaped[:, 1]).astype(BF16)
        arrived = swapped(product, "row", 0)
        kept = dot(tie(shaped[:, 0], product))
        chain.leave(kept)
        return kept, arrived

    def out_second(kept, arrived):
        kept, arrived = chain.enter(kept, arrived)
        for bit in range(1, bits_of("row")):
            total = (kept + arrived.astype(F32)).reshape(-1, 2, *kept.shape[1:])
            product = total[:, 1].astype(BF16)
            kept, arrived = total[:, 0], swapped(product, "row", bit)
        chain.leave(product)
        return kept, arrived

    def out_third(c, kept, arrived, which, steps):
        kept, arrived = chain.enter(kept, arrived)
        residual = c.x.reshape(n_col, sub, -1)
        own = jnp.stack([pick(residual, z ^ o, 0) for o in which]).astype(F32)
        total = kept[0] + arrived[0].astype(F32)
        fresh = (own + total.reshape(own.shape)).astype(BF16)
        chain.leave(fresh)
        return from_behind(fresh, "section", steps)

    def finish(c, *sent):
        by_name = {o: piece[i] for names, piece in zip(groups, sent) for i, o in enumerate(names)}
        both = jnp.stack([by_name[o] for o in range(n_col)])
        both = both.reshape((2,) * bits_of("col") + (sub, -1))
        for bit in range(bits_of("col")):
            dim = bits_of("col") - 1 - bit
            both = jnp.where(my_bit("col", bit) == 0, both, jnp.flip(both, dim))
        return both.reshape(c.x.shape)[None]

    def far_pieces(got):
        names = [o for o in got if o >= 2]
        values = chain.enter(*[got[o] for o in names])
        values = list(values) if len(names) > 1 else [values]
        chain.leave(values[-1])
        for o, value in zip(names, values):
            got[o] = value
            got[o | 1] = swapped(value, "col", 0)

    groups = [[0, 1], [o for o in range(2, n_col) if o % 2 == 0], [o for o in range(2, n_col) if o % 2]]

    def first(c, got, i):
        return out_first(c, [got[o] for o in groups[i]])

    d_p = first(d, d_got, 0)
    far_pieces(d_got)
    d_p = out_second(*d_p)
    d_m = first(d, d_got, 1)
    d_m = out_second(*d_m)
    u_p = first(u, u_got, 0)
    far_pieces(u_got)
    d_p = out_third(d, *d_p, groups[0], 1)
    u_p = out_second(*u_p)
    d_m = out_third(d, *d_m, groups[1], 1)
    d_q = first(d, d_got, 2)
    u_m = first(u, u_got, 1)
    d_q = out_second(*d_q)
    u_m = out_second(*u_m)
    u_p = out_third(u, *u_p, groups[0], -1)
    d_q = out_third(d, *d_q, groups[2], 1)
    u_m = out_third(u, *u_m, groups[1], -1)
    u_q = first(u, u_got, 2)
    u_q = out_second(*u_q)
    u_q = out_third(u, *u_q, groups[2], -1)
    return finish(d, d_p, d_m, d_q), finish(u, u_p, u_m, u_q)


def solution(mesh):
    tokens = P("section", "row", "col")
    into, out_of = P("section", "col", "row"), P("section", "row", "col")
    one = (tokens, P("section", "col"), into, into, into, out_of)
    return jax.shard_map(
        on_device, mesh=mesh, in_specs=one + one, out_specs=(tokens, tokens), check_vma=False
    )
```

```python
import functools

import jax
import jax.numpy as jnp
from jax import lax
from jax.experimental import pallas as pl
from jax.experimental.pallas import tpu as pltpu
from jax.sharding import PartitionSpec as P

HD = 128
EPSILON = 1e-05
HIDDEN = -1e30
LOG2E = 1.4426950408889634
BF16 = jnp.bfloat16
F32 = jnp.float32


def swapped(value, axis, bit):
    return lax.ppermute(value, axis, [(i, i ^ (1 << bit)) for i in range(lax.axis_size(axis))])


def crossed(value, axis, bits):
    return lax.ppermute(value, axis, [(i, i ^ bits) for i in range(lax.axis_size(axis))])


def from_behind(value, axis, steps):
    count = lax.axis_size(axis)
    return lax.ppermute(value, axis, [(i, (i + steps) % count) for i in range(count)])


def bits_of(axis):
    return lax.axis_size(axis).bit_length() - 1


def my_bit(axis, bit):
    return (lax.axis_index(axis) >> bit) & 1


def pick(value, index, dim):
    return lax.dynamic_index_in_dim(value, index, dim, keepdims=False)


def tie(value, *deps):
    return lax.optimization_barrier((value, deps))[0]


class Chain:
    def __init__(self):
        self.token = None

    def enter(self, *values):
        out = values if self.token is None else tie(values, self.token)
        return out[0] if len(values) == 1 else out

    def leave(self, array):
        self.token = array


def turn(value, cosine, sine):
    return value * cosine + pltpu.roll(value, HD // 2, 1) * sine


def rows_of(keeps, arrivals, inverse, columns):
    parts = [k[:, columns] + a[:, columns].astype(F32) for k, a in zip(keeps, arrivals)]
    return jnp.concatenate(parts, axis=0) * inverse[...]


def kv_kernel(qw, kvw, keep_a, keep_b, arr_a, arr_b, inverse, cosine, sine, out):
    for start in range(0, 2 * kvw, HD):
        columns = slice(qw + start, qw + start + HD)
        value = rows_of((keep_a, keep_b), (arr_a, arr_b), inverse, columns)
        if start < kvw:
            value = turn(value, cosine[...], sine[...])
        out[:, start : start + HD] = value.astype(BF16)


def attention_kernel(
    qw, kvw, count, keep_a, keep_b, arr_a, arr_b, inverse, cosine, sine, q_pos, k_pos, *rest
):
    pairs, (out, keys, values, bias) = rest[:count], rest[count:]
    rows = pairs[0].shape[0]
    for i, pair in enumerate(pairs):
        keys[i * rows : (i + 1) * rows] = pair[:, :kvw]
        values[i * rows : (i + 1) * rows] = pair[:, kvw:]
    bias[...] = jnp.where(q_pos[...] >= k_pos[...], 0.0, HIDDEN)
    group = (qw // HD) // (kvw // HD)
    for head in range(qw // HD):
        columns = slice(head * HD, (head + 1) * HD)
        kv_columns = slice(head // group * HD, (head // group + 1) * HD)
        query = rows_of((keep_a, keep_b), (arr_a, arr_b), inverse, columns)
        query = turn(query, cosine[...], sine[...]).astype(BF16)
        scores = lax.dot_general(
            query, keys[:, kv_columns], (((1,), (1,)), ((), ())), preferred_element_type=F32
        )
        scores = scores + bias[...]
        top = jnp.max(scores, axis=1, keepdims=True)
        probs = jnp.exp2((scores - top) * (LOG2E / HD**0.5))
        total = jnp.sum(probs, axis=1, keepdims=True)
        mixed = jnp.dot(probs.astype(BF16), values[:, kv_columns], preferred_element_type=F32)
        out[:, columns] = (mixed / total).astype(BF16)


def gather(block, axis):
    blocks = {0: block}
    for bit in range(1, bits_of(axis)):
        for o in list(blocks):
            blocks[o | 1 << bit] = swapped(blocks[o], axis, bit)
    return blocks


class Cascade:
    def __init__(self, x, gain, wq, wk, wv, wo):
        self.x, self.gain, self.wo = x, gain, wo
        if wk.shape[1] < HD:
            other_k, other_v = swapped((wk, wv), "row", 0)
            even = lax.axis_index("row") % 2 == 0
            wk = jnp.where(even, jnp.concatenate([wk, other_k], 1), jnp.concatenate([other_k, wk], 1))
            wv = jnp.where(even, jnp.concatenate([wv, other_v], 1), jnp.concatenate([other_v, wv], 1))
        self.qw, self.kvw = wq.shape[1], wk.shape[1]
        self.w = jnp.concatenate([wq, wk, wv], axis=1)
        self.n_row, self.n_col = lax.axis_size("row"), lax.axis_size("col")
        self.sub = x.shape[0] // self.n_col
        self.keep, self.arrived = [], []

    def halves(self, block_list):
        low = my_bit("col", 0)
        blocks = jnp.stack(block_list).reshape(len(block_list), self.n_col // 2, 2, self.sub, -1)
        return pick(blocks, 1 - low, 2), pick(blocks, low, 2)

    def project(self, half):
        scaled = (half.astype(F32) * self.gain).astype(BF16)
        rows = scaled.reshape(-1, scaled.shape[-1])
        out = jnp.dot(rows, self.w, preferred_element_type=F32)
        return out.reshape(half.shape[:-1] + (-1,))

    def halve(self, total, arrived, bit):
        mine = my_bit("col", bit)
        shape = (total.shape[0], -1, 2) + total.shape[2:]
        total, arrived = total.reshape(shape), arrived.reshape(shape)

        def part(which):
            return pick(total, which, 2) + pick(arrived, which, 2).astype(F32)

        return part(mine), part(1 - mine).astype(BF16)

    def flat(self, value):
        return value.reshape(-1, value.shape[-1])

    def kernel_rows(self):
        return [self.flat(v) for v in self.keep] + [self.flat(v) for v in self.arrived]


def whole(body, out_shape, scratch=(), flops=0, exps=0, moved=0):
    return pl.pallas_call(
        body,
        out_shape=out_shape,
        scratch_shapes=list(scratch),
        compiler_params=pltpu.CompilerParams(vmem_limit_bytes=40 * 1024 * 1024),
        cost_estimate=pl.CostEstimate(flops=flops, transcendentals=exps, bytes_accessed=moved),
    )


def on_device(*arrays):
    arrays = [a[0] for a in arrays]
    half = len(arrays) // 2
    d, u = Cascade(*arrays[:half]), Cascade(*arrays[half:])
    n_row, n_col, sub = d.n_row, d.n_col, d.sub
    block = n_col * sub
    features = d.x.shape[1] * n_col
    rows = n_row * sub
    qw, kvw = d.qw, d.kvw
    z, r = lax.axis_index("col"), lax.axis_index("row")
    chain = Chain()

    order = [o for o in range(n_row) if o < 2] + [o for o in range(n_row) if o >= 2]
    starts = (r ^ jnp.array(order, jnp.int32)) * block
    offsets = jnp.arange(sub, dtype=jnp.int32)
    q_pos = (starts[:, None] + z * sub + offsets).astype(F32).reshape(rows, 1)
    owners = (z ^ jnp.arange(n_col, dtype=jnp.int32)) * sub
    k_pos = (owners[:, None, None] + starts[:, None] + offsets).astype(F32).reshape(1, -1)
    width = HD // 2
    inverse_freq = 10000.0 ** (-jnp.arange(width, dtype=F32) / width)
    angles = q_pos * inverse_freq
    cosine = jnp.concatenate([jnp.cos(angles)] * 2, axis=1)
    sine = jnp.sin(angles)
    sine = jnp.concatenate([-sine, sine], axis=1)

    d_blocks = gather(d.x, "row")
    d_blocks[1] = swapped(d.x, "row", 0)

    def send_first(c, group, blocks_):
        send, kept = c.halves(chain.enter(*blocks_))
        product = c.project(send).astype(BF16)
        return product, kept

    def keep_first(c, kept, token):
        return c.project(tie(kept, token))

    def second(c, total, arrived):
        total, arrived = chain.enter(total, arrived)
        kept, product = c.halve(total, arrived, 1)
        arrived = swapped(product, "col", 1)
        chain.leave(product)
        for bit in range(2, bits_of("col")):
            kept, product = c.halve(kept, arrived, bit)
            arrived = swapped(product, "col", bit)
        c.keep.append(kept)
        c.arrived.append(arrived)

    def settle(c):
        c.arrived[-1] = chain.enter(c.arrived[-1])
        chain.leave(c.arrived[-1])

    def take_far(blocks_):
        values = chain.enter(*[blocks_[o] for o in far])
        values = list(values) if len(far) > 1 else [values]
        for o, value in zip(far, values):
            blocks_[o] = value
            blocks_[o | 1] = swapped(value, "row", 0)
        chain.leave(values[-1])
        return values

    far = [o for o in d_blocks if o >= 2]
    far_order = [o for o in order if o >= 2]

    product, kept = send_first(d, 0, [d_blocks[0], d_blocks[1]])
    d_arr_a = swapped(product, "col", 0)
    d_tot_a = keep_first(d, kept, product)
    u_near = swapped(tie(u.x, product), "row", 0)
    chain.leave(d_tot_a)
    squares = jnp.stack([jnp.sum(jnp.square(chain.enter(c.x).astype(F32)), axis=1) for c in (d, u)])
    other = swapped(squares, "col", 0)
    chain.leave(squares)
    u_prod_a, kept = send_first(u, 0, [u.x, u_near])
    u_kept = kept
    chain.leave(u_prod_a)
    second(d, d_tot_a, d_arr_a)
    u_arr_a = swapped(tie(u_prod_a, chain.token), "col", 0)

    d_far = take_far(d_blocks)
    u_blocks = gather(tie(u.x, *d_far), "row")
    squares, other = chain.enter(squares, other)
    squares = squares + other
    other = swapped(squares, "col", 1)
    chain.leave(squares)
    u_tot_a = u.project(chain.enter(u_kept))
    chain.leave(u_tot_a)
    product, kept = send_first(d, 1, [d_blocks[o] for o in far_order])
    d_arr_b = swapped(product, "col", 0)
    d_tot_b = keep_first(d, kept, product)
    chain.leave(d_tot_b)
    settle(d)
    squares, other = chain.enter(squares, other)
    squares = squares + other
    for bit in range(2, bits_of("col")):
        squares = squares + swapped(squares, "col", bit)
    chain.leave(squares)
    sq = gather(squares, "row")
    second(u, u_tot_a, u_arr_a)

    take_far(u_blocks)
    second(d, d_tot_b, d_arr_b)
    for o in list(sq):
        sq[o | 1] = swapped(tie(sq[o], chain.token), "row", 0)
    u_prod_b, kept = send_first(u, 1, [u_blocks[o] for o in far_order])
    u_arr_b = swapped(u_prod_b, "col", 0)
    u_tot_b = keep_first(u, kept, u_prod_b)
    chain.leave(u_tot_b)
    settle(u)

    sums = jnp.stack([sq[o] for o in order])
    sums = pick(sums.reshape(n_row, 2, n_col, sub), z, 2)
    inverse = lax.rsqrt(sums / features + EPSILON).transpose(1, 0, 2).reshape(2, rows, 1)

    def make_pairs(c, scale):
        inputs = chain.enter(*c.kernel_rows())
        pair = whole(
            functools.partial(kv_kernel, qw, kvw),
            jax.ShapeDtypeStruct((rows, 2 * kvw), BF16),
            moved=2 * rows * (qw + 2 * kvw) * 6,
        )(*inputs, scale, cosine, sine)
        chain.leave(pair)
        return inputs, [pair] + [crossed(pair, "col", o) for o in range(1, n_col)]

    def attend(c, inputs, scale, pairs):
        pairs = chain.enter(*pairs)
        keys = rows * n_col
        out = whole(
            functools.partial(attention_kernel, qw, kvw, n_col),
            jax.ShapeDtypeStruct((rows, qw), BF16),
            scratch=[pltpu.VMEM((keys, kvw), BF16), pltpu.VMEM((keys, kvw), BF16), pltpu.VMEM((rows, keys), F32)],
            flops=4 * rows * keys * qw,
            exps=rows * keys * qw // HD,
            moved=rows * qw * 8,
        )(*inputs, scale, cosine, sine, q_pos, k_pos, *pairs)
        chain.leave(out)
        return out

    d_inputs, d_pairs = make_pairs(d, inverse[0])
    second(u, u_tot_b, u_arr_b)
    d_pairs = list(chain.enter(*d_pairs))
    chain.leave(d_pairs[-1])
    u_inputs, u_pairs = make_pairs(u, inverse[1])
    d_att = attend(d, d_inputs, inverse[0], d_pairs)
    d_got = gather(d_att, "col")
    d_got[1] = swapped(d_att, "col", 0)
    u_att = attend(u, u_inputs, inverse[1], u_pairs)
    u_got = gather(u_att, "col")
    u_got[1] = swapped(u_att, "col", 0)

    def out_first(c, pieces):
        pieces = chain.enter(*pieces)
        pieces = pieces if isinstance(pieces, (list, tuple)) else [pieces]
        shaped = jnp.stack([p.reshape(n_row // 2, 2, sub, qw) for p in pieces], axis=2)

        def dot(value):
            out = jnp.dot(value.reshape(-1, qw), c.wo, preferred_element_type=F32)
            return out.reshape(n_row // 2, -1, c.wo.shape[1])

        product = dot(shaped[:, 1]).astype(BF16)
        arrived = swapped(product, "row", 0)
        kept = dot(tie(shaped[:, 0], product))
        chain.leave(kept)
        return kept, arrived

    def out_second(kept, arrived):
        kept, arrived = chain.enter(kept, arrived)
        for bit in range(1, bits_of("row")):
            total = (kept + arrived.astype(F32)).reshape(-1, 2, *kept.shape[1:])
            product = total[:, 1].astype(BF16)
            kept, arrived = total[:, 0], swapped(product, "row", bit)
        chain.leave(product)
        return kept, arrived

    def out_third(c, kept, arrived, which, steps):
        kept, arrived = chain.enter(kept, arrived)
        residual = c.x.reshape(n_col, sub, -1)
        own = jnp.stack([pick(residual, z ^ o, 0) for o in which]).astype(F32)
        total = kept[0] + arrived[0].astype(F32)
        fresh = (own + total.reshape(own.shape)).astype(BF16)
        chain.leave(fresh)
        return from_behind(fresh, "section", steps)

    def finish(c, *sent):
        by_name = {o: piece[i] for names, piece in zip(groups, sent) for i, o in enumerate(names)}
        both = jnp.stack([by_name[o] for o in range(n_col)])
        both = both.reshape((2,) * bits_of("col") + (sub, -1))
        for bit in range(bits_of("col")):
            dim = bits_of("col") - 1 - bit
            both = jnp.where(my_bit("col", bit) == 0, both, jnp.flip(both, dim))
        return both.reshape(c.x.shape)[None]

    def far_pieces(got):
        names = [o for o in got if o >= 2]
        values = chain.enter(*[got[o] for o in names])
        values = list(values) if len(names) > 1 else [values]
        chain.leave(values[-1])
        for o, value in zip(names, values):
            got[o] = value
            got[o | 1] = swapped(value, "col", 0)

    groups = [[0, 1], [o for o in range(2, n_col) if o % 2 == 0], [o for o in range(2, n_col) if o % 2]]

    def first(c, got, i):
        return out_first(c, [got[o] for o in groups[i]])

    far_pieces(d_got)
    d_p = first(d, d_got, 0)
    d_p = out_second(*d_p)
    d_m = first(d, d_got, 1)
    d_m = out_second(*d_m)
    u_p = first(u, u_got, 0)
    far_pieces(u_got)
    d_p = out_third(d, *d_p, groups[0], 1)
    u_p = out_second(*u_p)
    d_m = out_third(d, *d_m, groups[1], 1)
    d_q = first(d, d_got, 2)
    u_m = first(u, u_got, 1)
    d_q = out_second(*d_q)
    u_m = out_second(*u_m)
    u_p = out_third(u, *u_p, groups[0], -1)
    d_q = out_third(d, *d_q, groups[2], 1)
    u_m = out_third(u, *u_m, groups[1], -1)
    u_q = first(u, u_got, 2)
    u_q = out_second(*u_q)
    u_q = out_third(u, *u_q, groups[2], -1)
    return finish(d, d_p, d_m, d_q), finish(u, u_p, u_m, u_q)


def solution(mesh):
    tokens = P("section", "row", "col")
    into, out_of = P("section", "col", "row"), P("section", "row", "col")
    one = (tokens, P("section", "col"), into, into, into, out_of)
    return jax.shard_map(
        on_device, mesh=mesh, in_specs=one + one, out_specs=(tokens, tokens), check_vma=False
    )
```

```python
import functools

import jax
import jax.numpy as jnp
from jax import lax
from jax.experimental import pallas as pl
from jax.experimental.pallas import tpu as pltpu
from jax.sharding import PartitionSpec as P

HD = 128
EPSILON = 1e-05
HIDDEN = -1e30
LOG2E = 1.4426950408889634
BF16 = jnp.bfloat16
F32 = jnp.float32


def swapped(value, axis, bit):
    return lax.ppermute(value, axis, [(i, i ^ (1 << bit)) for i in range(lax.axis_size(axis))])


def crossed(value, axis, bits):
    return lax.ppermute(value, axis, [(i, i ^ bits) for i in range(lax.axis_size(axis))])


def from_behind(value, axis, steps):
    count = lax.axis_size(axis)
    return lax.ppermute(value, axis, [(i, (i + steps) % count) for i in range(count)])


def bits_of(axis):
    return lax.axis_size(axis).bit_length() - 1


def my_bit(axis, bit):
    return (lax.axis_index(axis) >> bit) & 1


def pick(value, index, dim):
    return lax.dynamic_index_in_dim(value, index, dim, keepdims=False)


def tie(value, *deps):
    return lax.optimization_barrier((value, deps))[0]


class Chain:
    def __init__(self):
        self.token = None

    def enter(self, *values):
        out = values if self.token is None else tie(values, self.token)
        return out[0] if len(values) == 1 else out

    def leave(self, array):
        self.token = array


def turn(value, cosine, sine):
    return value * cosine + pltpu.roll(value, HD // 2, 1) * sine


def rows_of(keeps, arrivals, inverse, columns):
    parts = [k[:, columns] + a[:, columns].astype(F32) for k, a in zip(keeps, arrivals)]
    return jnp.concatenate(parts, axis=0) * inverse[...]


def kv_kernel(qw, kvw, keep_a, keep_b, arr_a, arr_b, inverse, cosine, sine, out):
    for start in range(0, 2 * kvw, HD):
        columns = slice(qw + start, qw + start + HD)
        value = rows_of((keep_a, keep_b), (arr_a, arr_b), inverse, columns)
        if start < kvw:
            value = turn(value, cosine[...], sine[...])
        out[:, start : start + HD] = value.astype(BF16)


def attention_kernel(
    qw, kvw, count, keep_a, keep_b, arr_a, arr_b, inverse, cosine, sine, q_pos, k_pos, *rest
):
    pairs, (out, keys, values, bias) = rest[:count], rest[count:]
    rows = pairs[0].shape[0]
    for i, pair in enumerate(pairs):
        keys[i * rows : (i + 1) * rows] = pair[:, :kvw]
        values[i * rows : (i + 1) * rows] = pair[:, kvw:]
    bias[...] = jnp.where(q_pos[...] >= k_pos[...], 0.0, HIDDEN)
    group = (qw // HD) // (kvw // HD)
    for head in range(qw // HD):
        columns = slice(head * HD, (head + 1) * HD)
        kv_columns = slice(head // group * HD, (head // group + 1) * HD)
        query = rows_of((keep_a, keep_b), (arr_a, arr_b), inverse, columns)
        query = turn(query, cosine[...], sine[...]).astype(BF16)
        scores = lax.dot_general(
            query, keys[:, kv_columns], (((1,), (1,)), ((), ())), preferred_element_type=F32
        )
        scores = scores + bias[...]
        top = jnp.max(scores, axis=1, keepdims=True)
        probs = jnp.exp2((scores - top) * (LOG2E / HD**0.5))
        total = jnp.sum(probs, axis=1, keepdims=True)
        mixed = jnp.dot(probs.astype(BF16), values[:, kv_columns], preferred_element_type=F32)
        out[:, columns] = (mixed / total).astype(BF16)


def gather(block, axis):
    blocks = {0: block}
    for bit in range(1, bits_of(axis)):
        for o in list(blocks):
            blocks[o | 1 << bit] = swapped(blocks[o], axis, bit)
    return blocks


class Cascade:
    def __init__(self, x, gain, wq, wk, wv, wo):
        self.x, self.gain, self.wo = x, gain, wo
        if wk.shape[1] < HD:
            other_k, other_v = swapped((wk, wv), "row", 0)
            even = lax.axis_index("row") % 2 == 0
            wk = jnp.where(even, jnp.concatenate([wk, other_k], 1), jnp.concatenate([other_k, wk], 1))
            wv = jnp.where(even, jnp.concatenate([wv, other_v], 1), jnp.concatenate([other_v, wv], 1))
        self.qw, self.kvw = wq.shape[1], wk.shape[1]
        self.w = jnp.concatenate([wq, wk, wv], axis=1)
        self.n_row, self.n_col = lax.axis_size("row"), lax.axis_size("col")
        self.sub = x.shape[0] // self.n_col
        self.keep, self.arrived = [], []

    def halves(self, block_list):
        low = my_bit("col", 0)
        blocks = jnp.stack(block_list).reshape(len(block_list), self.n_col // 2, 2, self.sub, -1)
        return pick(blocks, 1 - low, 2), pick(blocks, low, 2)

    def project(self, half):
        scaled = (half.astype(F32) * self.gain).astype(BF16)
        rows = scaled.reshape(-1, scaled.shape[-1])
        out = jnp.dot(rows, self.w, preferred_element_type=F32)
        return out.reshape(half.shape[:-1] + (-1,))

    def halve(self, total, arrived, bit):
        mine = my_bit("col", bit)
        shape = (total.shape[0], -1, 2) + total.shape[2:]
        total, arrived = total.reshape(shape), arrived.reshape(shape)

        def part(which):
            return pick(total, which, 2) + pick(arrived, which, 2).astype(F32)

        return part(mine), part(1 - mine).astype(BF16)

    def flat(self, value):
        return value.reshape(-1, value.shape[-1])

    def kernel_rows(self):
        return [self.flat(v) for v in self.keep] + [self.flat(v) for v in self.arrived]


def whole(body, out_shape, scratch=(), flops=0, exps=0, moved=0):
    return pl.pallas_call(
        body,
        out_shape=out_shape,
        scratch_shapes=list(scratch),
        compiler_params=pltpu.CompilerParams(vmem_limit_bytes=40 * 1024 * 1024),
        cost_estimate=pl.CostEstimate(flops=flops, transcendentals=exps, bytes_accessed=moved),
    )


def on_device(*arrays):
    arrays = [a[0] for a in arrays]
    half = len(arrays) // 2
    d, u = Cascade(*arrays[:half]), Cascade(*arrays[half:])
    n_row, n_col, sub = d.n_row, d.n_col, d.sub
    block = n_col * sub
    features = d.x.shape[1] * n_col
    rows = n_row * sub
    qw, kvw = d.qw, d.kvw
    z, r = lax.axis_index("col"), lax.axis_index("row")
    chain = Chain()

    order = [o for o in range(n_row) if o < 2] + [o for o in range(n_row) if o >= 2]
    starts = (r ^ jnp.array(order, jnp.int32)) * block
    offsets = jnp.arange(sub, dtype=jnp.int32)
    q_pos = (starts[:, None] + z * sub + offsets).astype(F32).reshape(rows, 1)
    owners = (z ^ jnp.arange(n_col, dtype=jnp.int32)) * sub
    k_pos = (owners[:, None, None] + starts[:, None] + offsets).astype(F32).reshape(1, -1)
    width = HD // 2
    inverse_freq = 10000.0 ** (-jnp.arange(width, dtype=F32) / width)
    angles = q_pos * inverse_freq
    cosine = jnp.concatenate([jnp.cos(angles)] * 2, axis=1)
    sine = jnp.sin(angles)
    sine = jnp.concatenate([-sine, sine], axis=1)

    d_blocks = gather(d.x, "row")
    d_blocks[1] = swapped(d.x, "row", 0)

    def send_first(c, group, blocks_):
        send, kept = c.halves(chain.enter(*blocks_))
        product = c.project(send).astype(BF16)
        return product, kept

    def keep_first(c, kept, token):
        return c.project(tie(kept, token))

    def second(c, total, arrived):
        total, arrived = chain.enter(total, arrived)
        kept, product = c.halve(total, arrived, 1)
        arrived = swapped(product, "col", 1)
        chain.leave(product)
        for bit in range(2, bits_of("col")):
            kept, product = c.halve(kept, arrived, bit)
            arrived = swapped(product, "col", bit)
        c.keep.append(kept)
        c.arrived.append(arrived)

    def settle(c):
        c.arrived[-1] = chain.enter(c.arrived[-1])
        chain.leave(c.arrived[-1])

    def take_far(blocks_):
        values = chain.enter(*[blocks_[o] for o in far])
        values = list(values) if len(far) > 1 else [values]
        for o, value in zip(far, values):
            blocks_[o] = value
            blocks_[o | 1] = swapped(value, "row", 0)
        chain.leave(values[-1])
        return values

    far = [o for o in d_blocks if o >= 2]
    far_order = [o for o in order if o >= 2]

    product, kept = send_first(d, 0, [d_blocks[0], d_blocks[1]])
    d_arr_a = swapped(product, "col", 0)
    d_tot_a = keep_first(d, kept, product)
    u_near = swapped(tie(u.x, product), "row", 0)
    chain.leave(d_tot_a)
    squares = jnp.stack([jnp.sum(jnp.square(chain.enter(c.x).astype(F32)), axis=1) for c in (d, u)])
    other = swapped(squares, "col", 0)
    chain.leave(squares)
    u_prod_a, kept = send_first(u, 0, [u.x, u_near])
    u_kept = kept
    chain.leave(u_prod_a)
    second(d, d_tot_a, d_arr_a)
    u_arr_a = swapped(tie(u_prod_a, chain.token), "col", 0)

    d_far = take_far(d_blocks)
    u_blocks = gather(tie(u.x, *d_far), "row")
    squares, other = chain.enter(squares, other)
    squares = squares + other
    other = swapped(squares, "col", 1)
    chain.leave(squares)
    u_tot_a = u.project(chain.enter(u_kept))
    chain.leave(u_tot_a)
    product, kept = send_first(d, 1, [d_blocks[o] for o in far_order])
    d_arr_b = swapped(product, "col", 0)
    d_tot_b = keep_first(d, kept, product)
    chain.leave(d_tot_b)
    settle(d)
    squares, other = chain.enter(squares, other)
    squares = squares + other
    for bit in range(2, bits_of("col")):
        squares = squares + swapped(squares, "col", bit)
    chain.leave(squares)
    sq = gather(squares, "row")
    second(u, u_tot_a, u_arr_a)

    take_far(u_blocks)
    second(d, d_tot_b, d_arr_b)
    for o in list(sq):
        sq[o | 1] = swapped(tie(sq[o], chain.token), "row", 0)
    u_prod_b, kept = send_first(u, 1, [u_blocks[o] for o in far_order])
    u_arr_b = swapped(u_prod_b, "col", 0)
    u_tot_b = keep_first(u, kept, u_prod_b)
    chain.leave(u_tot_b)
    settle(u)

    sums = jnp.stack([sq[o] for o in order])
    sums = pick(sums.reshape(n_row, 2, n_col, sub), z, 2)
    inverse = lax.rsqrt(sums / features + EPSILON).transpose(1, 0, 2).reshape(2, rows, 1)

    def make_pairs(c, scale):
        inputs = chain.enter(*c.kernel_rows())
        pair = whole(
            functools.partial(kv_kernel, qw, kvw),
            jax.ShapeDtypeStruct((rows, 2 * kvw), BF16),
            moved=2 * rows * (qw + 2 * kvw) * 6,
        )(*inputs, scale, cosine, sine)
        chain.leave(pair)
        return inputs, [pair] + [crossed(pair, "col", o) for o in range(1, n_col)]

    def attend(c, inputs, scale, pairs):
        pairs = chain.enter(*pairs)
        keys = rows * n_col
        out = whole(
            functools.partial(attention_kernel, qw, kvw, n_col),
            jax.ShapeDtypeStruct((rows, qw), BF16),
            scratch=[pltpu.VMEM((keys, kvw), BF16), pltpu.VMEM((keys, kvw), BF16), pltpu.VMEM((rows, keys), F32)],
            flops=4 * rows * keys * qw,
            exps=rows * keys * qw // HD,
            moved=rows * qw * 8,
        )(*inputs, scale, cosine, sine, q_pos, k_pos, *pairs)
        chain.leave(out)
        return out

    d_inputs, d_pairs = make_pairs(d, inverse[0])
    second(u, u_tot_b, u_arr_b)
    d_att = attend(d, d_inputs, inverse[0], d_pairs)
    d_got = gather(d_att, "col")
    d_got[1] = swapped(d_att, "col", 0)

    def out_first(c, pieces):
        pieces = chain.enter(*pieces)
        pieces = pieces if isinstance(pieces, (list, tuple)) else [pieces]
        shaped = jnp.stack([p.reshape(n_row // 2, 2, sub, qw) for p in pieces], axis=2)

        def dot(value):
            out = jnp.dot(value.reshape(-1, qw), c.wo, preferred_element_type=F32)
            return out.reshape(n_row // 2, -1, c.wo.shape[1])

        product = dot(shaped[:, 1]).astype(BF16)
        arrived = swapped(product, "row", 0)
        kept = dot(tie(shaped[:, 0], product))
        chain.leave(kept)
        return kept, arrived

    def out_second(kept, arrived):
        kept, arrived = chain.enter(kept, arrived)
        for bit in range(1, bits_of("row")):
            total = (kept + arrived.astype(F32)).reshape(-1, 2, *kept.shape[1:])
            product = total[:, 1].astype(BF16)
            kept, arrived = total[:, 0], swapped(product, "row", bit)
        chain.leave(product)
        return kept, arrived

    def out_third(c, kept, arrived, which, steps):
        kept, arrived = chain.enter(kept, arrived)
        residual = c.x.reshape(n_col, sub, -1)
        own = jnp.stack([pick(residual, z ^ o, 0) for o in which]).astype(F32)
        total = kept[0] + arrived[0].astype(F32)
        fresh = (own + total.reshape(own.shape)).astype(BF16)
        chain.leave(fresh)
        return from_behind(fresh, "section", steps)

    def finish(c, *sent):
        by_name = {o: piece[i] for names, piece in zip(groups, sent) for i, o in enumerate(names)}
        both = jnp.stack([by_name[o] for o in range(n_col)])
        both = both.reshape((2,) * bits_of("col") + (sub, -1))
        for bit in range(bits_of("col")):
            dim = bits_of("col") - 1 - bit
            both = jnp.where(my_bit("col", bit) == 0, both, jnp.flip(both, dim))
        return both.reshape(c.x.shape)[None]

    def far_pieces(got):
        names = [o for o in got if o >= 2]
        values = chain.enter(*[got[o] for o in names])
        values = list(values) if len(names) > 1 else [values]
        chain.leave(values[-1])
        for o, value in zip(names, values):
            got[o] = value
            got[o | 1] = swapped(value, "col", 0)

    groups = [[0, 1], [o for o in range(2, n_col) if o % 2 == 0], [o for o in range(2, n_col) if o % 2]]

    def first(c, got, i):
        return out_first(c, [got[o] for o in groups[i]])

    u_inputs, u_pairs = make_pairs(u, inverse[1])
    d_p = first(d, d_got, 0)
    far_pieces(d_got)
    d_p = out_second(*d_p)
    u_att = attend(u, u_inputs, inverse[1], u_pairs)
    u_got = gather(u_att, "col")
    u_got[1] = swapped(u_att, "col", 0)
    d_p = out_third(d, *d_p, groups[0], 1)
    d_m = first(d, d_got, 1)
    d_m = out_second(*d_m)
    d_q = first(d, d_got, 2)
    u_p = first(u, u_got, 0)
    d_q = out_second(*d_q)
    u_p = out_second(*u_p)
    d_m = out_third(d, *d_m, groups[1], 1)
    far_pieces(u_got)
    u_m = first(u, u_got, 1)
    u_m = out_second(*u_m)
    d_q = out_third(d, *d_q, groups[2], 1)
    u_p = out_third(u, *u_p, groups[0], -1)
    u_q = first(u, u_got, 2)
    u_q = out_second(*u_q)
    u_m = out_third(u, *u_m, groups[1], -1)
    u_q = out_third(u, *u_q, groups[2], -1)
    return finish(d, d_p, d_m, d_q), finish(u, u_p, u_m, u_q)


def solution(mesh):
    tokens = P("section", "row", "col")
    into, out_of = P("section", "col", "row"), P("section", "row", "col")
    one = (tokens, P("section", "col"), into, into, into, out_of)
    return jax.shard_map(
        on_device, mesh=mesh, in_specs=one + one, out_specs=(tokens, tokens), check_vma=False
    )
```

```python
import functools

import jax
import jax.numpy as jnp
from jax import lax
from jax.experimental import pallas as pl
from jax.experimental.pallas import tpu as pltpu
from jax.sharding import PartitionSpec as P

HD = 128
EPSILON = 1e-05
HIDDEN = -1e30
LOG2E = 1.4426950408889634
BF16 = jnp.bfloat16
F32 = jnp.float32


def swapped(value, axis, bit):
    return lax.ppermute(value, axis, [(i, i ^ (1 << bit)) for i in range(lax.axis_size(axis))])


def crossed(value, axis, bits):
    return lax.ppermute(value, axis, [(i, i ^ bits) for i in range(lax.axis_size(axis))])


def from_behind(value, axis, steps):
    count = lax.axis_size(axis)
    return lax.ppermute(value, axis, [(i, (i + steps) % count) for i in range(count)])


def bits_of(axis):
    return lax.axis_size(axis).bit_length() - 1


def my_bit(axis, bit):
    return (lax.axis_index(axis) >> bit) & 1


def pick(value, index, dim):
    return lax.dynamic_index_in_dim(value, index, dim, keepdims=False)


def tie(value, *deps):
    return lax.optimization_barrier((value, deps))[0]


class Chain:
    def __init__(self):
        self.token = None

    def enter(self, *values):
        out = values if self.token is None else tie(values, self.token)
        return out[0] if len(values) == 1 else out

    def leave(self, array):
        self.token = array


def turn(value, cosine, sine):
    return value * cosine + pltpu.roll(value, HD // 2, 1) * sine


def rows_of(keeps, arrivals, inverse, columns):
    parts = [k[:, columns] + a[:, columns].astype(F32) for k, a in zip(keeps, arrivals)]
    return jnp.concatenate(parts, axis=0) * inverse[...]


def kv_kernel(qw, kvw, keep_a, keep_b, arr_a, arr_b, inverse, cosine, sine, out):
    for start in range(0, 2 * kvw, HD):
        columns = slice(qw + start, qw + start + HD)
        value = rows_of((keep_a, keep_b), (arr_a, arr_b), inverse, columns)
        if start < kvw:
            value = turn(value, cosine[...], sine[...])
        out[:, start : start + HD] = value.astype(BF16)


def attention_kernel(
    qw, kvw, count, keep_a, keep_b, arr_a, arr_b, inverse, cosine, sine, q_pos, k_pos, *rest
):
    pairs, (out, keys, values, bias) = rest[:count], rest[count:]
    rows = pairs[0].shape[0]
    for i, pair in enumerate(pairs):
        keys[i * rows : (i + 1) * rows] = pair[:, :kvw]
        values[i * rows : (i + 1) * rows] = pair[:, kvw:]
    bias[...] = jnp.where(q_pos[...] >= k_pos[...], 0.0, HIDDEN)
    group = (qw // HD) // (kvw // HD)
    for head in range(qw // HD):
        columns = slice(head * HD, (head + 1) * HD)
        kv_columns = slice(head // group * HD, (head // group + 1) * HD)
        query = rows_of((keep_a, keep_b), (arr_a, arr_b), inverse, columns)
        query = turn(query, cosine[...], sine[...]).astype(BF16)
        scores = lax.dot_general(
            query, keys[:, kv_columns], (((1,), (1,)), ((), ())), preferred_element_type=F32
        )
        scores = scores + bias[...]
        top = jnp.max(scores, axis=1, keepdims=True)
        probs = jnp.exp2((scores - top) * (LOG2E / HD**0.5))
        total = jnp.sum(probs, axis=1, keepdims=True)
        mixed = jnp.dot(probs.astype(BF16), values[:, kv_columns], preferred_element_type=F32)
        out[:, columns] = (mixed / total).astype(BF16)


def gather(block, axis):
    blocks = {0: block}
    for bit in range(1, bits_of(axis)):
        for o in list(blocks):
            blocks[o | 1 << bit] = swapped(blocks[o], axis, bit)
    return blocks


class Cascade:
    def __init__(self, x, gain, wq, wk, wv, wo):
        self.x, self.gain, self.wo = x, gain, wo
        if wk.shape[1] < HD:
            other_k, other_v = swapped((wk, wv), "row", 0)
            even = lax.axis_index("row") % 2 == 0
            wk = jnp.where(even, jnp.concatenate([wk, other_k], 1), jnp.concatenate([other_k, wk], 1))
            wv = jnp.where(even, jnp.concatenate([wv, other_v], 1), jnp.concatenate([other_v, wv], 1))
        self.qw, self.kvw = wq.shape[1], wk.shape[1]
        self.w = jnp.concatenate([wq, wk, wv], axis=1)
        self.n_row, self.n_col = lax.axis_size("row"), lax.axis_size("col")
        self.sub = x.shape[0] // self.n_col
        self.keep, self.arrived = [], []

    def halves(self, block_list):
        low = my_bit("col", 0)
        blocks = jnp.stack(block_list).reshape(len(block_list), self.n_col // 2, 2, self.sub, -1)
        return pick(blocks, 1 - low, 2), pick(blocks, low, 2)

    def project(self, half):
        scaled = (half.astype(F32) * self.gain).astype(BF16)
        rows = scaled.reshape(-1, scaled.shape[-1])
        out = jnp.dot(rows, self.w, preferred_element_type=F32)
        return out.reshape(half.shape[:-1] + (-1,))

    def halve(self, total, arrived, bit):
        mine = my_bit("col", bit)
        shape = (total.shape[0], -1, 2) + total.shape[2:]
        total, arrived = total.reshape(shape), arrived.reshape(shape)

        def part(which):
            return pick(total, which, 2) + pick(arrived, which, 2).astype(F32)

        return part(mine), part(1 - mine).astype(BF16)

    def flat(self, value):
        return value.reshape(-1, value.shape[-1])

    def kernel_rows(self):
        return [self.flat(v) for v in self.keep] + [self.flat(v) for v in self.arrived]


def whole(body, out_shape, scratch=(), flops=0, exps=0, moved=0):
    return pl.pallas_call(
        body,
        out_shape=out_shape,
        scratch_shapes=list(scratch),
        compiler_params=pltpu.CompilerParams(vmem_limit_bytes=40 * 1024 * 1024),
        cost_estimate=pl.CostEstimate(flops=flops, transcendentals=exps, bytes_accessed=moved),
    )


def on_device(*arrays):
    arrays = [a[0] for a in arrays]
    half = len(arrays) // 2
    d, u = Cascade(*arrays[:half]), Cascade(*arrays[half:])
    n_row, n_col, sub = d.n_row, d.n_col, d.sub
    block = n_col * sub
    features = d.x.shape[1] * n_col
    rows = n_row * sub
    qw, kvw = d.qw, d.kvw
    z, r = lax.axis_index("col"), lax.axis_index("row")
    chain = Chain()

    order = [o for o in range(n_row) if o < 2] + [o for o in range(n_row) if o >= 2]
    starts = (r ^ jnp.array(order, jnp.int32)) * block
    offsets = jnp.arange(sub, dtype=jnp.int32)
    q_pos = (starts[:, None] + z * sub + offsets).astype(F32).reshape(rows, 1)
    owners = (z ^ jnp.arange(n_col, dtype=jnp.int32)) * sub
    k_pos = (owners[:, None, None] + starts[:, None] + offsets).astype(F32).reshape(1, -1)
    width = HD // 2
    inverse_freq = 10000.0 ** (-jnp.arange(width, dtype=F32) / width)
    angles = q_pos * inverse_freq
    cosine = jnp.concatenate([jnp.cos(angles)] * 2, axis=1)
    sine = jnp.sin(angles)
    sine = jnp.concatenate([-sine, sine], axis=1)

    d_blocks = gather(d.x, "row")
    d_blocks[1] = swapped(d.x, "row", 0)

    def send_first(c, group, blocks_):
        send, kept = c.halves(chain.enter(*blocks_))
        product = c.project(send).astype(BF16)
        return product, kept

    def keep_first(c, kept, token):
        return c.project(tie(kept, token))

    def second(c, total, arrived):
        total, arrived = chain.enter(total, arrived)
        kept, product = c.halve(total, arrived, 1)
        arrived = swapped(product, "col", 1)
        chain.leave(product)
        for bit in range(2, bits_of("col")):
            kept, product = c.halve(kept, arrived, bit)
            arrived = swapped(product, "col", bit)
        c.keep.append(kept)
        c.arrived.append(arrived)

    def settle(c):
        c.arrived[-1] = chain.enter(c.arrived[-1])
        chain.leave(c.arrived[-1])

    def take_far(blocks_):
        values = chain.enter(*[blocks_[o] for o in far])
        values = list(values) if len(far) > 1 else [values]
        for o, value in zip(far, values):
            blocks_[o] = value
            blocks_[o | 1] = swapped(value, "row", 0)
        chain.leave(values[-1])
        return values

    far = [o for o in d_blocks if o >= 2]
    far_order = [o for o in order if o >= 2]

    product, kept = send_first(d, 0, [d_blocks[0], d_blocks[1]])
    d_arr_a = swapped(product, "col", 0)
    d_tot_a = keep_first(d, kept, product)
    u_near = swapped(tie(u.x, product), "row", 0)
    chain.leave(d_tot_a)
    squares = jnp.stack([jnp.sum(jnp.square(chain.enter(c.x).astype(F32)), axis=1) for c in (d, u)])
    other = swapped(squares, "col", 0)
    chain.leave(squares)
    u_prod_a, kept = send_first(u, 0, [u.x, u_near])
    u_kept = kept
    chain.leave(u_prod_a)
    second(d, d_tot_a, d_arr_a)
    u_arr_a = swapped(tie(u_prod_a, chain.token), "col", 0)

    d_far = take_far(d_blocks)
    u_blocks = gather(tie(u.x, *d_far), "row")
    product, kept = send_first(d, 1, [d_blocks[o] for o in far_order])
    d_arr_b = swapped(product, "col", 0)
    chain.leave(product)
    squares, other = chain.enter(squares, other)
    squares = squares + other
    other = swapped(squares, "col", 1)
    chain.leave(squares)
    u_tot_a = u.project(chain.enter(u_kept))
    chain.leave(u_tot_a)
    d_tot_b = d.project(chain.enter(kept))
    chain.leave(d_tot_b)
    settle(d)
    squares, other = chain.enter(squares, other)
    squares = squares + other
    for bit in range(2, bits_of("col")):
        squares = squares + swapped(squares, "col", bit)
    chain.leave(squares)
    sq = gather(squares, "row")
    second(u, u_tot_a, u_arr_a)

    take_far(u_blocks)
    settle(u)
    second(d, d_tot_b, d_arr_b)
    for o in list(sq):
        sq[o | 1] = swapped(tie(sq[o], chain.token), "row", 0)
    u_prod_b, kept = send_first(u, 1, [u_blocks[o] for o in far_order])
    u_arr_b = swapped(u_prod_b, "col", 0)
    u_tot_b = keep_first(u, kept, u_prod_b)
    chain.leave(u_tot_b)

    sums = jnp.stack([sq[o] for o in order])
    sums = pick(sums.reshape(n_row, 2, n_col, sub), z, 2)
    inverse = lax.rsqrt(sums / features + EPSILON).transpose(1, 0, 2).reshape(2, rows, 1)

    def make_pairs(c, scale):
        inputs = chain.enter(*c.kernel_rows())
        pair = whole(
            functools.partial(kv_kernel, qw, kvw),
            jax.ShapeDtypeStruct((rows, 2 * kvw), BF16),
            moved=2 * rows * (qw + 2 * kvw) * 6,
        )(*inputs, scale, cosine, sine)
        chain.leave(pair)
        return inputs, [pair] + [crossed(pair, "col", o) for o in range(1, n_col)]

    def attend(c, inputs, scale, pairs):
        pairs = chain.enter(*pairs)
        keys = rows * n_col
        out = whole(
            functools.partial(attention_kernel, qw, kvw, n_col),
            jax.ShapeDtypeStruct((rows, qw), BF16),
            scratch=[pltpu.VMEM((keys, kvw), BF16), pltpu.VMEM((keys, kvw), BF16), pltpu.VMEM((rows, keys), F32)],
            flops=4 * rows * keys * qw,
            exps=rows * keys * qw // HD,
            moved=rows * qw * 8,
        )(*inputs, scale, cosine, sine, q_pos, k_pos, *pairs)
        chain.leave(out)
        return out

    d_inputs, d_pairs = make_pairs(d, inverse[0])
    second(u, u_tot_b, u_arr_b)
    d_att = attend(d, d_inputs, inverse[0], d_pairs)
    d_got = gather(d_att, "col")
    d_got[1] = swapped(d_att, "col", 0)

    def out_first(c, pieces):
        pieces = chain.enter(*pieces)
        pieces = pieces if isinstance(pieces, (list, tuple)) else [pieces]
        shaped = jnp.stack([p.reshape(n_row // 2, 2, sub, qw) for p in pieces], axis=2)

        def dot(value):
            out = jnp.dot(value.reshape(-1, qw), c.wo, preferred_element_type=F32)
            return out.reshape(n_row // 2, -1, c.wo.shape[1])

        product = dot(shaped[:, 1]).astype(BF16)
        arrived = swapped(product, "row", 0)
        kept = dot(tie(shaped[:, 0], product))
        chain.leave(kept)
        return kept, arrived

    def out_second(kept, arrived):
        kept, arrived = chain.enter(kept, arrived)
        for bit in range(1, bits_of("row")):
            total = (kept + arrived.astype(F32)).reshape(-1, 2, *kept.shape[1:])
            product = total[:, 1].astype(BF16)
            kept, arrived = total[:, 0], swapped(product, "row", bit)
        chain.leave(product)
        return kept, arrived

    def out_third(c, kept, arrived, which, steps):
        kept, arrived = chain.enter(kept, arrived)
        residual = c.x.reshape(n_col, sub, -1)
        own = jnp.stack([pick(residual, z ^ o, 0) for o in which]).astype(F32)
        total = kept[0] + arrived[0].astype(F32)
        fresh = (own + total.reshape(own.shape)).astype(BF16)
        chain.leave(fresh)
        return from_behind(fresh, "section", steps)

    def finish(c, groups, *sent):
        by_name = {o: piece[i] for names, piece in zip(groups, sent) for i, o in enumerate(names)}
        both = jnp.stack([by_name[o] for o in range(n_col)])
        both = both.reshape((2,) * bits_of("col") + (sub, -1))
        for bit in range(bits_of("col")):
            dim = bits_of("col") - 1 - bit
            both = jnp.where(my_bit("col", bit) == 0, both, jnp.flip(both, dim))
        return both.reshape(c.x.shape)[None]

    def far_pieces(got):
        names = [o for o in got if o >= 2]
        values = chain.enter(*[got[o] for o in names])
        values = list(values) if len(names) > 1 else [values]
        chain.leave(values[-1])
        for o, value in zip(names, values):
            got[o] = value
            got[o | 1] = swapped(value, "col", 0)

    far_names = [[o for o in range(2, n_col) if o % 2 == 0], [o for o in range(2, n_col) if o % 2]]
    of_d, of_u = [[0, 1]] + far_names, [[0], [1]] + far_names

    def first(c, got, names):
        return out_first(c, [got[o] for o in names])

    u_inputs, u_pairs = make_pairs(u, inverse[1])
    d_p = first(d, d_got, of_d[0])
    far_pieces(d_got)
    d_p = out_second(*d_p)
    u_att = attend(u, u_inputs, inverse[1], u_pairs)
    u_got = gather(u_att, "col")
    u_got[1] = swapped(u_att, "col", 0)
    d_p = out_third(d, *d_p, of_d[0], 1)
    u_o = first(u, u_got, of_u[0])
    u_o = out_second(*u_o)
    d_m = first(d, d_got, of_d[1])
    d_m = out_second(*d_m)
    d_q = first(d, d_got, of_d[2])
    u_o = out_third(u, *u_o, of_u[0], -1)
    u_p = first(u, u_got, of_u[1])
    d_q = out_second(*d_q)
    u_p = out_second(*u_p)
    d_m = out_third(d, *d_m, of_d[1], 1)
    far_pieces(u_got)
    u_m = first(u, u_got, of_u[2])
    u_m = out_second(*u_m)
    d_q = out_third(d, *d_q, of_d[2], 1)
    u_p = out_third(u, *u_p, of_u[1], -1)
    u_q = first(u, u_got, of_u[3])
    u_q = out_second(*u_q)
    u_m = out_third(u, *u_m, of_u[2], -1)
    u_q = out_third(u, *u_q, of_u[3], -1)
    return finish(d, of_d, d_p, d_m, d_q), finish(u, of_u, u_o, u_p, u_m, u_q)


def solution(mesh):
    tokens = P("section", "row", "col")
    into, out_of = P("section", "col", "row"), P("section", "row", "col")
    one = (tokens, P("section", "col"), into, into, into, out_of)
    return jax.shard_map(
        on_device, mesh=mesh, in_specs=one + one, out_specs=(tokens, tokens), check_vma=False
    )
```

```python
import functools

import jax
import jax.numpy as jnp
from jax import lax
from jax.experimental import pallas as pl
from jax.experimental.pallas import tpu as pltpu
from jax.sharding import PartitionSpec as P

HD = 128
EPSILON = 1e-05
HIDDEN = -1e30
LOG2E = 1.4426950408889634
BF16 = jnp.bfloat16
F32 = jnp.float32


def swapped(value, axis, bit):
    return lax.ppermute(value, axis, [(i, i ^ (1 << bit)) for i in range(lax.axis_size(axis))])


def crossed(value, axis, bits):
    return lax.ppermute(value, axis, [(i, i ^ bits) for i in range(lax.axis_size(axis))])


def from_behind(value, axis, steps):
    count = lax.axis_size(axis)
    return lax.ppermute(value, axis, [(i, (i + steps) % count) for i in range(count)])


def bits_of(axis):
    return lax.axis_size(axis).bit_length() - 1


def my_bit(axis, bit):
    return (lax.axis_index(axis) >> bit) & 1


def pick(value, index, dim):
    return lax.dynamic_index_in_dim(value, index, dim, keepdims=False)


def tie(value, *deps):
    return lax.optimization_barrier((value, deps))[0]


class Chain:
    def __init__(self):
        self.token = None

    def enter(self, *values):
        out = values if self.token is None else tie(values, self.token)
        return out[0] if len(values) == 1 else out

    def leave(self, array):
        self.token = array


def turn(value, cosine, sine):
    return value * cosine + pltpu.roll(value, HD // 2, 1) * sine


def rows_of(keeps, arrivals, inverse, columns):
    parts = [k[:, columns] + a[:, columns].astype(F32) for k, a in zip(keeps, arrivals)]
    return jnp.concatenate(parts, axis=0) * inverse[...]


def kv_kernel(qw, kvw, keep_a, keep_b, arr_a, arr_b, inverse, cosine, sine, out):
    for start in range(0, 2 * kvw, HD):
        columns = slice(qw + start, qw + start + HD)
        value = rows_of((keep_a, keep_b), (arr_a, arr_b), inverse, columns)
        if start < kvw:
            value = turn(value, cosine[...], sine[...])
        out[:, start : start + HD] = value.astype(BF16)


def attention_kernel(
    qw, kvw, count, keep_a, keep_b, arr_a, arr_b, inverse, cosine, sine, q_pos, k_pos, *rest
):
    pairs, (out, keys, values, bias) = rest[:count], rest[count:]
    rows = pairs[0].shape[0]
    for i, pair in enumerate(pairs):
        keys[i * rows : (i + 1) * rows] = pair[:, :kvw]
        values[i * rows : (i + 1) * rows] = pair[:, kvw:]
    bias[...] = jnp.where(q_pos[...] >= k_pos[...], 0.0, HIDDEN)
    group = (qw // HD) // (kvw // HD)
    for head in range(qw // HD):
        columns = slice(head * HD, (head + 1) * HD)
        kv_columns = slice(head // group * HD, (head // group + 1) * HD)
        query = rows_of((keep_a, keep_b), (arr_a, arr_b), inverse, columns)
        query = turn(query, cosine[...], sine[...]).astype(BF16)
        scores = lax.dot_general(
            query, keys[:, kv_columns], (((1,), (1,)), ((), ())), preferred_element_type=F32
        )
        scores = scores + bias[...]
        top = jnp.max(scores, axis=1, keepdims=True)
        probs = jnp.exp2((scores - top) * (LOG2E / HD**0.5))
        total = jnp.sum(probs, axis=1, keepdims=True)
        mixed = jnp.dot(probs.astype(BF16), values[:, kv_columns], preferred_element_type=F32)
        out[:, columns] = (mixed / total).astype(BF16)


def gather(block, axis):
    blocks = {0: block}
    for bit in range(1, bits_of(axis)):
        for o in list(blocks):
            blocks[o | 1 << bit] = swapped(blocks[o], axis, bit)
    return blocks


class Cascade:
    def __init__(self, x, gain, wq, wk, wv, wo):
        self.x, self.gain, self.wo = x, gain, wo
        if wk.shape[1] < HD:
            other_k, other_v = swapped((wk, wv), "row", 0)
            even = lax.axis_index("row") % 2 == 0
            wk = jnp.where(even, jnp.concatenate([wk, other_k], 1), jnp.concatenate([other_k, wk], 1))
            wv = jnp.where(even, jnp.concatenate([wv, other_v], 1), jnp.concatenate([other_v, wv], 1))
        self.qw, self.kvw = wq.shape[1], wk.shape[1]
        self.w = jnp.concatenate([wq, wk, wv], axis=1)
        self.n_row, self.n_col = lax.axis_size("row"), lax.axis_size("col")
        self.sub = x.shape[0] // self.n_col
        self.keep, self.arrived = [], []

    def halves(self, block_list):
        low = my_bit("col", 0)
        blocks = jnp.stack(block_list).reshape(len(block_list), self.n_col // 2, 2, self.sub, -1)
        return pick(blocks, 1 - low, 2), pick(blocks, low, 2)

    def project(self, half):
        scaled = (half.astype(F32) * self.gain).astype(BF16)
        rows = scaled.reshape(-1, scaled.shape[-1])
        out = jnp.dot(rows, self.w, preferred_element_type=F32)
        return out.reshape(half.shape[:-1] + (-1,))

    def halve(self, total, arrived, bit):
        mine = my_bit("col", bit)
        shape = (total.shape[0], -1, 2) + total.shape[2:]
        total, arrived = total.reshape(shape), arrived.reshape(shape)

        def part(which):
            return pick(total, which, 2) + pick(arrived, which, 2).astype(F32)

        return part(mine), part(1 - mine).astype(BF16)

    def flat(self, value):
        return value.reshape(-1, value.shape[-1])

    def kernel_rows(self):
        return [self.flat(v) for v in self.keep] + [self.flat(v) for v in self.arrived]


def whole(body, out_shape, scratch=(), flops=0, exps=0, moved=0):
    return pl.pallas_call(
        body,
        out_shape=out_shape,
        scratch_shapes=list(scratch),
        compiler_params=pltpu.CompilerParams(vmem_limit_bytes=40 * 1024 * 1024),
        cost_estimate=pl.CostEstimate(flops=flops, transcendentals=exps, bytes_accessed=moved),
    )


def on_device(*arrays):
    arrays = [a[0] for a in arrays]
    half = len(arrays) // 2
    d, u = Cascade(*arrays[:half]), Cascade(*arrays[half:])
    n_row, n_col, sub = d.n_row, d.n_col, d.sub
    block = n_col * sub
    features = d.x.shape[1] * n_col
    rows = n_row * sub
    qw, kvw = d.qw, d.kvw
    z, r = lax.axis_index("col"), lax.axis_index("row")
    chain = Chain()

    order = [o for o in range(n_row) if o < 2] + [o for o in range(n_row) if o >= 2]
    starts = (r ^ jnp.array(order, jnp.int32)) * block
    offsets = jnp.arange(sub, dtype=jnp.int32)
    q_pos = (starts[:, None] + z * sub + offsets).astype(F32).reshape(rows, 1)
    owners = (z ^ jnp.arange(n_col, dtype=jnp.int32)) * sub
    k_pos = (owners[:, None, None] + starts[:, None] + offsets).astype(F32).reshape(1, -1)
    width = HD // 2
    inverse_freq = 10000.0 ** (-jnp.arange(width, dtype=F32) / width)
    angles = q_pos * inverse_freq
    cosine = jnp.concatenate([jnp.cos(angles)] * 2, axis=1)
    sine = jnp.sin(angles)
    sine = jnp.concatenate([-sine, sine], axis=1)

    d_blocks = gather(d.x, "row")
    d_blocks[1] = swapped(d.x, "row", 0)

    def send_first(c, group, blocks_):
        send, kept = c.halves(chain.enter(*blocks_))
        product = c.project(send).astype(BF16)
        return product, kept

    def keep_first(c, kept, token):
        return c.project(tie(kept, token))

    def second(c, total, arrived):
        total, arrived = chain.enter(total, arrived)
        kept, product = c.halve(total, arrived, 1)
        arrived = swapped(product, "col", 1)
        chain.leave(product)
        for bit in range(2, bits_of("col")):
            kept, product = c.halve(kept, arrived, bit)
            arrived = swapped(product, "col", bit)
        c.keep.append(kept)
        c.arrived.append(arrived)

    def settle(c):
        c.arrived[-1] = chain.enter(c.arrived[-1])
        chain.leave(c.arrived[-1])

    def take_far(blocks_):
        values = chain.enter(*[blocks_[o] for o in far])
        values = list(values) if len(far) > 1 else [values]
        for o, value in zip(far, values):
            blocks_[o] = value
            blocks_[o | 1] = swapped(value, "row", 0)
        chain.leave(values[-1])
        return values

    far = [o for o in d_blocks if o >= 2]
    far_order = [o for o in order if o >= 2]

    product, kept = send_first(d, 0, [d_blocks[0], d_blocks[1]])
    d_arr_a = swapped(product, "col", 0)
    d_tot_a = keep_first(d, kept, product)
    u_near = swapped(tie(u.x, product), "row", 0)
    chain.leave(d_tot_a)
    squares = jnp.stack([jnp.sum(jnp.square(chain.enter(c.x).astype(F32)), axis=1) for c in (d, u)])
    other = swapped(squares, "col", 0)
    chain.leave(squares)
    u_prod_a, kept = send_first(u, 0, [u.x, u_near])
    u_kept = kept
    chain.leave(u_prod_a)
    second(d, d_tot_a, d_arr_a)
    u_arr_a = swapped(tie(u_prod_a, chain.token), "col", 0)

    d_far = take_far(d_blocks)
    u_blocks = gather(tie(u.x, *d_far), "row")
    squares, other = chain.enter(squares, other)
    squares = squares + other
    other = swapped(squares, "col", 1)
    chain.leave(squares)
    u_tot_a = u.project(chain.enter(u_kept))
    chain.leave(u_tot_a)
    product, kept = send_first(d, 1, [d_blocks[o] for o in far_order])
    d_arr_b = swapped(product, "col", 0)
    d_tot_b = keep_first(d, kept, product)
    chain.leave(d_tot_b)
    settle(d)
    squares, other = chain.enter(squares, other)
    squares = squares + other
    for bit in range(2, bits_of("col")):
        squares = squares + swapped(squares, "col", bit)
    chain.leave(squares)
    sq = gather(squares, "row")
    second(u, u_tot_a, u_arr_a)

    take_far(u_blocks)
    second(d, d_tot_b, d_arr_b)
    for o in list(sq):
        sq[o | 1] = swapped(tie(sq[o], chain.token), "row", 0)
    u_prod_b, kept = send_first(u, 1, [u_blocks[o] for o in far_order])
    u_arr_b = swapped(u_prod_b, "col", 0)
    u_tot_b = keep_first(u, kept, u_prod_b)
    chain.leave(u_tot_b)
    settle(u)

    sums = jnp.stack([sq[o] for o in order])
    sums = pick(sums.reshape(n_row, 2, n_col, sub), z, 2)
    inverse = lax.rsqrt(sums / features + EPSILON).transpose(1, 0, 2).reshape(2, rows, 1)

    def make_pairs(c, scale):
        inputs = chain.enter(*c.kernel_rows())
        pair = whole(
            functools.partial(kv_kernel, qw, kvw),
            jax.ShapeDtypeStruct((rows, 2 * kvw), BF16),
            moved=2 * rows * (qw + 2 * kvw) * 6,
        )(*inputs, scale, cosine, sine)
        chain.leave(pair)
        return inputs, [pair] + [crossed(pair, "col", o) for o in range(1, n_col)]

    def attend(c, inputs, scale, pairs):
        pairs = chain.enter(*pairs)
        keys = rows * n_col
        out = whole(
            functools.partial(attention_kernel, qw, kvw, n_col),
            jax.ShapeDtypeStruct((rows, qw), BF16),
            scratch=[pltpu.VMEM((keys, kvw), BF16), pltpu.VMEM((keys, kvw), BF16), pltpu.VMEM((rows, keys), F32)],
            flops=4 * rows * keys * qw,
            exps=rows * keys * qw // HD,
            moved=rows * qw * 8,
        )(*inputs, scale, cosine, sine, q_pos, k_pos, *pairs)
        chain.leave(out)
        return out

    d_inputs, d_pairs = make_pairs(d, inverse[0])
    second(u, u_tot_b, u_arr_b)
    d_att = attend(d, d_inputs, inverse[0], d_pairs)
    d_got = gather(d_att, "col")
    d_got[1] = swapped(d_att, "col", 0)

    def out_first(c, pieces):
        pieces = chain.enter(*pieces)
        pieces = pieces if isinstance(pieces, (list, tuple)) else [pieces]
        shaped = jnp.stack([p.reshape(n_row // 2, 2, sub, qw) for p in pieces], axis=2)

        def dot(value):
            out = jnp.dot(value.reshape(-1, qw), c.wo, preferred_element_type=F32)
            return out.reshape(n_row // 2, -1, c.wo.shape[1])

        product = dot(shaped[:, 1]).astype(BF16)
        arrived = swapped(product, "row", 0)
        kept = dot(tie(shaped[:, 0], product))
        chain.leave(kept)
        return kept, arrived

    def out_second(kept, arrived):
        kept, arrived = chain.enter(kept, arrived)
        for bit in range(1, bits_of("row")):
            total = (kept + arrived.astype(F32)).reshape(-1, 2, *kept.shape[1:])
            product = total[:, 1].astype(BF16)
            kept, arrived = total[:, 0], swapped(product, "row", bit)
        chain.leave(product)
        return kept, arrived

    def out_third(c, kept, arrived, which, steps):
        kept, arrived = chain.enter(kept, arrived)
        residual = c.x.reshape(n_col, sub, -1)
        own = jnp.stack([pick(residual, z ^ o, 0) for o in which]).astype(F32)
        total = kept[0] + arrived[0].astype(F32)
        fresh = (own + total.reshape(own.shape)).astype(BF16)
        chain.leave(fresh)
        return from_behind(fresh, "section", steps)

    def finish(c, *sent):
        by_name = {o: piece[i] for names, piece in zip(groups, sent) for i, o in enumerate(names)}
        both = jnp.stack([by_name[o] for o in range(n_col)])
        both = both.reshape((2,) * bits_of("col") + (sub, -1))
        for bit in range(bits_of("col")):
            dim = bits_of("col") - 1 - bit
            both = jnp.where(my_bit("col", bit) == 0, both, jnp.flip(both, dim))
        return both.reshape(c.x.shape)[None]

    def far_pieces(got):
        names = [o for o in got if o >= 2]
        values = chain.enter(*[got[o] for o in names])
        values = list(values) if len(names) > 1 else [values]
        chain.leave(values[-1])
        for o, value in zip(names, values):
            got[o] = value
            got[o | 1] = swapped(value, "col", 0)

    groups = [[0, 1], [o for o in range(2, n_col) if o % 2 == 0], [o for o in range(2, n_col) if o % 2]]

    def first(c, got, i):
        return out_first(c, [got[o] for o in groups[i]])

    u_inputs, u_pairs = make_pairs(u, inverse[1])
    far_pieces(d_got)
    d_p = first(d, d_got, 0)
    d_p = out_second(*d_p)
    u_att = attend(u, u_inputs, inverse[1], u_pairs)
    u_got = gather(u_att, "col")
    u_got[1] = swapped(u_att, "col", 0)
    d_p = out_third(d, *d_p, groups[0], 1)
    d_m = first(d, d_got, 1)
    d_m = out_second(*d_m)
    d_q = first(d, d_got, 2)
    u_p = first(u, u_got, 0)
    d_q = out_second(*d_q)
    u_p = out_second(*u_p)
    d_m = out_third(d, *d_m, groups[1], 1)
    far_pieces(u_got)
    u_m = first(u, u_got, 1)
    u_m = out_second(*u_m)
    d_q = out_third(d, *d_q, groups[2], 1)
    u_p = out_third(u, *u_p, groups[0], -1)
    u_q = first(u, u_got, 2)
    u_q = out_second(*u_q)
    u_m = out_third(u, *u_m, groups[1], -1)
    u_q = out_third(u, *u_q, groups[2], -1)
    return finish(d, d_p, d_m, d_q), finish(u, u_p, u_m, u_q)


def solution(mesh):
    tokens = P("section", "row", "col")
    into, out_of = P("section", "col", "row"), P("section", "row", "col")
    one = (tokens, P("section", "col"), into, into, into, out_of)
    return jax.shard_map(
        on_device, mesh=mesh, in_specs=one + one, out_specs=(tokens, tokens), check_vma=False
    )
```

```python
import functools

import jax
import jax.numpy as jnp
from jax import lax
from jax.experimental import pallas as pl
from jax.experimental.pallas import tpu as pltpu
from jax.sharding import PartitionSpec as P

HD = 128
EPSILON = 1e-05
HIDDEN = -1e30
LOG2E = 1.4426950408889634
BF16 = jnp.bfloat16
F32 = jnp.float32


def swapped(value, axis, bit):
    return lax.ppermute(value, axis, [(i, i ^ (1 << bit)) for i in range(lax.axis_size(axis))])


def crossed(value, axis, bits):
    return lax.ppermute(value, axis, [(i, i ^ bits) for i in range(lax.axis_size(axis))])


def from_behind(value, axis, steps):
    count = lax.axis_size(axis)
    return lax.ppermute(value, axis, [(i, (i + steps) % count) for i in range(count)])


def bits_of(axis):
    return lax.axis_size(axis).bit_length() - 1


def my_bit(axis, bit):
    return (lax.axis_index(axis) >> bit) & 1


def pick(value, index, dim):
    return lax.dynamic_index_in_dim(value, index, dim, keepdims=False)


def tie(value, *deps):
    return lax.optimization_barrier((value, deps))[0]


class Chain:
    def __init__(self):
        self.token = None

    def enter(self, *values):
        out = values if self.token is None else tie(values, self.token)
        return out[0] if len(values) == 1 else out

    def leave(self, array):
        self.token = array


def turn(value, cosine, sine):
    return value * cosine + pltpu.roll(value, HD // 2, 1) * sine


def rows_of(keeps, arrivals, inverse, columns):
    parts = [k[:, columns] + a[:, columns].astype(F32) for k, a in zip(keeps, arrivals)]
    return jnp.concatenate(parts, axis=0) * inverse[...]


def kv_kernel(qw, kvw, keep_a, keep_b, arr_a, arr_b, inverse, cosine, sine, out):
    for start in range(0, 2 * kvw, HD):
        columns = slice(qw + start, qw + start + HD)
        value = rows_of((keep_a, keep_b), (arr_a, arr_b), inverse, columns)
        if start < kvw:
            value = turn(value, cosine[...], sine[...])
        out[:, start : start + HD] = value.astype(BF16)


def attention_kernel(
    qw, kvw, count, keep_a, keep_b, arr_a, arr_b, inverse, cosine, sine, q_pos, k_pos, *rest
):
    pairs, (out, keys, values, bias) = rest[:count], rest[count:]
    rows = pairs[0].shape[0]
    for i, pair in enumerate(pairs):
        keys[i * rows : (i + 1) * rows] = pair[:, :kvw]
        values[i * rows : (i + 1) * rows] = pair[:, kvw:]
    bias[...] = jnp.where(q_pos[...] >= k_pos[...], 0.0, HIDDEN)
    group = (qw // HD) // (kvw // HD)
    for head in range(qw // HD):
        columns = slice(head * HD, (head + 1) * HD)
        kv_columns = slice(head // group * HD, (head // group + 1) * HD)
        query = rows_of((keep_a, keep_b), (arr_a, arr_b), inverse, columns)
        query = turn(query, cosine[...], sine[...]).astype(BF16)
        scores = lax.dot_general(
            query, keys[:, kv_columns], (((1,), (1,)), ((), ())), preferred_element_type=F32
        )
        scores = scores + bias[...]
        top = jnp.max(scores, axis=1, keepdims=True)
        probs = jnp.exp2((scores - top) * (LOG2E / HD**0.5))
        total = jnp.sum(probs, axis=1, keepdims=True)
        mixed = jnp.dot(probs.astype(BF16), values[:, kv_columns], preferred_element_type=F32)
        out[:, columns] = (mixed / total).astype(BF16)


def gather(block, axis):
    blocks = {0: block}
    for bit in range(1, bits_of(axis)):
        for o in list(blocks):
            blocks[o | 1 << bit] = swapped(blocks[o], axis, bit)
    return blocks


class Cascade:
    def __init__(self, x, gain, wq, wk, wv, wo):
        self.x, self.gain, self.wo = x, gain, wo
        if wk.shape[1] < HD:
            other_k, other_v = swapped((wk, wv), "row", 0)
            even = lax.axis_index("row") % 2 == 0
            wk = jnp.where(even, jnp.concatenate([wk, other_k], 1), jnp.concatenate([other_k, wk], 1))
            wv = jnp.where(even, jnp.concatenate([wv, other_v], 1), jnp.concatenate([other_v, wv], 1))
        self.qw, self.kvw = wq.shape[1], wk.shape[1]
        self.w = jnp.concatenate([wq, wk, wv], axis=1)
        self.n_row, self.n_col = lax.axis_size("row"), lax.axis_size("col")
        self.sub = x.shape[0] // self.n_col
        self.keep, self.arrived = [], []

    def halves(self, block_list):
        low = my_bit("col", 0)
        blocks = jnp.stack(block_list).reshape(len(block_list), self.n_col // 2, 2, self.sub, -1)
        return pick(blocks, 1 - low, 2), pick(blocks, low, 2)

    def project(self, half):
        scaled = (half.astype(F32) * self.gain).astype(BF16)
        rows = scaled.reshape(-1, scaled.shape[-1])
        out = jnp.dot(rows, self.w, preferred_element_type=F32)
        return out.reshape(half.shape[:-1] + (-1,))

    def halve(self, total, arrived, bit):
        mine = my_bit("col", bit)
        shape = (total.shape[0], -1, 2) + total.shape[2:]
        total, arrived = total.reshape(shape), arrived.reshape(shape)

        def part(which):
            return pick(total, which, 2) + pick(arrived, which, 2).astype(F32)

        return part(mine), part(1 - mine).astype(BF16)

    def flat(self, value):
        return value.reshape(-1, value.shape[-1])

    def kernel_rows(self):
        return [self.flat(v) for v in self.keep] + [self.flat(v) for v in self.arrived]


def whole(body, out_shape, scratch=(), flops=0, exps=0, moved=0):
    return pl.pallas_call(
        body,
        out_shape=out_shape,
        scratch_shapes=list(scratch),
        compiler_params=pltpu.CompilerParams(vmem_limit_bytes=40 * 1024 * 1024),
        cost_estimate=pl.CostEstimate(flops=flops, transcendentals=exps, bytes_accessed=moved),
    )


def on_device(*arrays):
    arrays = [a[0] for a in arrays]
    half = len(arrays) // 2
    d, u = Cascade(*arrays[:half]), Cascade(*arrays[half:])
    n_row, n_col, sub = d.n_row, d.n_col, d.sub
    block = n_col * sub
    features = d.x.shape[1] * n_col
    rows = n_row * sub
    qw, kvw = d.qw, d.kvw
    z, r = lax.axis_index("col"), lax.axis_index("row")
    chain = Chain()

    order = [o for o in range(n_row) if o < 2] + [o for o in range(n_row) if o >= 2]
    starts = (r ^ jnp.array(order, jnp.int32)) * block
    offsets = jnp.arange(sub, dtype=jnp.int32)
    q_pos = (starts[:, None] + z * sub + offsets).astype(F32).reshape(rows, 1)
    owners = (z ^ jnp.arange(n_col, dtype=jnp.int32)) * sub
    k_pos = (owners[:, None, None] + starts[:, None] + offsets).astype(F32).reshape(1, -1)
    width = HD // 2
    inverse_freq = 10000.0 ** (-jnp.arange(width, dtype=F32) / width)
    angles = q_pos * inverse_freq
    cosine = jnp.concatenate([jnp.cos(angles)] * 2, axis=1)
    sine = jnp.sin(angles)
    sine = jnp.concatenate([-sine, sine], axis=1)

    d_blocks = gather(d.x, "row")
    d_blocks[1] = swapped(d.x, "row", 0)

    def send_first(c, group, blocks_):
        send, kept = c.halves(chain.enter(*blocks_))
        product = c.project(send).astype(BF16)
        return product, kept

    def keep_first(c, kept, token):
        return c.project(tie(kept, token))

    def second(c, total, arrived):
        total, arrived = chain.enter(total, arrived)
        kept, product = c.halve(total, arrived, 1)
        arrived = swapped(product, "col", 1)
        chain.leave(product)
        for bit in range(2, bits_of("col")):
            kept, product = c.halve(kept, arrived, bit)
            arrived = swapped(product, "col", bit)
        c.keep.append(kept)
        c.arrived.append(arrived)

    def settle(c):
        c.arrived[-1] = chain.enter(c.arrived[-1])
        chain.leave(c.arrived[-1])

    def take_far(blocks_):
        values = chain.enter(*[blocks_[o] for o in far])
        values = list(values) if len(far) > 1 else [values]
        for o, value in zip(far, values):
            blocks_[o] = value
            blocks_[o | 1] = swapped(value, "row", 0)
        chain.leave(values[-1])
        return values

    far = [o for o in d_blocks if o >= 2]
    far_order = [o for o in order if o >= 2]

    product, kept = send_first(d, 0, [d_blocks[0], d_blocks[1]])
    d_arr_a = swapped(product, "col", 0)
    d_tot_a = keep_first(d, kept, product)
    u_near = swapped(tie(u.x, product), "row", 0)
    chain.leave(d_tot_a)
    squares = jnp.stack([jnp.sum(jnp.square(chain.enter(c.x).astype(F32)), axis=1) for c in (d, u)])
    other = swapped(squares, "col", 0)
    chain.leave(squares)
    u_prod_a, kept = send_first(u, 0, [u.x, u_near])
    u_kept = kept
    chain.leave(u_prod_a)
    second(d, d_tot_a, d_arr_a)
    u_arr_a = swapped(tie(u_prod_a, chain.token), "col", 0)

    d_far = take_far(d_blocks)
    u_blocks = gather(tie(u.x, *d_far), "row")
    squares, other = chain.enter(squares, other)
    squares = squares + other
    other = swapped(squares, "col", 1)
    chain.leave(squares)
    u_tot_a = u.project(chain.enter(u_kept))
    chain.leave(u_tot_a)
    product, kept = send_first(d, 1, [d_blocks[o] for o in far_order])
    d_arr_b = swapped(product, "col", 0)
    d_tot_b = keep_first(d, kept, product)
    chain.leave(d_tot_b)
    settle(d)
    squares, other = chain.enter(squares, other)
    squares = squares + other
    for bit in range(2, bits_of("col")):
        squares = squares + swapped(squares, "col", bit)
    chain.leave(squares)
    sq = gather(squares, "row")
    second(u, u_tot_a, u_arr_a)

    take_far(u_blocks)
    second(d, d_tot_b, d_arr_b)
    for o in list(sq):
        sq[o | 1] = swapped(tie(sq[o], chain.token), "row", 0)
    u_prod_b, kept = send_first(u, 1, [u_blocks[o] for o in far_order])
    u_arr_b = swapped(u_prod_b, "col", 0)
    u_tot_b = keep_first(u, kept, u_prod_b)
    chain.leave(u_tot_b)
    settle(u)

    sums = jnp.stack([sq[o] for o in order])
    sums = pick(sums.reshape(n_row, 2, n_col, sub), z, 2)
    inverse = lax.rsqrt(sums / features + EPSILON).transpose(1, 0, 2).reshape(2, rows, 1)

    def make_pairs(c, scale):
        inputs = chain.enter(*c.kernel_rows())
        pair = whole(
            functools.partial(kv_kernel, qw, kvw),
            jax.ShapeDtypeStruct((rows, 2 * kvw), BF16),
            moved=2 * rows * (qw + 2 * kvw) * 6,
        )(*inputs, scale, cosine, sine)
        chain.leave(pair)
        return inputs, [pair] + [crossed(pair, "col", o) for o in range(1, n_col)]

    def attend(c, inputs, scale, pairs):
        pairs = chain.enter(*pairs)
        keys = rows * n_col
        out = whole(
            functools.partial(attention_kernel, qw, kvw, n_col),
            jax.ShapeDtypeStruct((rows, qw), BF16),
            scratch=[pltpu.VMEM((keys, kvw), BF16), pltpu.VMEM((keys, kvw), BF16), pltpu.VMEM((rows, keys), F32)],
            flops=4 * rows * keys * qw,
            exps=rows * keys * qw // HD,
            moved=rows * qw * 8,
        )(*inputs, scale, cosine, sine, q_pos, k_pos, *pairs)
        chain.leave(out)
        return out

    d_inputs, d_pairs = make_pairs(d, inverse[0])
    second(u, u_tot_b, u_arr_b)
    d_att = attend(d, d_inputs, inverse[0], d_pairs)
    d_got = gather(d_att, "col")
    d_got[1] = swapped(d_att, "col", 0)

    def out_first(c, pieces):
        pieces = chain.enter(*pieces)
        pieces = pieces if isinstance(pieces, (list, tuple)) else [pieces]
        shaped = jnp.stack([p.reshape(n_row // 2, 2, sub, qw) for p in pieces], axis=2)

        def dot(value):
            out = jnp.dot(value.reshape(-1, qw), c.wo, preferred_element_type=F32)
            return out.reshape(n_row // 2, -1, c.wo.shape[1])

        product = dot(shaped[:, 1]).astype(BF16)
        arrived = swapped(product, "row", 0)
        kept = dot(tie(shaped[:, 0], product))
        chain.leave(kept)
        return kept, arrived

    def out_second(kept, arrived):
        kept, arrived = chain.enter(kept, arrived)
        for bit in range(1, bits_of("row")):
            total = (kept + arrived.astype(F32)).reshape(-1, 2, *kept.shape[1:])
            product = total[:, 1].astype(BF16)
            kept, arrived = total[:, 0], swapped(product, "row", bit)
        chain.leave(product)
        return kept, arrived

    def out_third(c, kept, arrived, which, steps):
        kept, arrived = chain.enter(kept, arrived)
        residual = c.x.reshape(n_col, sub, -1)
        own = jnp.stack([pick(residual, z ^ o, 0) for o in which]).astype(F32)
        total = kept[0] + arrived[0].astype(F32)
        fresh = (own + total.reshape(own.shape)).astype(BF16)
        chain.leave(fresh)
        return from_behind(fresh, "section", steps)

    def finish(c, groups, *sent):
        by_name = {o: piece[i] for names, piece in zip(groups, sent) for i, o in enumerate(names)}
        both = jnp.stack([by_name[o] for o in range(n_col)])
        both = both.reshape((2,) * bits_of("col") + (sub, -1))
        for bit in range(bits_of("col")):
            dim = bits_of("col") - 1 - bit
            both = jnp.where(my_bit("col", bit) == 0, both, jnp.flip(both, dim))
        return both.reshape(c.x.shape)[None]

    def far_pieces(got):
        names = [o for o in got if o >= 2]
        values = chain.enter(*[got[o] for o in names])
        values = list(values) if len(names) > 1 else [values]
        chain.leave(values[-1])
        for o, value in zip(names, values):
            got[o] = value
            got[o | 1] = swapped(value, "col", 0)

    far_names = [[o for o in range(2, n_col) if o % 2 == 0], [o for o in range(2, n_col) if o % 2]]
    of_d, of_u = [[0, 1]] + far_names, [[0], [1]] + far_names

    def first(c, got, names):
        return out_first(c, [got[o] for o in names])

    def landed(sent):
        sent = chain.enter(sent)
        chain.leave(sent)
        return sent

    u_inputs, u_pairs = make_pairs(u, inverse[1])
    far_pieces(d_got)
    d_p = first(d, d_got, of_d[0])
    d_p = out_second(*d_p)
    u_att = attend(u, u_inputs, inverse[1], u_pairs)
    u_got = gather(u_att, "col")
    u_got[1] = swapped(u_att, "col", 0)
    d_p = out_third(d, *d_p, of_d[0], 1)
    d_m = first(d, d_got, of_d[1])
    d_m = out_second(*d_m)
    d_q = first(d, d_got, of_d[2])
    d_q = out_second(*d_q)
    u_o = first(u, u_got, of_u[0])
    u_o = out_second(*u_o)
    d_m = out_third(d, *d_m, of_d[1], 1)
    d_q = out_third(d, *d_q, of_d[2], 1)
    d_p = landed(d_p)
    d_m = landed(d_m)
    u_p = first(u, u_got, of_u[1])
    u_p = out_second(*u_p)
    far_pieces(u_got)
    u_m = first(u, u_got, of_u[2])
    u_m = out_second(*u_m)
    u_o = out_third(u, *u_o, of_u[0], -1)
    d_q = landed(d_q)
    u_p = out_third(u, *u_p, of_u[1], -1)
    u_q = first(u, u_got, of_u[3])
    u_q = out_second(*u_q)
    u_o = landed(u_o)
    u_m = out_third(u, *u_m, of_u[2], -1)
    u_p = landed(u_p)
    u_q = out_third(u, *u_q, of_u[3], -1)
    return finish(d, of_d, d_p, d_m, d_q), finish(u, of_u, u_o, u_p, u_m, u_q)


def solution(mesh):
    tokens = P("section", "row", "col")
    into, out_of = P("section", "col", "row"), P("section", "row", "col")
    one = (tokens, P("section", "col"), into, into, into, out_of)
    return jax.shard_map(
        on_device, mesh=mesh, in_specs=one + one, out_specs=(tokens, tokens), check_vma=False
    )
```

```python
import functools

import jax
import jax.numpy as jnp
from jax import lax
from jax.experimental import pallas as pl
from jax.experimental.pallas import tpu as pltpu
from jax.sharding import PartitionSpec as P

HD = 128
EPSILON = 1e-05
HIDDEN = -1e30
LOG2E = 1.4426950408889634
BF16 = jnp.bfloat16
F32 = jnp.float32


def swapped(value, axis, bit):
    return lax.ppermute(value, axis, [(i, i ^ (1 << bit)) for i in range(lax.axis_size(axis))])


def crossed(value, axis, bits):
    return lax.ppermute(value, axis, [(i, i ^ bits) for i in range(lax.axis_size(axis))])


def from_behind(value, axis, steps):
    count = lax.axis_size(axis)
    return lax.ppermute(value, axis, [(i, (i + steps) % count) for i in range(count)])


def bits_of(axis):
    return lax.axis_size(axis).bit_length() - 1


def my_bit(axis, bit):
    return (lax.axis_index(axis) >> bit) & 1


def pick(value, index, dim):
    return lax.dynamic_index_in_dim(value, index, dim, keepdims=False)


def tie(value, *deps):
    return lax.optimization_barrier((value, deps))[0]


class Chain:
    def __init__(self):
        self.token = None

    def enter(self, *values):
        out = values if self.token is None else tie(values, self.token)
        return out[0] if len(values) == 1 else out

    def leave(self, array):
        self.token = array


def turn(value, cosine, sine):
    return value * cosine + pltpu.roll(value, HD // 2, 1) * sine


def rows_of(keeps, arrivals, inverse, columns):
    parts = [k[:, columns] + a[:, columns].astype(F32) for k, a in zip(keeps, arrivals)]
    return jnp.concatenate(parts, axis=0) * inverse[...]


def kv_kernel(qw, kvw, keep_a, keep_b, arr_a, arr_b, inverse, cosine, sine, out):
    for start in range(0, 2 * kvw, HD):
        columns = slice(qw + start, qw + start + HD)
        value = rows_of((keep_a, keep_b), (arr_a, arr_b), inverse, columns)
        if start < kvw:
            value = turn(value, cosine[...], sine[...])
        out[:, start : start + HD] = value.astype(BF16)


def attention_kernel(
    qw, kvw, count, keep_a, keep_b, arr_a, arr_b, inverse, cosine, sine, q_pos, k_pos, *rest
):
    pairs, (out, keys, values, bias) = rest[:count], rest[count:]
    rows = pairs[0].shape[0]
    for i, pair in enumerate(pairs):
        keys[i * rows : (i + 1) * rows] = pair[:, :kvw]
        values[i * rows : (i + 1) * rows] = pair[:, kvw:]
    bias[...] = jnp.where(q_pos[...] >= k_pos[...], 0.0, HIDDEN)
    group = (qw // HD) // (kvw // HD)
    for head in range(qw // HD):
        columns = slice(head * HD, (head + 1) * HD)
        kv_columns = slice(head // group * HD, (head // group + 1) * HD)
        query = rows_of((keep_a, keep_b), (arr_a, arr_b), inverse, columns)
        query = turn(query, cosine[...], sine[...]).astype(BF16)
        scores = lax.dot_general(
            query, keys[:, kv_columns], (((1,), (1,)), ((), ())), preferred_element_type=F32
        )
        scores = scores + bias[...]
        top = jnp.max(scores, axis=1, keepdims=True)
        probs = jnp.exp2((scores - top) * (LOG2E / HD**0.5))
        total = jnp.sum(probs, axis=1, keepdims=True)
        mixed = jnp.dot(probs.astype(BF16), values[:, kv_columns], preferred_element_type=F32)
        out[:, columns] = (mixed / total).astype(BF16)


def gather(block, axis):
    blocks = {0: block}
    for bit in range(1, bits_of(axis)):
        for o in list(blocks):
            blocks[o | 1 << bit] = swapped(blocks[o], axis, bit)
    return blocks


class Cascade:
    def __init__(self, x, gain, wq, wk, wv, wo):
        self.x, self.gain, self.wo = x, gain, wo
        if wk.shape[1] < HD:
            other_k, other_v = swapped((wk, wv), "row", 0)
            even = lax.axis_index("row") % 2 == 0
            wk = jnp.where(even, jnp.concatenate([wk, other_k], 1), jnp.concatenate([other_k, wk], 1))
            wv = jnp.where(even, jnp.concatenate([wv, other_v], 1), jnp.concatenate([other_v, wv], 1))
        self.qw, self.kvw = wq.shape[1], wk.shape[1]
        self.w = jnp.concatenate([wq, wk, wv], axis=1)
        self.n_row, self.n_col = lax.axis_size("row"), lax.axis_size("col")
        self.sub = x.shape[0] // self.n_col
        self.keep, self.arrived = [], []

    def halves(self, block_list):
        low = my_bit("col", 0)
        blocks = jnp.stack(block_list).reshape(len(block_list), self.n_col // 2, 2, self.sub, -1)
        return pick(blocks, 1 - low, 2), pick(blocks, low, 2)

    def project(self, half):
        scaled = (half.astype(F32) * self.gain).astype(BF16)
        rows = scaled.reshape(-1, scaled.shape[-1])
        out = jnp.dot(rows, self.w, preferred_element_type=F32)
        return out.reshape(half.shape[:-1] + (-1,))

    def halve(self, total, arrived, bit):
        mine = my_bit("col", bit)
        shape = (total.shape[0], -1, 2) + total.shape[2:]
        total, arrived = total.reshape(shape), arrived.reshape(shape)

        def part(which):
            return pick(total, which, 2) + pick(arrived, which, 2).astype(F32)

        return part(mine), part(1 - mine).astype(BF16)

    def flat(self, value):
        return value.reshape(-1, value.shape[-1])

    def kernel_rows(self):
        return [self.flat(v) for v in self.keep] + [self.flat(v) for v in self.arrived]


def whole(body, out_shape, scratch=(), flops=0, exps=0, moved=0):
    return pl.pallas_call(
        body,
        out_shape=out_shape,
        scratch_shapes=list(scratch),
        compiler_params=pltpu.CompilerParams(vmem_limit_bytes=40 * 1024 * 1024),
        cost_estimate=pl.CostEstimate(flops=flops, transcendentals=exps, bytes_accessed=moved),
    )


def on_device(*arrays):
    arrays = [a[0] for a in arrays]
    half = len(arrays) // 2
    d, u = Cascade(*arrays[:half]), Cascade(*arrays[half:])
    n_row, n_col, sub = d.n_row, d.n_col, d.sub
    block = n_col * sub
    features = d.x.shape[1] * n_col
    rows = n_row * sub
    qw, kvw = d.qw, d.kvw
    z, r = lax.axis_index("col"), lax.axis_index("row")
    chain = Chain()

    order = [o for o in range(n_row) if o < 2] + [o for o in range(n_row) if o >= 2]
    starts = (r ^ jnp.array(order, jnp.int32)) * block
    offsets = jnp.arange(sub, dtype=jnp.int32)
    q_pos = (starts[:, None] + z * sub + offsets).astype(F32).reshape(rows, 1)
    owners = (z ^ jnp.arange(n_col, dtype=jnp.int32)) * sub
    k_pos = (owners[:, None, None] + starts[:, None] + offsets).astype(F32).reshape(1, -1)
    width = HD // 2
    inverse_freq = 10000.0 ** (-jnp.arange(width, dtype=F32) / width)
    angles = q_pos * inverse_freq
    cosine = jnp.concatenate([jnp.cos(angles)] * 2, axis=1)
    sine = jnp.sin(angles)
    sine = jnp.concatenate([-sine, sine], axis=1)

    d_blocks = gather(d.x, "row")
    d_blocks[1] = swapped(d.x, "row", 0)

    def send_first(c, group, blocks_):
        send, kept = c.halves(chain.enter(*blocks_))
        product = c.project(send).astype(BF16)
        return product, kept

    def keep_first(c, kept, token):
        return c.project(tie(kept, token))

    def second(c, total, arrived):
        total, arrived = chain.enter(total, arrived)
        kept, product = c.halve(total, arrived, 1)
        arrived = swapped(product, "col", 1)
        chain.leave(product)
        for bit in range(2, bits_of("col")):
            kept, product = c.halve(kept, arrived, bit)
            arrived = swapped(product, "col", bit)
        c.keep.append(kept)
        c.arrived.append(arrived)

    def settle(c):
        c.arrived[-1] = chain.enter(c.arrived[-1])
        chain.leave(c.arrived[-1])

    def take_far(blocks_):
        values = chain.enter(*[blocks_[o] for o in far])
        values = list(values) if len(far) > 1 else [values]
        for o, value in zip(far, values):
            blocks_[o] = value
            blocks_[o | 1] = swapped(value, "row", 0)
        chain.leave(values[-1])
        return values

    far = [o for o in d_blocks if o >= 2]
    far_order = [o for o in order if o >= 2]

    product, kept = send_first(d, 0, [d_blocks[0], d_blocks[1]])
    d_arr_a = swapped(product, "col", 0)
    d_tot_a = keep_first(d, kept, product)
    u_near = swapped(tie(u.x, product), "row", 0)
    chain.leave(d_tot_a)
    squares = jnp.stack([jnp.sum(jnp.square(chain.enter(c.x).astype(F32)), axis=1) for c in (d, u)])
    other = swapped(squares, "col", 0)
    chain.leave(squares)
    u_prod_a, kept = send_first(u, 0, [u.x, u_near])
    u_kept = kept
    chain.leave(u_prod_a)
    second(d, d_tot_a, d_arr_a)
    u_arr_a = swapped(tie(u_prod_a, chain.token), "col", 0)

    d_far = take_far(d_blocks)
    u_blocks = gather(tie(u.x, *d_far), "row")
    squares, other = chain.enter(squares, other)
    squares = squares + other
    other = swapped(squares, "col", 1)
    chain.leave(squares)
    u_tot_a = u.project(chain.enter(u_kept))
    chain.leave(u_tot_a)
    product, kept = send_first(d, 1, [d_blocks[o] for o in far_order])
    d_arr_b = swapped(product, "col", 0)
    d_tot_b = keep_first(d, kept, product)
    chain.leave(d_tot_b)
    settle(d)
    squares, other = chain.enter(squares, other)
    squares = squares + other
    for bit in range(2, bits_of("col")):
        squares = squares + swapped(squares, "col", bit)
    chain.leave(squares)
    sq = gather(squares, "row")
    second(u, u_tot_a, u_arr_a)

    take_far(u_blocks)
    second(d, d_tot_b, d_arr_b)
    for o in list(sq):
        sq[o | 1] = swapped(tie(sq[o], chain.token), "row", 0)
    u_prod_b, kept = send_first(u, 1, [u_blocks[o] for o in far_order])
    u_arr_b = swapped(u_prod_b, "col", 0)
    u_tot_b = keep_first(u, kept, u_prod_b)
    chain.leave(u_tot_b)
    settle(u)

    sums = jnp.stack([sq[o] for o in order])
    sums = pick(sums.reshape(n_row, 2, n_col, sub), z, 2)
    inverse = lax.rsqrt(sums / features + EPSILON).transpose(1, 0, 2).reshape(2, rows, 1)

    def make_pairs(c, scale):
        inputs = chain.enter(*c.kernel_rows())
        pair = whole(
            functools.partial(kv_kernel, qw, kvw),
            jax.ShapeDtypeStruct((rows, 2 * kvw), BF16),
            moved=2 * rows * (qw + 2 * kvw) * 6,
        )(*inputs, scale, cosine, sine)
        chain.leave(pair)
        return inputs, [pair] + [crossed(pair, "col", o) for o in range(1, n_col)]

    def attend(c, inputs, scale, pairs):
        pairs = chain.enter(*pairs)
        keys = rows * n_col
        out = whole(
            functools.partial(attention_kernel, qw, kvw, n_col),
            jax.ShapeDtypeStruct((rows, qw), BF16),
            scratch=[pltpu.VMEM((keys, kvw), BF16), pltpu.VMEM((keys, kvw), BF16), pltpu.VMEM((rows, keys), F32)],
            flops=4 * rows * keys * qw,
            exps=rows * keys * qw // HD,
            moved=rows * qw * 8,
        )(*inputs, scale, cosine, sine, q_pos, k_pos, *pairs)
        chain.leave(out)
        return out

    d_inputs, d_pairs = make_pairs(d, inverse[0])
    second(u, u_tot_b, u_arr_b)
    d_att = attend(d, d_inputs, inverse[0], d_pairs)
    d_got = gather(d_att, "col")
    d_got[1] = swapped(d_att, "col", 0)

    def out_first(c, pieces):
        pieces = chain.enter(*pieces)
        pieces = pieces if isinstance(pieces, (list, tuple)) else [pieces]
        shaped = jnp.stack([p.reshape(n_row // 2, 2, sub, qw) for p in pieces], axis=2)

        def dot(value):
            out = jnp.dot(value.reshape(-1, qw), c.wo, preferred_element_type=F32)
            return out.reshape(n_row // 2, -1, c.wo.shape[1])

        product = dot(shaped[:, 1]).astype(BF16)
        arrived = swapped(product, "row", 0)
        kept = dot(tie(shaped[:, 0], product))
        chain.leave(kept)
        return kept, arrived

    def out_second(kept, arrived):
        kept, arrived = chain.enter(kept, arrived)
        for bit in range(1, bits_of("row")):
            total = (kept + arrived.astype(F32)).reshape(-1, 2, *kept.shape[1:])
            product = total[:, 1].astype(BF16)
            kept, arrived = total[:, 0], swapped(product, "row", bit)
        chain.leave(product)
        return kept, arrived

    def out_third(c, kept, arrived, which, steps):
        kept, arrived = chain.enter(kept, arrived)
        residual = c.x.reshape(n_col, sub, -1)
        own = jnp.stack([pick(residual, z ^ o, 0) for o in which]).astype(F32)
        total = kept[0] + arrived[0].astype(F32)
        fresh = (own + total.reshape(own.shape)).astype(BF16)
        chain.leave(fresh)
        return from_behind(fresh, "section", steps)

    def finish(c, groups, *sent):
        by_name = {o: piece[i] for names, piece in zip(groups, sent) for i, o in enumerate(names)}
        both = jnp.stack([by_name[o] for o in range(n_col)])
        both = both.reshape((2,) * bits_of("col") + (sub, -1))
        for bit in range(bits_of("col")):
            dim = bits_of("col") - 1 - bit
            both = jnp.where(my_bit("col", bit) == 0, both, jnp.flip(both, dim))
        return both.reshape(c.x.shape)[None]

    def far_pieces(got):
        names = [o for o in got if o >= 2]
        values = chain.enter(*[got[o] for o in names])
        values = list(values) if len(names) > 1 else [values]
        chain.leave(values[-1])
        for o, value in zip(names, values):
            got[o] = value
            got[o | 1] = swapped(value, "col", 0)

    far_names = [[o for o in range(2, n_col) if o % 2 == 0], [o for o in range(2, n_col) if o % 2]]
    of_d, of_u = [[0, 1]] + far_names, [[0], [1]] + far_names

    def first(c, got, names):
        return out_first(c, [got[o] for o in names])

    def landed(sent):
        sent = chain.enter(sent)
        chain.leave(sent)
        return sent

    u_inputs, u_pairs = make_pairs(u, inverse[1])
    far_pieces(d_got)
    d_p = first(d, d_got, of_d[0])
    d_p = out_second(*d_p)
    u_att = attend(u, u_inputs, inverse[1], u_pairs)
    u_got = gather(u_att, "col")
    u_got[1] = swapped(u_att, "col", 0)
    d_p = out_third(d, *d_p, of_d[0], 1)
    d_m = first(d, d_got, of_d[1])
    d_m = out_second(*d_m)
    d_q = first(d, d_got, of_d[2])
    d_q = out_second(*d_q)
    u_o = first(u, u_got, of_u[0])
    u_o = out_second(*u_o)
    d_m = out_third(d, *d_m, of_d[1], 1)
    d_q = out_third(d, *d_q, of_d[2], 1)
    d_p = landed(d_p)
    u_p = first(u, u_got, of_u[1])
    u_p = out_second(*u_p)
    far_pieces(u_got)
    u_m = first(u, u_got, of_u[2])
    u_m = out_second(*u_m)
    u_o = out_third(u, *u_o, of_u[0], -1)
    d_m = landed(d_m)
    d_q = landed(d_q)
    u_p = out_third(u, *u_p, of_u[1], -1)
    u_q = first(u, u_got, of_u[3])
    u_q = out_second(*u_q)
    u_o = landed(u_o)
    u_m = out_third(u, *u_m, of_u[2], -1)
    u_p = landed(u_p)
    u_q = out_third(u, *u_q, of_u[3], -1)
    return finish(d, of_d, d_p, d_m, d_q), finish(u, of_u, u_o, u_p, u_m, u_q)


def solution(mesh):
    tokens = P("section", "row", "col")
    into, out_of = P("section", "col", "row"), P("section", "row", "col")
    one = (tokens, P("section", "col"), into, into, into, out_of)
    return jax.shard_map(
        on_device, mesh=mesh, in_specs=one + one, out_specs=(tokens, tokens), check_vma=False
    )
```

```python
import functools

import jax
import jax.numpy as jnp
from jax import lax
from jax.experimental import pallas as pl
from jax.experimental.pallas import tpu as pltpu
from jax.sharding import PartitionSpec as P

HD = 128
EPSILON = 1e-05
HIDDEN = -1e30
LOG2E = 1.4426950408889634
BF16 = jnp.bfloat16
F32 = jnp.float32


def swapped(value, axis, bit):
    return lax.ppermute(value, axis, [(i, i ^ (1 << bit)) for i in range(lax.axis_size(axis))])


def crossed(value, axis, bits):
    return lax.ppermute(value, axis, [(i, i ^ bits) for i in range(lax.axis_size(axis))])


def from_behind(value, axis, steps):
    count = lax.axis_size(axis)
    return lax.ppermute(value, axis, [(i, (i + steps) % count) for i in range(count)])


def bits_of(axis):
    return lax.axis_size(axis).bit_length() - 1


def my_bit(axis, bit):
    return (lax.axis_index(axis) >> bit) & 1


def pick(value, index, dim):
    return lax.dynamic_index_in_dim(value, index, dim, keepdims=False)


def tie(value, *deps):
    return lax.optimization_barrier((value, deps))[0]


class Chain:
    def __init__(self):
        self.token = None

    def enter(self, *values):
        out = values if self.token is None else tie(values, self.token)
        return out[0] if len(values) == 1 else out

    def leave(self, array):
        self.token = array


def turn(value, cosine, sine):
    return value * cosine + pltpu.roll(value, HD // 2, 1) * sine


def rows_of(keeps, arrivals, inverse, columns):
    parts = [k[:, columns] + a[:, columns].astype(F32) for k, a in zip(keeps, arrivals)]
    return jnp.concatenate(parts, axis=0) * inverse[...]


def kv_kernel(qw, kvw, keep_a, keep_b, arr_a, arr_b, inverse, cosine, sine, out):
    for start in range(0, 2 * kvw, HD):
        columns = slice(qw + start, qw + start + HD)
        value = rows_of((keep_a, keep_b), (arr_a, arr_b), inverse, columns)
        if start < kvw:
            value = turn(value, cosine[...], sine[...])
        out[:, start : start + HD] = value.astype(BF16)


def attention_kernel(
    qw, kvw, count, keep_a, keep_b, arr_a, arr_b, inverse, cosine, sine, q_pos, k_pos, *rest
):
    pairs, (out, keys, values, bias) = rest[:count], rest[count:]
    rows = pairs[0].shape[0]
    for i, pair in enumerate(pairs):
        keys[i * rows : (i + 1) * rows] = pair[:, :kvw]
        values[i * rows : (i + 1) * rows] = pair[:, kvw:]
    bias[...] = jnp.where(q_pos[...] >= k_pos[...], 0.0, HIDDEN)
    group = (qw // HD) // (kvw // HD)
    for head in range(qw // HD):
        columns = slice(head * HD, (head + 1) * HD)
        kv_columns = slice(head // group * HD, (head // group + 1) * HD)
        query = rows_of((keep_a, keep_b), (arr_a, arr_b), inverse, columns)
        query = turn(query, cosine[...], sine[...]).astype(BF16)
        scores = lax.dot_general(
            query, keys[:, kv_columns], (((1,), (1,)), ((), ())), preferred_element_type=F32
        )
        scores = scores + bias[...]
        top = jnp.max(scores, axis=1, keepdims=True)
        probs = jnp.exp2((scores - top) * (LOG2E / HD**0.5))
        total = jnp.sum(probs, axis=1, keepdims=True)
        mixed = jnp.dot(probs.astype(BF16), values[:, kv_columns], preferred_element_type=F32)
        out[:, columns] = (mixed / total).astype(BF16)


def gather(block, axis):
    blocks = {0: block}
    for bit in range(1, bits_of(axis)):
        for o in list(blocks):
            blocks[o | 1 << bit] = swapped(blocks[o], axis, bit)
    return blocks


class Cascade:
    def __init__(self, x, gain, wq, wk, wv, wo):
        self.x, self.gain, self.wo = x, gain, wo
        if wk.shape[1] < HD:
            other_k, other_v = swapped((wk, wv), "row", 0)
            even = lax.axis_index("row") % 2 == 0
            wk = jnp.where(even, jnp.concatenate([wk, other_k], 1), jnp.concatenate([other_k, wk], 1))
            wv = jnp.where(even, jnp.concatenate([wv, other_v], 1), jnp.concatenate([other_v, wv], 1))
        self.qw, self.kvw = wq.shape[1], wk.shape[1]
        self.w = jnp.concatenate([wq, wk, wv], axis=1)
        self.n_row, self.n_col = lax.axis_size("row"), lax.axis_size("col")
        self.sub = x.shape[0] // self.n_col
        self.keep, self.arrived = [], []

    def halves(self, block_list):
        low = my_bit("col", 0)
        blocks = jnp.stack(block_list).reshape(len(block_list), self.n_col // 2, 2, self.sub, -1)
        return pick(blocks, 1 - low, 2), pick(blocks, low, 2)

    def project(self, half):
        scaled = (half.astype(F32) * self.gain).astype(BF16)
        rows = scaled.reshape(-1, scaled.shape[-1])
        out = jnp.dot(rows, self.w, preferred_element_type=F32)
        return out.reshape(half.shape[:-1] + (-1,))

    def halve(self, total, arrived, bit):
        mine = my_bit("col", bit)
        shape = (total.shape[0], -1, 2) + total.shape[2:]
        total, arrived = total.reshape(shape), arrived.reshape(shape)

        def part(which):
            return pick(total, which, 2) + pick(arrived, which, 2).astype(F32)

        return part(mine), part(1 - mine).astype(BF16)

    def flat(self, value):
        return value.reshape(-1, value.shape[-1])

    def kernel_rows(self):
        return [self.flat(v) for v in self.keep] + [self.flat(v) for v in self.arrived]


def whole(body, out_shape, scratch=(), flops=0, exps=0, moved=0):
    return pl.pallas_call(
        body,
        out_shape=out_shape,
        scratch_shapes=list(scratch),
        compiler_params=pltpu.CompilerParams(vmem_limit_bytes=40 * 1024 * 1024),
        cost_estimate=pl.CostEstimate(flops=flops, transcendentals=exps, bytes_accessed=moved),
    )


def on_device(*arrays):
    arrays = [a[0] for a in arrays]
    half = len(arrays) // 2
    d, u = Cascade(*arrays[:half]), Cascade(*arrays[half:])
    n_row, n_col, sub = d.n_row, d.n_col, d.sub
    block = n_col * sub
    features = d.x.shape[1] * n_col
    rows = n_row * sub
    qw, kvw = d.qw, d.kvw
    z, r = lax.axis_index("col"), lax.axis_index("row")
    chain = Chain()

    order = [o for o in range(n_row) if o < 2] + [o for o in range(n_row) if o >= 2]
    starts = (r ^ jnp.array(order, jnp.int32)) * block
    offsets = jnp.arange(sub, dtype=jnp.int32)
    q_pos = (starts[:, None] + z * sub + offsets).astype(F32).reshape(rows, 1)
    owners = (z ^ jnp.arange(n_col, dtype=jnp.int32)) * sub
    k_pos = (owners[:, None, None] + starts[:, None] + offsets).astype(F32).reshape(1, -1)
    width = HD // 2
    inverse_freq = 10000.0 ** (-jnp.arange(width, dtype=F32) / width)
    angles = q_pos * inverse_freq
    cosine = jnp.concatenate([jnp.cos(angles)] * 2, axis=1)
    sine = jnp.sin(angles)
    sine = jnp.concatenate([-sine, sine], axis=1)

    d_blocks = gather(d.x, "row")
    d_blocks[1] = swapped(d.x, "row", 0)

    def send_first(c, group, blocks_):
        send, kept = c.halves(chain.enter(*blocks_))
        product = c.project(send).astype(BF16)
        return product, kept

    def keep_first(c, kept, token):
        return c.project(tie(kept, token))

    def second(c, total, arrived):
        total, arrived = chain.enter(total, arrived)
        kept, product = c.halve(total, arrived, 1)
        arrived = swapped(product, "col", 1)
        chain.leave(product)
        for bit in range(2, bits_of("col")):
            kept, product = c.halve(kept, arrived, bit)
            arrived = swapped(product, "col", bit)
        c.keep.append(kept)
        c.arrived.append(arrived)

    def settle(c):
        c.arrived[-1] = chain.enter(c.arrived[-1])
        chain.leave(c.arrived[-1])

    def take_far(blocks_):
        values = chain.enter(*[blocks_[o] for o in far])
        values = list(values) if len(far) > 1 else [values]
        for o, value in zip(far, values):
            blocks_[o] = value
            blocks_[o | 1] = swapped(value, "row", 0)
        chain.leave(values[-1])
        return values

    far = [o for o in d_blocks if o >= 2]
    far_order = [o for o in order if o >= 2]

    product, kept = send_first(d, 0, [d_blocks[0], d_blocks[1]])
    d_arr_a = swapped(product, "col", 0)
    d_tot_a = keep_first(d, kept, product)
    u_near = swapped(tie(u.x, product), "row", 0)
    chain.leave(d_tot_a)
    squares = jnp.stack([jnp.sum(jnp.square(chain.enter(c.x).astype(F32)), axis=1) for c in (d, u)])
    other = swapped(squares, "col", 0)
    chain.leave(squares)
    u_prod_a, kept = send_first(u, 0, [u.x, u_near])
    u_kept = kept
    chain.leave(u_prod_a)
    second(d, d_tot_a, d_arr_a)
    u_arr_a = swapped(tie(u_prod_a, chain.token), "col", 0)

    d_far = take_far(d_blocks)
    u_blocks = gather(tie(u.x, *d_far), "row")
    squares, other = chain.enter(squares, other)
    squares = squares + other
    other = swapped(squares, "col", 1)
    chain.leave(squares)
    u_tot_a = u.project(chain.enter(u_kept))
    chain.leave(u_tot_a)
    product, kept = send_first(d, 1, [d_blocks[o] for o in far_order])
    d_arr_b = swapped(product, "col", 0)
    d_tot_b = keep_first(d, kept, product)
    chain.leave(d_tot_b)
    settle(d)
    squares, other = chain.enter(squares, other)
    squares = squares + other
    for bit in range(2, bits_of("col")):
        squares = squares + swapped(squares, "col", bit)
    chain.leave(squares)
    sq = gather(squares, "row")
    second(u, u_tot_a, u_arr_a)

    take_far(u_blocks)
    second(d, d_tot_b, d_arr_b)
    for o in list(sq):
        sq[o | 1] = swapped(tie(sq[o], chain.token), "row", 0)
    u_prod_b, kept = send_first(u, 1, [u_blocks[o] for o in far_order])
    u_arr_b = swapped(u_prod_b, "col", 0)
    u_tot_b = keep_first(u, kept, u_prod_b)
    chain.leave(u_tot_b)
    settle(u)

    sums = jnp.stack([sq[o] for o in order])
    sums = pick(sums.reshape(n_row, 2, n_col, sub), z, 2)
    inverse = lax.rsqrt(sums / features + EPSILON).transpose(1, 0, 2).reshape(2, rows, 1)

    def make_pairs(c, scale):
        inputs = chain.enter(*c.kernel_rows())
        pair = whole(
            functools.partial(kv_kernel, qw, kvw),
            jax.ShapeDtypeStruct((rows, 2 * kvw), BF16),
            moved=2 * rows * (qw + 2 * kvw) * 6,
        )(*inputs, scale, cosine, sine)
        chain.leave(pair)
        return inputs, [pair] + [crossed(pair, "col", o) for o in range(1, n_col)]

    def attend(c, inputs, scale, pairs):
        pairs = chain.enter(*pairs)
        keys = rows * n_col
        out = whole(
            functools.partial(attention_kernel, qw, kvw, n_col),
            jax.ShapeDtypeStruct((rows, qw), BF16),
            scratch=[pltpu.VMEM((keys, kvw), BF16), pltpu.VMEM((keys, kvw), BF16), pltpu.VMEM((rows, keys), F32)],
            flops=4 * rows * keys * qw,
            exps=rows * keys * qw // HD,
            moved=rows * qw * 8,
        )(*inputs, scale, cosine, sine, q_pos, k_pos, *pairs)
        chain.leave(out)
        return out

    d_inputs, d_pairs = make_pairs(d, inverse[0])
    second(u, u_tot_b, u_arr_b)
    d_att = attend(d, d_inputs, inverse[0], d_pairs)
    d_got = gather(d_att, "col")
    d_got[1] = swapped(d_att, "col", 0)

    def out_first(c, pieces):
        pieces = chain.enter(*pieces)
        pieces = pieces if isinstance(pieces, (list, tuple)) else [pieces]
        shaped = jnp.stack([p.reshape(n_row // 2, 2, sub, qw) for p in pieces], axis=2)

        def dot(value):
            out = jnp.dot(value.reshape(-1, qw), c.wo, preferred_element_type=F32)
            return out.reshape(n_row // 2, -1, c.wo.shape[1])

        product = dot(shaped[:, 1]).astype(BF16)
        arrived = swapped(product, "row", 0)
        kept = dot(tie(shaped[:, 0], product))
        chain.leave(kept)
        return kept, arrived

    def out_second(kept, arrived):
        kept, arrived = chain.enter(kept, arrived)
        for bit in range(1, bits_of("row")):
            total = (kept + arrived.astype(F32)).reshape(-1, 2, *kept.shape[1:])
            product = total[:, 1].astype(BF16)
            kept, arrived = total[:, 0], swapped(product, "row", bit)
        chain.leave(product)
        return kept, arrived

    def out_third(c, kept, arrived, which, steps):
        kept, arrived = chain.enter(kept, arrived)
        residual = c.x.reshape(n_col, sub, -1)
        own = jnp.stack([pick(residual, z ^ o, 0) for o in which]).astype(F32)
        total = kept[0] + arrived[0].astype(F32)
        fresh = (own + total.reshape(own.shape)).astype(BF16)
        chain.leave(fresh)
        return from_behind(fresh, "section", steps)

    def finish(c, groups, *sent):
        by_name = {o: piece[i] for names, piece in zip(groups, sent) for i, o in enumerate(names)}
        both = jnp.stack([by_name[o] for o in range(n_col)])
        both = both.reshape((2,) * bits_of("col") + (sub, -1))
        for bit in range(bits_of("col")):
            dim = bits_of("col") - 1 - bit
            both = jnp.where(my_bit("col", bit) == 0, both, jnp.flip(both, dim))
        return both.reshape(c.x.shape)[None]

    def far_pieces(got):
        names = [o for o in got if o >= 2]
        values = chain.enter(*[got[o] for o in names])
        values = list(values) if len(names) > 1 else [values]
        chain.leave(values[-1])
        for o, value in zip(names, values):
            got[o] = value
            got[o | 1] = swapped(value, "col", 0)

    far_names = [[o for o in range(2, n_col) if o % 2 == 0], [o for o in range(2, n_col) if o % 2]]
    of_d, of_u = [[0, 1]] + far_names, [[0], [1]] + far_names

    def first(c, got, names):
        return out_first(c, [got[o] for o in names])

    def landed(sent):
        sent = chain.enter(sent)
        chain.leave(sent)
        return sent

    u_inputs, u_pairs = make_pairs(u, inverse[1])
    far_pieces(d_got)
    d_p = first(d, d_got, of_d[0])
    d_p = out_second(*d_p)
    u_att = attend(u, u_inputs, inverse[1], u_pairs)
    u_got = gather(u_att, "col")
    u_got[1] = swapped(u_att, "col", 0)
    d_p = out_third(d, *d_p, of_d[0], 1)
    d_m = first(d, d_got, of_d[1])
    d_m = out_second(*d_m)
    d_q = first(d, d_got, of_d[2])
    d_q = out_second(*d_q)
    u_o = first(u, u_got, of_u[0])
    u_o = out_second(*u_o)
    d_m = out_third(d, *d_m, of_d[1], 1)
    d_q = out_third(d, *d_q, of_d[2], 1)
    d_p = landed(d_p)
    u_p = first(u, u_got, of_u[1])
    u_p = out_second(*u_p)
    far_pieces(u_got)
    u_m = first(u, u_got, of_u[2])
    u_m = out_second(*u_m)
    u_o = out_third(u, *u_o, of_u[0], -1)
    d_m = landed(d_m)
    d_q = landed(d_q)
    u_p = out_third(u, *u_p, of_u[1], -1)
    u_o = landed(u_o)
    u_q = first(u, u_got, of_u[3])
    u_q = out_second(*u_q)
    u_m = out_third(u, *u_m, of_u[2], -1)
    u_p = landed(u_p)
    u_q = out_third(u, *u_q, of_u[3], -1)
    return finish(d, of_d, d_p, d_m, d_q), finish(u, of_u, u_o, u_p, u_m, u_q)


def solution(mesh):
    tokens = P("section", "row", "col")
    into, out_of = P("section", "col", "row"), P("section", "row", "col")
    one = (tokens, P("section", "col"), into, into, into, out_of)
    return jax.shard_map(
        on_device, mesh=mesh, in_specs=one + one, out_specs=(tokens, tokens), check_vma=False
    )
```

```python
import functools

import jax
import jax.numpy as jnp
from jax import lax
from jax.experimental import pallas as pl
from jax.experimental.pallas import tpu as pltpu
from jax.sharding import PartitionSpec as P

HD = 128
EPSILON = 1e-05
HIDDEN = -1e30
LOG2E = 1.4426950408889634
BF16 = jnp.bfloat16
F32 = jnp.float32


def swapped(value, axis, bit):
    return lax.ppermute(value, axis, [(i, i ^ (1 << bit)) for i in range(lax.axis_size(axis))])


def crossed(value, axis, bits):
    return lax.ppermute(value, axis, [(i, i ^ bits) for i in range(lax.axis_size(axis))])


def from_behind(value, axis, steps):
    count = lax.axis_size(axis)
    return lax.ppermute(value, axis, [(i, (i + steps) % count) for i in range(count)])


def bits_of(axis):
    return lax.axis_size(axis).bit_length() - 1


def my_bit(axis, bit):
    return (lax.axis_index(axis) >> bit) & 1


def pick(value, index, dim):
    return lax.dynamic_index_in_dim(value, index, dim, keepdims=False)


def tie(value, *deps):
    return lax.optimization_barrier((value, deps))[0]


class Chain:
    def __init__(self):
        self.token = None

    def enter(self, *values):
        out = values if self.token is None else tie(values, self.token)
        return out[0] if len(values) == 1 else out

    def leave(self, array):
        self.token = array


def turn(value, cosine, sine):
    return value * cosine + pltpu.roll(value, HD // 2, 1) * sine


def rows_of(keeps, arrivals, inverse, columns):
    parts = [k[:, columns] + a[:, columns].astype(F32) for k, a in zip(keeps, arrivals)]
    return jnp.concatenate(parts, axis=0) * inverse[...]


def kv_kernel(qw, kvw, keep_a, keep_b, arr_a, arr_b, inverse, cosine, sine, out):
    for start in range(0, 2 * kvw, HD):
        columns = slice(qw + start, qw + start + HD)
        value = rows_of((keep_a, keep_b), (arr_a, arr_b), inverse, columns)
        if start < kvw:
            value = turn(value, cosine[...], sine[...])
        out[:, start : start + HD] = value.astype(BF16)


def attention_kernel(
    qw, kvw, count, keep_a, keep_b, arr_a, arr_b, inverse, cosine, sine, q_pos, k_pos, *rest
):
    pairs, (out, keys, values, bias) = rest[:count], rest[count:]
    rows = pairs[0].shape[0]
    for i, pair in enumerate(pairs):
        keys[i * rows : (i + 1) * rows] = pair[:, :kvw]
        values[i * rows : (i + 1) * rows] = pair[:, kvw:]
    bias[...] = jnp.where(q_pos[...] >= k_pos[...], 0.0, HIDDEN)
    group = (qw // HD) // (kvw // HD)
    for head in range(qw // HD):
        columns = slice(head * HD, (head + 1) * HD)
        kv_columns = slice(head // group * HD, (head // group + 1) * HD)
        query = rows_of((keep_a, keep_b), (arr_a, arr_b), inverse, columns)
        query = turn(query, cosine[...], sine[...]).astype(BF16)
        scores = lax.dot_general(
            query, keys[:, kv_columns], (((1,), (1,)), ((), ())), preferred_element_type=F32
        )
        scores = scores + bias[...]
        top = jnp.max(scores, axis=1, keepdims=True)
        probs = jnp.exp2((scores - top) * (LOG2E / HD**0.5))
        total = jnp.sum(probs, axis=1, keepdims=True)
        mixed = jnp.dot(probs.astype(BF16), values[:, kv_columns], preferred_element_type=F32)
        out[:, columns] = (mixed / total).astype(BF16)


def gather(block, axis):
    blocks = {0: block}
    for bit in range(1, bits_of(axis)):
        for o in list(blocks):
            blocks[o | 1 << bit] = swapped(blocks[o], axis, bit)
    return blocks


class Cascade:
    def __init__(self, x, gain, wq, wk, wv, wo):
        self.x, self.gain, self.wo = x, gain, wo
        if wk.shape[1] < HD:
            other_k, other_v = swapped((wk, wv), "row", 0)
            even = lax.axis_index("row") % 2 == 0
            wk = jnp.where(even, jnp.concatenate([wk, other_k], 1), jnp.concatenate([other_k, wk], 1))
            wv = jnp.where(even, jnp.concatenate([wv, other_v], 1), jnp.concatenate([other_v, wv], 1))
        self.qw, self.kvw = wq.shape[1], wk.shape[1]
        self.w = jnp.concatenate([wq, wk, wv], axis=1)
        self.n_row, self.n_col = lax.axis_size("row"), lax.axis_size("col")
        self.sub = x.shape[0] // self.n_col
        self.keep, self.arrived = [], []

    def halves(self, block_list):
        low = my_bit("col", 0)
        blocks = jnp.stack(block_list).reshape(len(block_list), self.n_col // 2, 2, self.sub, -1)
        return pick(blocks, 1 - low, 2), pick(blocks, low, 2)

    def project(self, half):
        scaled = (half.astype(F32) * self.gain).astype(BF16)
        rows = scaled.reshape(-1, scaled.shape[-1])
        out = jnp.dot(rows, self.w, preferred_element_type=F32)
        return out.reshape(half.shape[:-1] + (-1,))

    def halve(self, total, arrived, bit):
        mine = my_bit("col", bit)
        shape = (total.shape[0], -1, 2) + total.shape[2:]
        total, arrived = total.reshape(shape), arrived.reshape(shape)

        def part(which):
            return pick(total, which, 2) + pick(arrived, which, 2).astype(F32)

        return part(mine), part(1 - mine).astype(BF16)

    def flat(self, value):
        return value.reshape(-1, value.shape[-1])

    def kernel_rows(self):
        return [self.flat(v) for v in self.keep] + [self.flat(v) for v in self.arrived]


def whole(body, out_shape, scratch=(), flops=0, exps=0, moved=0):
    return pl.pallas_call(
        body,
        out_shape=out_shape,
        scratch_shapes=list(scratch),
        compiler_params=pltpu.CompilerParams(vmem_limit_bytes=40 * 1024 * 1024),
        cost_estimate=pl.CostEstimate(flops=flops, transcendentals=exps, bytes_accessed=moved),
    )


def on_device(*arrays):
    arrays = [a[0] for a in arrays]
    half = len(arrays) // 2
    d, u = Cascade(*arrays[:half]), Cascade(*arrays[half:])
    n_row, n_col, sub = d.n_row, d.n_col, d.sub
    block = n_col * sub
    features = d.x.shape[1] * n_col
    rows = n_row * sub
    qw, kvw = d.qw, d.kvw
    z, r = lax.axis_index("col"), lax.axis_index("row")
    chain = Chain()

    order = [o for o in range(n_row) if o < 2] + [o for o in range(n_row) if o >= 2]
    starts = (r ^ jnp.array(order, jnp.int32)) * block
    offsets = jnp.arange(sub, dtype=jnp.int32)
    q_pos = (starts[:, None] + z * sub + offsets).astype(F32).reshape(rows, 1)
    owners = (z ^ jnp.arange(n_col, dtype=jnp.int32)) * sub
    k_pos = (owners[:, None, None] + starts[:, None] + offsets).astype(F32).reshape(1, -1)
    width = HD // 2
    inverse_freq = 10000.0 ** (-jnp.arange(width, dtype=F32) / width)
    angles = q_pos * inverse_freq
    cosine = jnp.concatenate([jnp.cos(angles)] * 2, axis=1)
    sine = jnp.sin(angles)
    sine = jnp.concatenate([-sine, sine], axis=1)

    d_blocks = gather(d.x, "row")
    d_blocks[1] = swapped(d.x, "row", 0)

    def send_first(c, group, blocks_):
        send, kept = c.halves(chain.enter(*blocks_))
        product = c.project(send).astype(BF16)
        return product, kept

    def keep_first(c, kept, token):
        return c.project(tie(kept, token))

    def second(c, total, arrived):
        total, arrived = chain.enter(total, arrived)
        kept, product = c.halve(total, arrived, 1)
        arrived = swapped(product, "col", 1)
        chain.leave(product)
        for bit in range(2, bits_of("col")):
            kept, product = c.halve(kept, arrived, bit)
            arrived = swapped(product, "col", bit)
        c.keep.append(kept)
        c.arrived.append(arrived)

    def settle(c):
        c.arrived[-1] = chain.enter(c.arrived[-1])
        chain.leave(c.arrived[-1])

    def take_far(blocks_):
        values = chain.enter(*[blocks_[o] for o in far])
        values = list(values) if len(far) > 1 else [values]
        for o, value in zip(far, values):
            blocks_[o] = value
            blocks_[o | 1] = swapped(value, "row", 0)
        chain.leave(values[-1])
        return values

    far = [o for o in d_blocks if o >= 2]
    far_order = [o for o in order if o >= 2]

    product, kept = send_first(d, 0, [d_blocks[0], d_blocks[1]])
    d_arr_a = swapped(product, "col", 0)
    d_tot_a = keep_first(d, kept, product)
    u_near = swapped(tie(u.x, product), "row", 0)
    chain.leave(d_tot_a)
    squares = jnp.stack([jnp.sum(jnp.square(chain.enter(c.x).astype(F32)), axis=1) for c in (d, u)])
    other = swapped(squares, "col", 0)
    chain.leave(squares)
    u_prod_a, kept = send_first(u, 0, [u.x, u_near])
    u_kept = kept
    chain.leave(u_prod_a)
    second(d, d_tot_a, d_arr_a)
    u_arr_a = swapped(tie(u_prod_a, chain.token), "col", 0)

    d_far = take_far(d_blocks)
    u_blocks = gather(tie(u.x, *d_far), "row")
    squares, other = chain.enter(squares, other)
    squares = squares + other
    other = swapped(squares, "col", 1)
    chain.leave(squares)
    u_tot_a = u.project(chain.enter(u_kept))
    chain.leave(u_tot_a)
    product, kept = send_first(d, 1, [d_blocks[o] for o in far_order])
    d_arr_b = swapped(product, "col", 0)
    d_tot_b = keep_first(d, kept, product)
    chain.leave(d_tot_b)
    settle(d)
    squares, other = chain.enter(squares, other)
    squares = squares + other
    for bit in range(2, bits_of("col")):
        squares = squares + swapped(squares, "col", bit)
    chain.leave(squares)
    sq = gather(squares, "row")
    second(u, u_tot_a, u_arr_a)

    take_far(u_blocks)
    second(d, d_tot_b, d_arr_b)
    for o in list(sq):
        sq[o | 1] = swapped(tie(sq[o], chain.token), "row", 0)
    u_prod_b, kept = send_first(u, 1, [u_blocks[o] for o in far_order])
    u_arr_b = swapped(u_prod_b, "col", 0)
    u_tot_b = keep_first(u, kept, u_prod_b)
    chain.leave(u_tot_b)
    settle(u)

    sums = jnp.stack([sq[o] for o in order])
    sums = pick(sums.reshape(n_row, 2, n_col, sub), z, 2)
    inverse = lax.rsqrt(sums / features + EPSILON).transpose(1, 0, 2).reshape(2, rows, 1)

    def make_pairs(c, scale):
        inputs = chain.enter(*c.kernel_rows())
        pair = whole(
            functools.partial(kv_kernel, qw, kvw),
            jax.ShapeDtypeStruct((rows, 2 * kvw), BF16),
            moved=2 * rows * (qw + 2 * kvw) * 6,
        )(*inputs, scale, cosine, sine)
        chain.leave(pair)
        return inputs, [pair] + [crossed(pair, "col", o) for o in range(1, n_col)]

    def attend(c, inputs, scale, pairs):
        pairs = chain.enter(*pairs)
        keys = rows * n_col
        out = whole(
            functools.partial(attention_kernel, qw, kvw, n_col),
            jax.ShapeDtypeStruct((rows, qw), BF16),
            scratch=[pltpu.VMEM((keys, kvw), BF16), pltpu.VMEM((keys, kvw), BF16), pltpu.VMEM((rows, keys), F32)],
            flops=4 * rows * keys * qw,
            exps=rows * keys * qw // HD,
            moved=rows * qw * 8,
        )(*inputs, scale, cosine, sine, q_pos, k_pos, *pairs)
        chain.leave(out)
        return out

    d_inputs, d_pairs = make_pairs(d, inverse[0])
    second(u, u_tot_b, u_arr_b)
    d_att = attend(d, d_inputs, inverse[0], d_pairs)
    d_got = gather(d_att, "col")
    d_got[1] = swapped(d_att, "col", 0)

    def out_first(c, pieces):
        pieces = chain.enter(*pieces)
        pieces = pieces if isinstance(pieces, (list, tuple)) else [pieces]
        shaped = jnp.stack([p.reshape(n_row // 2, 2, sub, qw) for p in pieces], axis=2)

        def dot(value):
            out = jnp.dot(value.reshape(-1, qw), c.wo, preferred_element_type=F32)
            return out.reshape(n_row // 2, -1, c.wo.shape[1])

        product = dot(shaped[:, 1]).astype(BF16)
        arrived = swapped(product, "row", 0)
        kept = dot(tie(shaped[:, 0], product))
        chain.leave(kept)
        return kept, arrived

    def out_second(kept, arrived):
        kept, arrived = chain.enter(kept, arrived)
        for bit in range(1, bits_of("row")):
            total = (kept + arrived.astype(F32)).reshape(-1, 2, *kept.shape[1:])
            product = total[:, 1].astype(BF16)
            kept, arrived = total[:, 0], swapped(product, "row", bit)
        chain.leave(product)
        return kept, arrived

    def out_third(c, kept, arrived, which, steps):
        kept, arrived = chain.enter(kept, arrived)
        residual = c.x.reshape(n_col, sub, -1)
        own = jnp.stack([pick(residual, z ^ o, 0) for o in which]).astype(F32)
        total = kept[0] + arrived[0].astype(F32)
        fresh = (own + total.reshape(own.shape)).astype(BF16)
        chain.leave(fresh)
        return from_behind(fresh, "section", steps)

    def finish(c, groups, *sent):
        by_name = {o: piece[i] for names, piece in zip(groups, sent) for i, o in enumerate(names)}
        both = jnp.stack([by_name[o] for o in range(n_col)])
        both = both.reshape((2,) * bits_of("col") + (sub, -1))
        for bit in range(bits_of("col")):
            dim = bits_of("col") - 1 - bit
            both = jnp.where(my_bit("col", bit) == 0, both, jnp.flip(both, dim))
        return both.reshape(c.x.shape)[None]

    def far_pieces(got):
        names = [o for o in got if o >= 2]
        values = chain.enter(*[got[o] for o in names])
        values = list(values) if len(names) > 1 else [values]
        chain.leave(values[-1])
        for o, value in zip(names, values):
            got[o] = value
            got[o | 1] = swapped(value, "col", 0)

    far_names = [[o for o in range(2, n_col) if o % 2 == 0], [o for o in range(2, n_col) if o % 2]]
    of_d, of_u = [[0, 1]] + far_names, [[0], [1]] + far_names

    def first(c, got, names):
        return out_first(c, [got[o] for o in names])

    def landed(sent):
        sent = chain.enter(sent)
        chain.leave(sent)
        return sent

    u_inputs, u_pairs = make_pairs(u, inverse[1])
    far_pieces(d_got)
    d_p = first(d, d_got, of_d[0])
    d_p = out_second(*d_p)
    u_att = attend(u, u_inputs, inverse[1], u_pairs)
    u_got = gather(u_att, "col")
    u_got[1] = swapped(u_att, "col", 0)
    d_p = out_third(d, *d_p, of_d[0], 1)
    d_m = first(d, d_got, of_d[1])
    d_m = out_second(*d_m)
    d_q = first(d, d_got, of_d[2])
    d_q = out_second(*d_q)
    u_o = first(u, u_got, of_u[0])
    u_o = out_second(*u_o)
    d_m = out_third(d, *d_m, of_d[1], 1)
    d_q = out_third(d, *d_q, of_d[2], 1)
    d_p = landed(d_p)
    u_p = first(u, u_got, of_u[1])
    u_p = out_second(*u_p)
    far_pieces(u_got)
    u_m = first(u, u_got, of_u[2])
    u_m = out_second(*u_m)
    u_o = out_third(u, *u_o, of_u[0], -1)
    d_m = landed(d_m)
    d_q = landed(d_q)
    u_p = out_third(u, *u_p, of_u[1], -1)
    u_o = landed(u_o)
    u_q = first(u, u_got, of_u[3])
    u_q = out_second(*u_q)
    u_p = landed(u_p)
    u_m = out_third(u, *u_m, of_u[2], -1)
    u_q = out_third(u, *u_q, of_u[3], -1)
    return finish(d, of_d, d_p, d_m, d_q), finish(u, of_u, u_o, u_p, u_m, u_q)


def solution(mesh):
    tokens = P("section", "row", "col")
    into, out_of = P("section", "col", "row"), P("section", "row", "col")
    one = (tokens, P("section", "col"), into, into, into, out_of)
    return jax.shard_map(
        on_device, mesh=mesh, in_specs=one + one, out_specs=(tokens, tokens), check_vma=False
    )
```
